32 devices in a mesh: ctx: 4 (over x, core), grp: 2 (over y), rep: 4 (over z).
Axes of the slice: x: 2, y: 2, z: 4, core: 2. Of those that a mesh axis runs over, the one named last changes fastest.
Arguments:
- tokens: bfloat16 [16, 1024, 1024], P(('grp', 'rep'), 'ctx'), may hold values from -6 to 6
- segment_ids: int32 [16, 1024], P(('grp', 'rep'), 'ctx'), may hold values from 0 to 2, as said below
- positions: int32 [16, 1024], P(('grp', 'rep'), 'ctx'), may hold values from 0 to 5119, as said below
- cotangent: bfloat16 [16, 1024, 1024], P(('grp', 'rep'), 'ctx'), may hold values from -6 to 6
- qkv_weight: float32 [1024, 4096], P(('ctx', 'grp')), may hold values from -0.1875 to 0.1875
- qkv_first: float32 [1024, 4096], P(('ctx', 'grp')), may hold values from -40 to 40
- qkv_second: float32 [1024, 4096], P(('ctx', 'grp')), may hold values from 212.992 to 868.352
- out_weight: float32 [2048, 1024], P(('ctx', 'grp')), may hold values from -1 to 1
- out_first: float32 [2048, 1024], P(('ctx', 'grp')), may hold values from -8 to 8
- out_second: float32 [2048, 1024], P(('ctx', 'grp')), may hold values from 8.68352 to 34.4064
- expand_weight: float32 [1024, 6144], P(('ctx', 'grp')), may hold values from -0.1875 to 0.1875
- expand_first: float32 [1024, 6144], P(('ctx', 'grp')), may hold values from -24 to 24
- expand_second: float32 [1024, 6144], P(('ctx', 'grp')), may hold values from 77.0048 to 311.296
- shrink_weight: float32 [3072, 1024], P(('ctx', 'grp')), may hold values from -0.109375 to 0.109375
- shrink_first: float32 [3072, 1024], P(('ctx', 'grp')), may hold values from -40 to 40
- shrink_second: float32 [3072, 1024], P(('ctx', 'grp')), may hold values from 212.992 to 868.352
- norm_gains: float32 [2304], P(('ctx', 'grp')), may hold values from 0.5 to 1.5
- gains_first: float32 [2304], P(('ctx', 'grp')), may hold values from -128 to 128
- gains_second: float32 [2304], P(('ctx', 'grp')), may hold values from 1966.08 to 7700.48
Outputs:
- block_output: bfloat16 [16, 1024, 1024], P(('grp', 'rep'), 'ctx')
- input_grad: bfloat16 [16, 1024, 1024], P(('grp', 'rep'), 'ctx')
- qkv_moment: float32 [1024, 4096], P(('ctx', 'grp'))
- qkv_square: float32 [1024, 4096], P(('ctx', 'grp'))
- qkv_updated: float32 [1024, 4096], P(('ctx', 'grp'))
- out_moment: float32 [2048, 1024], P(('ctx', 'grp'))
- out_square: float32 [2048, 1024], P(('ctx', 'grp'))
- out_updated: float32 [2048, 1024], P(('ctx', 'grp'))
- expand_moment: float32 [1024, 6144], P(('ctx', 'grp'))
- expand_square: float32 [1024, 6144], P(('ctx', 'grp'))
- expand_updated: float32 [1024, 6144], P(('ctx', 'grp'))
- shrink_moment: float32 [3072, 1024], P(('ctx', 'grp'))
- shrink_square: float32 [3072, 1024], P(('ctx', 'grp'))
- shrink_updated: float32 [3072, 1024], P(('ctx', 'grp'))
- gains_moment: float32 [2304], P(('ctx', 'grp'))
- gains_square: float32 [2304], P(('ctx', 'grp'))
- gains_updated: float32 [2304], P(('ctx', 'grp'))
The draws below stay inside these ranges and needn't reach their ends.
Inputs may be any that keep to these rules, and one draw needn't show every extreme that they name: `segment_ids`: along each sequence segment ids start at 0 and never fall. Within a document the positions rise by one from token to token.
All inputs are finite; a program needn't handle non-finite values.
Results may differ from the reference program's by a relative error of at most 0.025.
Values may be sent and summed in bfloat16 or wider, within the bound.
No kernel may reach another device: no remote copies, remote signals or barrier semaphores. Data moves between devices by JAX's collectives and lax.ppermute only.
A program may use at most 320 MiB of HBM per device.

```python
import math
import jax
import jax.numpy as jnp
from jax import lax

D = 1024
QUERY_HEADS = 16
KEY_VALUE_HEADS = 8
HEAD_SIZE = 128
FF = 3072
SEQS = 2
STEP = 10
QUERY_FEATURES = 2048
KEY_FEATURES = 1024
QKV = 4096
GAINS = 2304
SEQ = 1024
TOK_SEQ = 256
BATCH = 16
TOKENS = 16384


def document_layout(key):
    key_lens, key_left, key_right, key_pick = jax.random.split(key, 4)
    ladder = jnp.arange(SEQ, dtype=jnp.int32)
    lengths = jax.random.randint(key_lens, (BATCH, 16), SEQ // 10, SEQ, dtype=jnp.int32)
    doc_ends = jnp.cumsum(lengths, axis=1)
    short_ids = jnp.sum((doc_ends[:, None, :] <= ladder[None, :, None]).astype(jnp.int32), axis=2)
    short_ids = jnp.minimum(short_ids, 2)
    padded = jnp.concatenate([jnp.zeros((BATCH, 1), jnp.int32), doc_ends], axis=1)
    short_starts = jnp.take_along_axis(padded, short_ids, axis=1)
    left_edge = jax.random.randint(key_left, (BATCH, 1), 1, TOK_SEQ, dtype=jnp.int32)
    right_edge = SEQ - jax.random.randint(key_right, (BATCH, 1), 1, TOK_SEQ, dtype=jnp.int32)
    long_ids = (ladder[None, :] >= left_edge).astype(jnp.int32) + (ladder[None, :] >= right_edge).astype(jnp.int32)
    long_starts = jnp.where(ladder[None, :] >= right_edge, right_edge, jnp.where(ladder[None, :] >= left_edge, left_edge, 0))
    chosen = jax.random.randint(key_pick, (BATCH // SEQS, 1), 0, SEQS, dtype=jnp.int32)
    chosen_rows = jnp.repeat(chosen, SEQS, axis=0)
    is_long = jnp.arange(BATCH, dtype=jnp.int32)[:, None] % SEQS == chosen_rows
    return (jnp.where(is_long, long_ids, short_ids), jnp.where(is_long, long_starts, short_starts))


def draw_segment_ids(key, part):
    doc_ids, doc_starts = document_layout(key)
    return doc_ids


def draw_positions(key, part):
    doc_ids, doc_starts = document_layout(key)
    key = jax.random.fold_in(key, 5)
    offsets = jax.random.randint(key, (BATCH, 17), 0, 4096, dtype=jnp.int32)
    ladder = jnp.arange(SEQ, dtype=jnp.int32)
    picked = jnp.take_along_axis(offsets, doc_ids, axis=1)
    last_doc = doc_ids[:, SEQ - 1:]
    picked = jnp.where(doc_ids == last_doc, 4096 + doc_starts, jnp.where(doc_ids == 0, 0, picked))
    return ladder[None, :] - doc_starts + picked


def steps_of(own_key, extent, pieces, smallest, top_value):
    def one(dim, blocks):
        draws = jax.random.uniform(jax.random.fold_in(jax.random.fold_in(own_key, 6), dim), (blocks,), jnp.float32, smallest / len(pieces), top_value / len(pieces))
        return jnp.repeat(jnp.exp(draws), extent[dim] // blocks).reshape((-1,) + (1,) * (len(extent) - dim - 1))

    factor_of = one(*pieces[0])
    for cut in pieces[1:]:
        factor_of = factor_of * one(*cut)
    return factor_of


def normal_values(stream_key, dims, width, limit, shards=(), held_as=jnp.bfloat16):
    entries = width * jax.random.normal(stream_key, dims, jnp.float32)
    if shards:
        entries = entries * steps_of(stream_key, dims, shards, -0.22, 0.18)
    return jnp.clip(entries, -limit, limit).astype(held_as)


def setup_inputs(seed: int = 0) -> dict:
    splits = jax.random.split(jax.random.key(seed), 20)
    tokens = normal_values(splits[0], (BATCH, SEQ, D), 1.0, 6.0, ((0, 8), (1, 4)))
    segment_ids = draw_segment_ids(jax.random.fold_in(splits[19], 71), 0)
    positions = draw_positions(jax.random.fold_in(splits[19], 71), 0)
    cotangent = normal_values(splits[3], (BATCH, SEQ, D), 1.0, 6.0, ((0, 8), (1, 4)))
    qkv_weight = normal_values(splits[4], (D, QKV), D ** -0.5, 0.1875, ((0, 8),), jnp.float32)
    qkv_first = normal_values(splits[5], (D, QKV), (0.056 * TOKENS ** 0.5), 40.0, ((0, 8),), jnp.float32)
    qkv_second = jnp.clip(jnp.exp(math.log(868.352) - 1.40534252 * jax.random.uniform(splits[6], (D, QKV), jnp.float32) ** steps_of(splits[6], (D, QKV), ((0, 8),), -0.2, 0.2)), 212.992, 868.352)
    out_weight = normal_values(splits[7], (QUERY_FEATURES, D), (HEAD_SIZE // 4) ** -0.5, 1.0, ((0, 8),), jnp.float32)
    out_first = normal_values(splits[8], (QUERY_FEATURES, D), (0.011 * TOKENS ** 0.5), 8.0, ((0, 8),), jnp.float32)
    out_second = jnp.clip(jnp.exp(math.log(34.4064) - 1.3768155 * jax.random.uniform(splits[9], (QUERY_FEATURES, D), jnp.float32) ** steps_of(splits[9], (QUERY_FEATURES, D), ((0, 8),), -0.2, 0.2)), 8.68352, 34.4064)
    expand_weight = normal_values(splits[10], (D, 2 * FF), D ** -0.5, 0.1875, ((0, 8),), jnp.float32)
    expand_first = normal_values(splits[11], (D, 2 * FF), (0.033 * TOKENS ** 0.5), 24.0, ((0, 8),), jnp.float32)
    expand_second = jnp.clip(jnp.exp(math.log(311.296) - 1.3968765 * jax.random.uniform(splits[12], (D, 2 * FF), jnp.float32) ** steps_of(splits[12], (D, 2 * FF), ((0, 8),), -0.2, 0.2)), 77.0048, 311.296)
    shrink_weight = normal_values(splits[13], (FF, D), FF ** -0.5, 0.109375, ((0, 8),), jnp.float32)
    shrink_first = normal_values(splits[14], (FF, D), (0.056 * TOKENS ** 0.5), 40.0, ((0, 8),), jnp.float32)
    shrink_second = jnp.clip(jnp.exp(math.log(868.352) - 1.40534252 * jax.random.uniform(splits[15], (FF, D), jnp.float32) ** steps_of(splits[15], (FF, D), ((0, 8),), -0.2, 0.2)), 212.992, 868.352)
    norm_gains = jnp.clip(1.0 + 0.1 * jax.random.normal(splits[16], (GAINS,), jnp.float32), 0.5, 1.5)
    gains_first = normal_values(splits[17], (GAINS,), (0.17 * TOKENS ** 0.5), 128.0, ((0, 8),), jnp.float32)
    gains_second = jnp.clip(jnp.exp(math.log(7700.48) - 1.36524097 * jax.random.uniform(splits[18], (GAINS,), jnp.float32) ** steps_of(splits[18], (GAINS,), ((0, 8),), -0.2, 0.2)), 1966.08, 7700.48)
    return {"tokens": tokens, "segment_ids": segment_ids, "positions": positions, "cotangent": cotangent, "qkv_weight": qkv_weight, "qkv_first": qkv_first, "qkv_second": qkv_second, "out_weight": out_weight, "out_first": out_first, "out_second": out_second, "expand_weight": expand_weight, "expand_first": expand_first, "expand_second": expand_second, "shrink_weight": shrink_weight, "shrink_first": shrink_first, "shrink_second": shrink_second, "norm_gains": norm_gains, "gains_first": gains_first, "gains_second": gains_second}


EPS_NORM = 1e-06
ROPE_BASE = 1000000.0
MASKED_SCORE = -1e+30
BETA_ONE = 0.9
BETA_TWO = 0.95
ADAM_EPS = 1e-08
WEIGHT_DECAY = 0.1
RATE_QKV = 0.1
RATE_OUT = 0.5
RATE_EXPAND = 0.1
RATE_SHRINK = 0.06
RATE_GAINS = 0.6
PRECISE = lax.Precision.HIGHEST

@jax.custom_vjp
def reduced_copy(v):
    return lax.optimization_barrier(v.astype(jnp.bfloat16)).astype(jnp.float32)

@jax.custom_vjp
def low_back(v):
    return v

def low_keep(v):
    return (reduced_copy(v), None)

def low_pass(kept, grad):
    return (grad,)

def back_keep(v):
    return (v, None)

def back_low(kept, grad):
    return (reduced_copy(grad),)
reduced_copy.defvjp(low_keep, low_pass)
low_back.defvjp(back_keep, back_low)

def rms_scale(values, gain_vec):
    return values * lax.rsqrt(lax.optimization_barrier(jnp.mean(values * values, axis=-1, keepdims=True)) + EPS_NORM) * gain_vec

def rotate(values, places):
    half_size = values.shape[-1] // 2
    ladder = jnp.arange(half_size, dtype=jnp.float32)
    frequency = jnp.exp(ladder * (-2.0 * math.log(ROPE_BASE) / values.shape[-1]))
    angles = places.astype(jnp.float32)[:, None] * frequency[None, :]
    cosine = jnp.cos(angles)[:, None, :]
    sine_part = jnp.sin(angles)[:, None, :]
    first_half = values[..., :half_size]
    second_half = values[..., half_size:]
    return jnp.concatenate([first_half * cosine - second_half * sine_part, second_half * cosine + first_half * sine_part], axis=-1)

def split_heads(projected_output, g_query, g_key, places):
    token_row_list = projected_output.shape[0]
    query_rows = projected_output[:, :QUERY_FEATURES].reshape(token_row_list, QUERY_HEADS, HEAD_SIZE)
    key_entries = projected_output[:, QUERY_FEATURES:QUERY_FEATURES + KEY_FEATURES].reshape(token_row_list, KEY_VALUE_HEADS, HEAD_SIZE)
    value_entries = projected_output[:, QUERY_FEATURES + KEY_FEATURES:].reshape(token_row_list, KEY_VALUE_HEADS, HEAD_SIZE)
    return (rotate(rms_scale(query_rows, g_query), places), rotate(rms_scale(key_entries, g_key), places), value_entries)

def swiglu(gate_up):
    return jax.nn.silu(gate_up[:, :FF]) * gate_up[:, FF:]

def block_layer(inputs, params, segment, places):
    qkv_w, out_w, expand_w, shrink_w, gain_all = params
    qkv_w = reduced_copy(qkv_w)
    out_w = reduced_copy(out_w)
    expand_w = reduced_copy(expand_w)
    shrink_w = reduced_copy(shrink_w)
    gain_all = reduced_copy(gain_all)
    token_length = inputs.shape[0]
    head_groups = QUERY_HEADS // KEY_VALUE_HEADS
    normed = reduced_copy(rms_scale(inputs, gain_all[:D]))
    projected_output = low_back(jnp.dot(normed, qkv_w, precision=PRECISE))
    query_rows, key_entries, value_entries = split_heads(projected_output, gain_all[2 * D:2 * D + HEAD_SIZE], gain_all[2 * D + HEAD_SIZE:], places)
    query_rows = reduced_copy(query_rows).reshape(token_length, KEY_VALUE_HEADS, head_groups, HEAD_SIZE)
    key_entries = reduced_copy(key_entries)
    value_entries = reduced_copy(value_entries)
    scores = low_back(jnp.einsum('qkgd,skd->kgqs', query_rows, key_entries, precision=PRECISE) * HEAD_SIZE ** (-0.5))
    ladder = jnp.arange(token_length)
    allowed = (segment[:, None] == segment[None, :]) & (ladder[:, None] >= ladder[None, :])
    scores = jnp.where(allowed[None, None], scores, MASKED_SCORE)
    weights = reduced_copy(jax.nn.softmax(scores, axis=-1))
    attended = jnp.einsum('kgqs,skd->qkgd', weights, value_entries, precision=PRECISE).reshape(token_length, QUERY_FEATURES)
    attended = low_back(reduced_copy(attended))
    hidden_state = inputs + low_back(jnp.dot(attended, out_w, precision=PRECISE))
    normed_two = reduced_copy(rms_scale(hidden_state, gain_all[D:2 * D]))
    gate_up = low_back(jnp.dot(normed_two, expand_w, precision=PRECISE))
    active = low_back(reduced_copy(swiglu(gate_up)))
    return hidden_state + jnp.dot(active, shrink_w, precision=PRECISE)

def adam_step(weight, first_moment, second_moment, gradient, step_rate):
    first_moment = BETA_ONE * first_moment + (1.0 - BETA_ONE) * gradient
    second_moment = BETA_TWO * second_moment + (1.0 - BETA_TWO) * gradient * gradient
    fix_one = 1.0 - BETA_ONE ** STEP
    fix_two = 1.0 - BETA_TWO ** STEP
    step_dir = first_moment / fix_one / (jnp.sqrt(second_moment / fix_two) + ADAM_EPS)
    return (first_moment, second_moment, weight - step_rate * (step_dir + WEIGHT_DECAY * weight))

def reference(tokens, segment_ids, positions, cotangent, qkv_weight, qkv_first, qkv_second, out_weight, out_first, out_second, expand_weight, expand_first, expand_second, shrink_weight, shrink_first, shrink_second, norm_gains, gains_first, gains_second):
    params = (qkv_weight, out_weight, expand_weight, shrink_weight, norm_gains)

    def one_sequence(totals, sequence_items):
        inputs, segment, places, incoming = sequence_items

        def forward(values_in, weights_in):
            return block_layer(values_in, weights_in, segment, places)
        outputs, pullback = jax.vjp(forward, inputs.astype(jnp.float32), params)
        grad_in, grad_params = pullback(incoming.astype(jnp.float32))
        totals = jax.tree.map(jnp.add, totals, grad_params)
        return (totals, (outputs.astype(jnp.bfloat16), grad_in.astype(jnp.bfloat16)))
    zero_grads = jax.tree.map(jnp.zeros_like, params)
    totals, (outputs, grad_in) = lax.scan(one_sequence, zero_grads, (tokens, segment_ids, positions, cotangent))
    grad_qkv, grad_out, grad_expand, grad_shrink, grad_gains = totals
    qkv_m, qkv_v, qkv_w = adam_step(qkv_weight, qkv_first, qkv_second, grad_qkv, RATE_QKV)
    out_m, out_v, out_w = adam_step(out_weight, out_first, out_second, grad_out, RATE_OUT)
    expand_m, expand_v, expand_w = adam_step(expand_weight, expand_first, expand_second, grad_expand, RATE_EXPAND)
    shrink_m, shrink_v, shrink_w = adam_step(shrink_weight, shrink_first, shrink_second, grad_shrink, RATE_SHRINK)
    gains_m, gains_v, gains_w = adam_step(norm_gains, gains_first, gains_second, grad_gains, RATE_GAINS)
    return (outputs, grad_in, qkv_m, qkv_v, qkv_w, out_m, out_v, out_w, expand_m, expand_v, expand_w, shrink_m, shrink_v, shrink_w, gains_m, gains_v, gains_w)
```

```python
import functools
import math

import jax
import jax.numpy as jnp
from jax import lax
from jax.experimental import pallas as pl
from jax.experimental.pallas import tpu as pltpu
from jax.sharding import PartitionSpec as P

D = 1024
QUERY_HEADS = 16
KEY_VALUE_HEADS = 8
HEAD_SIZE = 128
FF = 3072
STEP = 10
QUERY_FEATURES = 2048
KEY_FEATURES = 1024
GROUP = QUERY_HEADS // KEY_VALUE_HEADS

EPS_NORM = 1e-06
ROPE_BASE = 1000000.0
MASKED_SCORE = -1e30
BETA_ONE = 0.9
BETA_TWO = 0.95
ADAM_EPS = 1e-08
WEIGHT_DECAY = 0.1
RATE_QKV = 0.1
RATE_OUT = 0.5
RATE_EXPAND = 0.1
RATE_SHRINK = 0.06
RATE_GAINS = 0.6

SCALE = HEAD_SIZE**-0.5
EXP_SCALE = SCALE * math.log2(math.e)
LOW = jnp.bfloat16
FULL = jnp.float32
MIB = 1 << 20
HALVES = 2


def dot_nn(a, b):
    return jnp.dot(a, b, preferred_element_type=FULL)


def dot_nt(a, b):
    return lax.dot_general(a, b, (((1,), (1,)), ((), ())), preferred_element_type=FULL)


def dot_tn(a, b):
    return lax.dot_general(a, b, (((0,), (0,)), ((), ())), preferred_element_type=FULL)


def inverse_rms(values):
    return lax.rsqrt(jnp.mean(values * values, axis=-1, keepdims=True) + EPS_NORM)


def norm_back(values, gain, incoming):
    scale = inverse_rms(values)
    normed = values * scale
    scaled = incoming * gain
    grad = scale * (scaled - normed * jnp.mean(scaled * normed, axis=-1, keepdims=True))
    return grad, incoming * normed


def adam_step(weight, first_moment, second_moment, gradient, step_rate):
    first_moment = BETA_ONE * first_moment + (1.0 - BETA_ONE) * gradient
    second_moment = BETA_TWO * second_moment + (1.0 - BETA_TWO) * gradient * gradient
    fix_one = 1.0 - BETA_ONE**STEP
    fix_two = 1.0 - BETA_TWO**STEP
    step_dir = first_moment / fix_one / (jnp.sqrt(second_moment / fix_two) + ADAM_EPS)
    return (first_moment, second_moment, weight - step_rate * (step_dir + WEIGHT_DECAY * weight))


def assemble(parts, whole, blocks):
    rows = whole.shape[0] // len(parts)
    for part, block in zip(parts, blocks):
        whole[pl.ds(pl.multiple_of(block * rows, rows), rows), :] = part[...]


def all_rows(place_ref, n, inner):
    return [(place_ref[0] ^ s) * inner + (place_ref[1] ^ t) for s in range(n) for t in range(inner)]


def chip_rows(place_ref, inner):
    return [
        ((place_ref[0] & 1) ^ k) * inner + (place_ref[1] ^ t) for k in range(2) for t in range(inner)
    ]


ANYWHERE = pl.BlockSpec(memory_space=pl.ANY)


def resident(shape, column=0):
    return pl.BlockSpec(shape, lambda *_: (0, column), pipeline_mode=pl.Buffered(1))


def project_kernel(n, inner, place_ref, *refs):
    parts = refs[: n * inner]
    pieces = refs[n * inner : n * inner + n]
    gain_ref, gain_q_ref, gain_k_ref, cos_ref, sin_ref = refs[n * inner + n : n * inner + n + 5]
    normed_ref, q_ref, k_ref, v_ref, raw_ref = refs[n * inner + n + 5 : n * inner + n + 10]
    weight, token = refs[n * inner + n + 10 :]
    step = pl.program_id(0)

    @pl.when(step == 0)
    def _():
        assemble(parts, weight, all_rows(place_ref, n, inner))

    for s in range(n):

        @pl.when((place_ref[0] ^ step) == s)
        def _():
            token[...] = pieces[s][...]

    x = token[...].astype(FULL)
    normed = (x * inverse_rms(x) * gain_ref[...]).astype(LOW)
    normed_ref[...] = normed
    projected = dot_nn(normed, weight[...])
    q_half, k_half = q_ref.shape[1] // HALVES, k_ref.shape[1] // HALVES
    raw_half = q_half + k_half
    half = raw_half + k_half
    cos, sin = cos_ref[...], sin_ref[...]

    def turn(values, gain):
        values = values * inverse_rms(values) * gain
        return (values * cos + pltpu.roll(values, HEAD_SIZE // 2, 1) * sin).astype(LOW)

    for i in range(HALVES):
        first = i * half
        raw_ref[:, i * raw_half : (i + 1) * raw_half] = projected[:, first : first + raw_half].astype(LOW)
        v_ref[:, i * k_half : (i + 1) * k_half] = projected[:, first + raw_half : first + half].astype(LOW)
        for h in range(0, q_half, HEAD_SIZE):
            values = projected[:, first + h : first + h + HEAD_SIZE]
            q_ref[:, i * q_half + h : i * q_half + h + HEAD_SIZE] = turn(values, gain_q_ref[...])
        for h in range(0, k_half, HEAD_SIZE):
            values = projected[:, first + q_half + h : first + q_half + h + HEAD_SIZE]
            k_ref[:, i * k_half + h : i * k_half + h + HEAD_SIZE] = turn(values, gain_k_ref[...])


def project(place, parts, pieces, gain, gain_q, gain_k, cos, sin):
    n = len(pieces)
    inner = len(parts) // n
    block = pieces[0].shape[0]
    length = n * block
    width = parts[0].shape[1]
    q_width, k_width = width // 2, width // 4
    whole = lambda j, p: (0, 0)
    natural = lambda j, p: (j, 0)
    return pl.pallas_call(
        functools.partial(project_kernel, n, inner),
        out_shape=(
            jax.ShapeDtypeStruct((length, D), LOW),
            jax.ShapeDtypeStruct((length, q_width), LOW),
            jax.ShapeDtypeStruct((length, k_width), LOW),
            jax.ShapeDtypeStruct((length, k_width), LOW),
            jax.ShapeDtypeStruct((length, q_width + k_width), LOW),
        ),
        grid_spec=pltpu.PrefetchScalarGridSpec(
            num_scalar_prefetch=1,
            grid=(n,),
            in_specs=[resident(p.shape) for p in parts]
            + [resident((block, D))] * n
            + [
                pl.BlockSpec((1, D), whole),
                pl.BlockSpec((1, HEAD_SIZE), whole),
                pl.BlockSpec((1, HEAD_SIZE), whole),
                pl.BlockSpec((block, HEAD_SIZE), natural),
                pl.BlockSpec((block, HEAD_SIZE), natural),
            ],
            out_specs=(
                pl.BlockSpec((block, D), natural),
                pl.BlockSpec((block, q_width), natural),
                pl.BlockSpec((block, k_width), natural),
                pl.BlockSpec((block, k_width), natural),
                pl.BlockSpec((block, q_width + k_width), natural),
            ),
            scratch_shapes=[
                pltpu.VMEM((D, width), LOW),
                pltpu.VMEM((block, D), LOW),
            ],
        ),
        compiler_params=pltpu.CompilerParams(vmem_limit_bytes=40 * MIB),
        cost_estimate=pl.CostEstimate(
            flops=2 * length * D * width, bytes_accessed=16 * MIB, transcendentals=0
        ),
        name="project",
    )(place, *parts, *pieces, gain, gain_q, gain_k, cos, sin)


def attend_kernel(n, inner, first, has_base, place_ref, *refs):
    parts = refs[: 2 * inner]
    q_ref, k_ref, v_ref, seg_col_ref, seg_row_ref = refs[2 * inner : 2 * inner + 5]
    rest = refs[2 * inner + 5 + (2 if has_base else 0) :]
    attended_ref, total_ref, share_ref, weight = rest
    block = q_ref.shape[0]
    heads = k_ref.shape[1] // HEAD_SIZE
    step = pl.program_id(0)

    @pl.when(step == 0)
    def _():
        assemble(parts, weight, chip_rows(place_ref, inner))

    def work(j):
        size = (j + 1) * block
        same = seg_col_ref[...] == seg_row_ref[:, :size]
        own = lax.broadcasted_iota(jnp.int32, (block, size), 0) + j * block
        key = lax.broadcasted_iota(jnp.int32, (block, size), 1)
        allowed = same & (own >= key)
        allowed = jnp.concatenate([allowed] * GROUP, axis=0)
        outs, totals = [], []
        for h in range(heads):
            lanes = slice(h * HEAD_SIZE, (h + 1) * HEAD_SIZE)
            q = jnp.concatenate(
                [
                    q_ref[:, (h * GROUP + g) * HEAD_SIZE : (h * GROUP + g + 1) * HEAD_SIZE]
                    for g in range(GROUP)
                ],
                axis=0,
            )
            scores = jnp.where(allowed, dot_nt(q, k_ref[:size, lanes]), MASKED_SCORE)
            top = jnp.max(scores, axis=-1, keepdims=True)
            weights = jnp.exp2((scores - top) * EXP_SCALE)
            total = jnp.sum(weights, axis=-1, keepdims=True)
            out = dot_nn(weights.astype(LOW), v_ref[:size, lanes]) / total
            log_total = top * EXP_SCALE + jnp.log2(total)
            for g in range(GROUP):
                outs.append(out[g * block : (g + 1) * block].astype(LOW))
                totals.append(log_total[g * block : (g + 1) * block])
        attended = jnp.concatenate(outs, axis=1)
        attended_ref[...] = attended
        share_ref[...] = dot_nn(attended, weight[...]).astype(LOW)
        lane = lax.broadcasted_iota(jnp.int32, (block, HEAD_SIZE), 1)
        packed = jnp.zeros((block, HEAD_SIZE), FULL)
        for i, column in enumerate(totals):
            packed = jnp.where(lane == i, column, packed)
        total_ref[...] = packed

    place = place_ref[0] ^ (first + step)
    for j in range(n):
        pl.when(place == j)(functools.partial(work, j))


def attend(place, parts, q, k, v, seg_col, seg_row, n, chip, base):
    inner = len(parts) // 2
    length, q_width = q.shape
    k_width = k.shape[1]
    block = length // n
    first = 2 * chip
    whole = lambda i, p: (0, 0)
    natural = lambda i, p: (p[0] ^ (first + i), 0)
    slot = lambda i, p: (first + i, 0)
    plain = lambda i, p: (i, 0)
    base = list(base or ())
    before = 1 + len(parts) + 5
    return pl.pallas_call(
        functools.partial(attend_kernel, n, inner, first, bool(base)),
        out_shape=(
            jax.ShapeDtypeStruct((length, q_width), LOW),
            jax.ShapeDtypeStruct((length, HEAD_SIZE), FULL),
            jax.ShapeDtypeStruct((2 * block, D), LOW),
        ),
        grid_spec=pltpu.PrefetchScalarGridSpec(
            num_scalar_prefetch=1,
            grid=(2,),
            in_specs=[resident(p.shape) for p in parts]
            + [
                pl.BlockSpec((block, q_width), natural),
                resident((length, k_width)),
                resident((length, k_width)),
                pl.BlockSpec((block, 1), natural),
                pl.BlockSpec((1, length), whole),
            ]
            + [ANYWHERE] * len(base),
            out_specs=(
                pl.BlockSpec((block, q_width), slot),
                pl.BlockSpec((block, HEAD_SIZE), slot),
                pl.BlockSpec((block, D), plain),
            ),
            scratch_shapes=[pltpu.VMEM((q_width, D), LOW)],
        ),
        input_output_aliases={before: 0, before + 1: 1} if base else {},
        compiler_params=pltpu.CompilerParams(vmem_limit_bytes=48 * MIB),
        cost_estimate=pl.CostEstimate(
            flops=4 * block * q_width * (D + 2 * length), bytes_accessed=8 * MIB, transcendentals=0
        ),
        name="attend",
    )(place, *parts, q, k, v, seg_col, seg_row, *base)


def feed_kernel(chips, place_ref, *refs):
    gates, ups, shrinks = refs[:chips], refs[chips : 2 * chips], refs[2 * chips : 3 * chips]
    own_ref, other_ref, c_ref, c_other_ref = refs[3 * chips : 3 * chips + 4]
    x_out, c_out, active_ref, grad_ref, share_ref, share_other, back_ref, back_other = refs[3 * chips + 4 :]
    mine = pl.program_id(0) == 0
    x = jnp.where(mine, own_ref[...], other_ref[...])
    c_near, c_far = c_ref[0], c_other_ref[0]
    c = jnp.concatenate([jnp.where(mine, c_near, c_far), jnp.where(mine, c_far, c_near)], axis=0)
    x_out[...] = x
    c_out[...] = c
    size = gates[0].shape[1]
    share, back = 0.0, 0.0
    for s in range(chips):
        here = slice(s * size, (s + 1) * size)
        there = slice((chips + s) * size, (chips + s + 1) * size)
        gate = dot_nn(x, gates[s][...])
        up = dot_nn(x, ups[s][...])
        grad_active = dot_nt(c, shrinks[s][...]).astype(LOW).astype(FULL)
        gated = jax.nn.sigmoid(gate)
        silu = gate * gated
        active = (silu * up).astype(LOW)
        grad_gate = (grad_active * up * gated * (1.0 + gate * (1.0 - gated))).astype(LOW)
        grad_up = (grad_active * silu).astype(LOW)
        active_ref[:, here] = active
        grad_ref[:, here] = grad_gate
        grad_ref[:, there] = grad_up
        share = share + dot_nn(active, shrinks[s][...])
        back = back + dot_nt(grad_gate, gates[s][...]) + dot_nt(grad_up, ups[s][...])
    share = share.astype(LOW)
    back = back.astype(LOW)

    @pl.when(mine)
    def _():
        share_ref[...] = share
        back_ref[...] = back

    @pl.when(jnp.logical_not(mine))
    def _():
        share_other[...] = share
        back_other[...] = back


def feed(place, n, expand, shrink, own, other, c, c_other):
    chips = n // 2
    rows = own.shape[0]
    size = FF // n
    whole = lambda i, p: (0, 0)
    flat = lambda i, p: (i, 0)
    core = lambda i, p: ((p[0] & 1) ^ i, 0, 0)
    once = pl.Buffered(1)
    gates = [
        pl.BlockSpec((D, size), lambda i, p, s=s: (0, 2 * s + (p[0] & 1)), pipeline_mode=once)
        for s in range(chips)
    ]
    ups = [
        pl.BlockSpec((D, size), lambda i, p, s=s: (0, n + 2 * s + (p[0] & 1)), pipeline_mode=once)
        for s in range(chips)
    ]
    shrinks = [
        pl.BlockSpec((size, D), lambda i, p, s=s: (2 * s + (p[0] & 1), 0), pipeline_mode=once)
        for s in range(chips)
    ]
    wide = lambda w: jax.ShapeDtypeStruct((2 * rows, w), LOW)
    part = jax.ShapeDtypeStruct((rows, D), LOW)
    return pl.pallas_call(
        functools.partial(feed_kernel, chips),
        out_shape=(wide(D), wide(D), wide(FF // 2), wide(FF), part, part, part, part),
        grid_spec=pltpu.PrefetchScalarGridSpec(
            num_scalar_prefetch=1,
            grid=(2,),
            in_specs=gates
            + ups
            + shrinks
            + [
                resident((rows, D)),
                resident((rows, D)),
                pl.BlockSpec((1, rows // 2, D), core),
                pl.BlockSpec((1, rows // 2, D), core),
            ],
            out_specs=(
                pl.BlockSpec((rows, D), flat),
                pl.BlockSpec((rows, D), flat),
                pl.BlockSpec((rows, FF // 2), flat),
                pl.BlockSpec((rows, FF), flat),
                pl.BlockSpec((rows, D), whole),
                pl.BlockSpec((rows, D), whole),
                pl.BlockSpec((rows, D), whole),
                pl.BlockSpec((rows, D), whole),
            ),
        ),
        compiler_params=pltpu.CompilerParams(vmem_limit_bytes=56 * MIB),
        cost_estimate=pl.CostEstimate(
            flops=12 * rows * D * FF, bytes_accessed=30 * MIB, transcendentals=0
        ),
        name="feed",
    )(place, *[expand] * (2 * chips), *[shrink] * chips, own, other, c, c_other)


def back_kernel(n, inner, half, place_ref, *refs):
    qkv_parts = refs[: n * inner]
    out_parts = refs[n * inner : (n + 2) * inner]
    refs = refs[(n + 2) * inner :]
    (
        h_ref,
        attended_ref,
        total_ref,
        q_ref,
        k_ref,
        v_ref,
        raw_ref,
        cos_ref,
        sin_ref,
        seg_col_ref,
        seg_row_ref,
        gain_q_ref,
        gain_k_ref,
    ) = refs[:13]
    refs = refs[13:]
    if half:
        base_ref, refs = refs[0], refs[1:]
    grad_ref, share_ref, gains_ref, qkv, out, key_sum, value_sum = refs
    block = q_ref.shape[0]
    heads = k_ref.shape[1] // HEAD_SIZE
    step = pl.program_id(0)

    @pl.when(step == 0)
    def _():
        assemble(qkv_parts, qkv, all_rows(place_ref, n, inner))
        rows = out_parts[0].shape[0]
        size = out.shape[0] // rows
        for part, spot in zip(out_parts, chip_rows(place_ref, inner)):

            @pl.when(spot // size == half)
            def _():
                out[pl.ds(pl.multiple_of((spot % size) * rows, rows), rows), :] = part[...]

        key_sum[...] = jnp.zeros_like(key_sum)
        value_sum[...] = jnp.zeros_like(value_sum)
        gains_ref[...] = jnp.zeros_like(gains_ref)

    def work(j):
        size = (j + 1) * block
        grad_attended = dot_nt(h_ref[...], out[...]).astype(LOW)
        attended = attended_ref[...]
        totals = total_ref[...].T
        same = seg_col_ref[:size, :] == seg_row_ref[:, j * block : size]
        key = lax.broadcasted_iota(jnp.int32, (size, block), 0)
        own = lax.broadcasted_iota(jnp.int32, (size, block), 1) + j * block
        allowed = same & (own >= key)
        allowed = jnp.concatenate([allowed] * GROUP, axis=1)
        cos, sin = cos_ref[...], sin_ref[...]
        gains = gains_ref[...]
        kind = lax.broadcasted_iota(jnp.int32, gains.shape, 0)

        def head_back(grad, values, gain):
            grad = grad * cos + pltpu.roll(grad * sin, HEAD_SIZE // 2, 1)
            grad, gain_part = norm_back(values.astype(FULL), gain, grad)
            return grad.astype(LOW), jnp.sum(gain_part, axis=0, keepdims=True)

        query_grads, key_grads, value_grads = [], [], []
        for h in range(heads):
            lanes = slice(h * HEAD_SIZE, (h + 1) * HEAD_SIZE)
            k, v = k_ref[:size, lanes], v_ref[:size, lanes]
            head_lanes = [
                slice((h * GROUP + g) * HEAD_SIZE, (h * GROUP + g + 1) * HEAD_SIZE)
                for g in range(GROUP)
            ]
            q = jnp.concatenate([q_ref[:, s] for s in head_lanes], axis=0)
            up = jnp.concatenate([grad_attended[:, s] for s in head_lanes], axis=0)
            seen = jnp.concatenate([attended[:, s] for s in head_lanes], axis=0)
            log_total = jnp.concatenate(
                [totals[(half * heads + h) * GROUP + g : (half * heads + h) * GROUP + g + 1, :] for g in range(GROUP)], axis=1
            )
            row = jnp.sum(up.astype(FULL) * seen.astype(FULL), axis=1, keepdims=True)
            row = jnp.broadcast_to(row, (GROUP * block, HEAD_SIZE)).T[:1, :]
            probs = jnp.where(allowed, jnp.exp2(dot_nt(k, q) * EXP_SCALE - log_total), 0.0)
            grad_probs = dot_nt(v, up)
            grad_scores = (probs * (grad_probs - row)).astype(LOW)
            value_sum[:size, lanes] += dot_nn(probs.astype(LOW), up)
            key_sum[:size, lanes] += dot_nn(grad_scores, q)
            query_grad = dot_tn(grad_scores, k) * SCALE
            for g in range(GROUP):
                grad, gain_part = head_back(
                    query_grad[g * block : (g + 1) * block], raw_ref[:, head_lanes[g]], gain_q_ref[...]
                )
                query_grads.append(grad)
                gains = jnp.where(kind == 0, gains + gain_part, gains)
        own_rows = slice(j * block, size)
        for h in range(heads):
            lanes = slice(h * HEAD_SIZE, (h + 1) * HEAD_SIZE)
            first = (heads * GROUP + h) * HEAD_SIZE
            grad, gain_part = head_back(
                key_sum[own_rows, lanes] * SCALE, raw_ref[:, first : first + HEAD_SIZE], gain_k_ref[...]
            )
            key_grads.append(grad)
            gains = jnp.where(kind == 1, gains + gain_part, gains)
            value_grads.append(value_sum[own_rows, lanes].astype(LOW))
        gains_ref[...] = gains
        grad = jnp.concatenate(query_grads + key_grads + value_grads, axis=1)
        grad_ref[...] = grad
        share = dot_nt(grad, qkv[...])
        if half:
            share = share + base_ref[...].astype(FULL)
        share_ref[...] = share.astype(LOW)

    for j in range(n):
        pl.when(step == n - 1 - j)(functools.partial(work, j))


def back(
    place, qkv_parts, out_parts, hidden_grad, attended, totals, q, k, v, raw, cos, sin, seg_col,
    seg_row, gain_q, gain_k, half, base,
):
    inner = len(out_parts) // 2
    n = len(qkv_parts) // inner
    length = q.shape[0]
    q_width, k_width = q.shape[1] // HALVES, k.shape[1] // HALVES
    block = length // n
    width = q_width + 2 * k_width
    whole = lambda i, p: (0, 0)
    natural = lambda i, p: (n - 1 - i, 0)
    slot = lambda i, p: (p[0] ^ (n - 1 - i), 0)
    natural_half = lambda i, p: (n - 1 - i, half)
    slot_half = lambda i, p: (p[0] ^ (n - 1 - i), half)
    base = [] if base is None else [base]
    return pl.pallas_call(
        functools.partial(back_kernel, n, inner, half),
        out_shape=(
            jax.ShapeDtypeStruct((length, width), LOW),
            jax.ShapeDtypeStruct((length, D), LOW),
            jax.ShapeDtypeStruct((8, HEAD_SIZE), FULL),
        ),
        grid_spec=pltpu.PrefetchScalarGridSpec(
            num_scalar_prefetch=1,
            grid=(n,),
            in_specs=[resident((p.shape[0], width), half) for p in qkv_parts]
            + [resident(p.shape) for p in out_parts]
            + [
                pl.BlockSpec((block, D), slot),
                pl.BlockSpec((block, q_width), slot_half),
                pl.BlockSpec((block, HEAD_SIZE), slot),
                pl.BlockSpec((block, q_width), natural_half),
                resident((length, k_width), half),
                resident((length, k_width), half),
                pl.BlockSpec((block, q_width + k_width), natural_half),
                pl.BlockSpec((block, HEAD_SIZE), natural),
                pl.BlockSpec((block, HEAD_SIZE), natural),
                pl.BlockSpec((length, 1), whole),
                pl.BlockSpec((1, length), whole),
                pl.BlockSpec((1, HEAD_SIZE), whole),
                pl.BlockSpec((1, HEAD_SIZE), whole),
            ]
            + [pl.BlockSpec((block, D), slot)] * len(base),
            out_specs=(
                pl.BlockSpec((block, width), natural),
                pl.BlockSpec((block, D), slot),
                pl.BlockSpec((8, HEAD_SIZE), whole),
            ),
            scratch_shapes=[
                pltpu.VMEM((D, width), LOW),
                pltpu.VMEM((q_width, D), LOW),
                pltpu.VMEM((length, k_width), FULL),
                pltpu.VMEM((length, k_width), FULL),
            ],
        ),
        compiler_params=pltpu.CompilerParams(vmem_limit_bytes=56 * MIB),
        cost_estimate=pl.CostEstimate(
            flops=2 * length * D * (q_width + width) + 5 * length * length * q_width,
            bytes_accessed=30 * MIB,
            transcendentals=0,
        ),
        name="back",
    )(
        place, *qkv_parts, *out_parts, hidden_grad, attended, totals, q, k, v, raw, cos, sin,
        seg_col, seg_row, gain_q, gain_k, *base,
    )


def adam_kernel(rate, blocks, key_ref, *refs):
    cuts = refs[:HALVES]
    weight_ref, first_ref, second_ref, new_first, new_second, new_weight, grad = refs[HALVES:]
    for i in range(HALVES):

        @pl.when(pl.program_id(0) // blocks == i)
        def _():
            grad[...] = cuts[i][0].astype(FULL)

    results = adam_step(weight_ref[...], first_ref[...], second_ref[...], grad[...], rate)
    new_first[...], new_second[...], new_weight[...] = results


def adam_cuts(key, cuts, weight, first, second, rate, size, column):
    chips, rows, columns = cuts[0].shape
    blocks = columns // size
    place = lambda i, s, p: (0, column(i, s))
    slot = lambda i, s, p: (p[0] ^ s, 0, i % blocks)
    spec = pl.BlockSpec((rows, size), place)
    shape = jax.ShapeDtypeStruct(weight.shape, FULL)
    return pl.pallas_call(
        functools.partial(adam_kernel, rate, blocks),
        out_shape=(shape, shape, shape),
        grid_spec=pltpu.PrefetchScalarGridSpec(
            num_scalar_prefetch=1,
            grid=(HALVES * blocks, chips),
            in_specs=[pl.BlockSpec((1, rows, size), slot)] * HALVES + [spec] * 3,
            out_specs=(spec,) * 3,
            scratch_shapes=[pltpu.VMEM((rows, size), FULL)],
        ),
        cost_estimate=pl.CostEstimate(
            flops=20 * weight.size, bytes_accessed=26 * weight.size, transcendentals=weight.size
        ),
        compiler_params=pltpu.CompilerParams(vmem_limit_bytes=24 * MIB),
        name="adam_cuts",
    )(key, *cuts, weight, first, second)


def adam_pair_kernel(rate, place_ref, own_ref, other_ref, weight_ref, first_ref, second_ref, *outs):
    mine = pl.program_id(1) == (place_ref[0] & 1)
    grad = jnp.where(mine, own_ref[...].astype(FULL), other_ref[...].astype(FULL))
    results = adam_step(weight_ref[...], first_ref[...], second_ref[...], grad, rate)
    outs[0][...], outs[1][...], outs[2][...] = results


def adam_pair(place, own, other, weight, first, second, rate, size):
    rows, width = own.shape
    cut = pl.BlockSpec((rows, size), lambda i, c, p: (0, i))
    spec = pl.BlockSpec((rows, size), lambda i, c, p: (0, 2 * i + c))
    shape = jax.ShapeDtypeStruct(weight.shape, FULL)
    return pl.pallas_call(
        functools.partial(adam_pair_kernel, rate),
        out_shape=(shape, shape, shape),
        grid_spec=pltpu.PrefetchScalarGridSpec(
            num_scalar_prefetch=1,
            grid=(width // size, 2),
            in_specs=[cut, cut] + [spec] * 3,
            out_specs=(spec,) * 3,
        ),
        cost_estimate=pl.CostEstimate(
            flops=20 * weight.size, bytes_accessed=26 * weight.size, transcendentals=weight.size
        ),
        compiler_params=pltpu.CompilerParams(vmem_limit_bytes=24 * MIB),
        name="adam_pair",
    )(place, own, other, weight, first, second)


def sum_kernel(lead, take, key_ref, kept_ref, landed_ref, *outs):
    size = outs[0].shape
    kept, landed = kept_ref[...].reshape(size), landed_ref[...].reshape(size)
    if take:
        total = jnp.where(key_ref[0] > 0, landed, kept)
    else:
        total = (kept.astype(FULL) + landed.astype(FULL)).astype(LOW)
    for s in range(lead):

        @pl.when(pl.program_id(0) == s)
        def _():
            outs[s][...] = total


def sum_parts(key, kept, kept_map, landed, landed_map, lead, steps, rows, take=False):
    columns = kept.shape[-1]

    def spec(array, place):
        ones = (1,) * (array.ndim - 2)
        return pl.BlockSpec(ones + (rows, columns), lambda i, j, p: (*place(i, j, p), 0))

    def out(s):
        spot = lambda i, j: jnp.where(i == s, j, jnp.where(i < s, 0, steps - 1))
        return pl.BlockSpec((1, rows, columns), lambda i, j, p: (spot(i, j), 0, 0))

    return pl.pallas_call(
        functools.partial(sum_kernel, lead, take),
        out_shape=(jax.ShapeDtypeStruct((steps, rows, columns), LOW),) * lead,
        grid_spec=pltpu.PrefetchScalarGridSpec(
            num_scalar_prefetch=1,
            grid=(lead, steps),
            in_specs=[spec(kept, kept_map), spec(landed, landed_map)],
            out_specs=tuple(out(s) for s in range(lead)),
        ),
        cost_estimate=pl.CostEstimate(flops=0, bytes_accessed=0, transcendentals=0),
        name="sum_parts",
    )(key, kept, landed)


def stack_kernel(*refs):
    for s, ref in enumerate(refs[:-1]):
        refs[-1][s] = ref[...]


def stack_parts(parts):
    rows, columns = parts[0].shape
    return pl.pallas_call(
        stack_kernel,
        out_shape=jax.ShapeDtypeStruct((len(parts), rows, columns), LOW),
        cost_estimate=pl.CostEstimate(flops=0, bytes_accessed=0, transcendentals=0),
        name="stack_parts",
    )(*parts)


def after(value, *others):
    return lax.optimization_barrier((value, *others))[0]


def make(n, inner, reps):
    chips = n // 2

    def swap_ctx(value, s):
        return lax.ppermute(value, "ctx", [(i, i ^ s) for i in range(n)])

    def swap_core(value):
        return swap_ctx(value, 1)

    def swap_chip(value, s):
        return swap_ctx(value, 2 * s)

    def swap_grp(value, t):
        return lax.ppermute(value, "grp", [(i, i ^ t) for i in range(inner)])

    def swap_rep(value, r):
        return lax.ppermute(value, "rep", [(i, i ^ r) for i in range(reps)])

    def over_chips(value):
        return [value] + [swap_chip(value, s) for s in range(1, chips)]

    def over_grp(value):
        return [value] + [swap_grp(value, t) for t in range(1, inner)]

    def sum_of(parts):
        total = parts[0].astype(FULL)
        for part in parts[1:]:
            total = total + part.astype(FULL)
        return total

    def swap_plane(value, s, t):
        pairs = [(c * inner + g, (c ^ s) * inner + (g ^ t)) for c in range(n) for g in range(inner)]
        return lax.ppermute(value, ("ctx", "grp"), pairs)

    def pick(value, axis, index):
        return lax.dynamic_index_in_dim(value, index, axis, False)

    middle = reps // 2
    hops = [([(k, k + 1), (reps - 1 - k, reps - 2 - k)], None) for k in range(middle - 1)]
    hops.append(([(middle - 1, middle), (middle, middle - 1)], None))
    hops += [
        ([(k, k - 1), (reps - 1 - k, reps - k)], (k - 1, reps - k)) for k in range(middle - 1, 0, -1)
    ]

    def gather_reps(value):
        return [value] + [swap_rep(value, r) for r in range(1, reps)]

    def on_device(
        tokens,
        segment_ids,
        positions,
        cotangent,
        qkv_weight,
        qkv_first,
        qkv_second,
        out_weight,
        out_first,
        out_second,
        expand_weight,
        expand_first,
        expand_second,
        shrink_weight,
        shrink_first,
        shrink_second,
        norm_gains,
        gains_first,
        gains_second,
    ):
        seqs, block, _ = tokens.shape
        length = n * block
        me = lax.axis_index("ctx")
        core = me & 1
        chip = me >> 1
        mine = lax.axis_index("grp")
        place = jnp.stack([me, mine]).astype(jnp.int32)
        order = me ^ jnp.arange(n)
        q_width = QUERY_FEATURES // chips
        k_width = KEY_FEATURES // chips
        width = q_width + 2 * k_width
        rows = qkv_weight.shape[0]

        rep = lax.axis_index("rep")

        def qkv_piece(s):
            to = chip ^ s
            parts = []
            for i in range(HALVES):
                for first, size in ((0, q_width), (QUERY_FEATURES, k_width), (QUERY_FEATURES + KEY_FEATURES, k_width)):
                    start = first + to * size + i * (size // HALVES)
                    parts.append(lax.dynamic_slice_in_dim(qkv_weight, start, size // HALVES, 1))
            return jnp.concatenate(parts, axis=1).astype(LOW)

        small = jnp.concatenate(
            [
                segment_ids.reshape(-1).astype(FULL),
                positions.reshape(-1).astype(FULL),
                norm_gains.astype(LOW).astype(FULL),
            ]
        ).reshape(1, -1)
        small = [
            swap_plane(small, s, t) if s or t else small for s in range(n) for t in range(inner)
        ]
        tokens, qkv_low, out_low, expand_low, shrink_low, other_tokens, *small = lax.optimization_barrier(
            (
                tokens,
                [qkv_piece(s) for s in range(chips)],
                out_weight.astype(LOW),
                expand_weight.astype(LOW),
                shrink_weight.astype(LOW),
                pick(tokens, 0, core ^ 1),
                *small,
            )
        )
        small = jnp.stack(small)
        small = small.reshape(n, inner, -1)[order]
        notes = small[:, 0, : 2 * seqs * block].reshape(n, 2, seqs, block)
        notes = pick(notes, 2, core)
        notes = jnp.moveaxis(notes, 0, 1).reshape(2, length)
        gains = small[:, mine ^ jnp.arange(inner), 2 * seqs * block :].reshape(1, -1)
        gain_one, gain_two = gains[:, :D], gains[:, D : 2 * D]
        gain_query = gains[:, 2 * D : 2 * D + HEAD_SIZE]
        gain_key = gains[:, 2 * D + HEAD_SIZE :]

        token_slots = [pick(tokens, 0, core), swap_core(other_tokens)]
        for s in range(1, chips):
            token_slots += [swap_chip(part, s) for part in token_slots[:2]]

        landed = [qkv_low[0]] + [swap_chip(qkv_low[s], s) for s in range(1, chips)]
        qkv_parts = []
        for part in landed:
            near = over_grp(part)
            qkv_parts += near + [swap_core(p) for p in near]

        near = over_grp(out_low)
        out_parts = near + [swap_core(p) for p in near]
        expand_full = lax.all_gather(expand_low, ("ctx", "grp"), axis=0, tiled=True)
        shrink_full = lax.all_gather(shrink_low, ("ctx", "grp"), axis=0, tiled=True)
        other_cotangent = swap_core(cotangent)

        ladder = jnp.arange(HEAD_SIZE) % (HEAD_SIZE // 2)
        frequency = jnp.exp(ladder.astype(FULL) * (-2.0 * math.log(ROPE_BASE) / HEAD_SIZE))
        angles = notes[1][:, None] * frequency[None, :]
        sign = jnp.where(jnp.arange(HEAD_SIZE) < HEAD_SIZE // 2, -1.0, 1.0)
        cos, sin = jnp.cos(angles), jnp.sin(angles) * sign
        seg_col, seg_row = notes[0][:, None], notes[0][None, :]

        normed, q, k, v, raw = project(
            place, qkv_parts, token_slots, gain_one, gain_query, gain_key, cos, sin
        )
        base, shares = None, []
        for s in range(chips - 1, -1, -1):
            *base, share = attend(place, out_parts, q, k, v, seg_col, seg_row, n, s, base)
            shares.append(swap_chip(share, s) if s else share)
        attended, totals = base
        inputs = jnp.concatenate(token_slots[:2]).astype(FULL)
        hidden = inputs + sum_of(shares)
        normed_two = (hidden * inverse_rms(hidden) * gain_two).astype(LOW)

        x_all, c_all, active, grad_gate_up, share, share_other, back_share, back_other = feed(
            place, n, expand_full, shrink_full, normed_two, swap_core(normed_two), cotangent,
            other_cotangent,
        )
        normed_grad = sum_of([back_share, swap_core(back_other)])
        hidden_grad, gain_part = norm_back(hidden, gain_two, normed_grad)
        gain_two_grad = jnp.sum(gain_part, axis=0)
        hidden_grad = hidden_grad + c_all[: 2 * block].astype(FULL)
        hidden_low = hidden_grad.astype(LOW)
        grad_slots = over_chips(hidden_low)
        grad_all = jnp.concatenate(grad_slots)

        def by_sequence(kept, landed):
            return jnp.where(core == 0, jnp.stack([kept, landed]), jnp.stack([landed, kept]))

        output = (hidden + sum_of([share, swap_core(share_other)])).astype(LOW)
        output = by_sequence(output[:block], swap_core(output[block:]))

        where = jnp.stack([chip, core, mine]).astype(jnp.int32)
        ends = {}
        for _, takes in hops:
            if takes:
                ends[takes] = ((rep == takes[0]) | (rep == takes[1])).astype(jnp.int32).reshape(1)
        line = []

        def next_sums(kept, kept_map, sent, sent_map, lead, steps, block_rows):
            for i, value in enumerate(sent):
                value = after(value, *line)
                totals = sum_parts(where, kept, kept_map, value, sent_map, lead, steps, block_rows)
                if i + 1 < len(sent):
                    kept, kept_map = jnp.stack(totals), lambda i, j, p: (i, j, 0)
            line[:] = [totals[0]]
            return totals

        def next_sum(kept, sent):
            plain = lambda i, j, p: (j, 0)
            for value in sent:
                value = after(value, *line)
                steps, block_rows = kept.shape[:2]
                (kept,) = sum_parts(where, kept, plain, value, plain, 1, steps, block_rows)
            line[:] = [kept]
            return kept

        def go(value, step=0):
            return [value, lax.ppermute(value, "rep", hops[step][0]), step]

        def step_on(trip):
            value, landed, step = trip
            if step == len(hops):
                return
            landed = after(landed, *line)
            takes = hops[step][1]
            plain = lambda i, j, p: (j, 0)
            (value,) = sum_parts(
                where if takes is None else ends[takes], value, plain, landed, plain, 1,
                value.shape[0], value.shape[1], takes is not None,
            )
            line[:] = [value]
            step += 1
            trip[:] = go(value, step) if step < len(hops) else [value, None, step]

        def send_x(parts):
            return parts[0], [swap_chip(parts[s], s) for s in range(1, chips)]

        def send_y(parts):
            return parts[0], [swap_grp(parts[t], t) for t in range(1, inner)]

        def back_part(half, attended, back_all):
            return back(
                place, qkv_parts, out_parts, grad_all, attended, totals, q, k, v, raw, cos, sin,
                seg_col, seg_row, gain_query, gain_key, half, back_all,
            )

        def cut_qkv(grad):
            grad_qkv = dot_tn(normed, grad).astype(LOW)
            cuts = grad_qkv.reshape(chips, 2, inner, rows, width // HALVES)
            return cuts, swap_core(pick(cuts, 1, core ^ 1))

        def sum_qkv_core(cuts, landed):
            return next_sums(
                cuts, lambda i, j, p: (j, p[1], p[2] ^ i, 0), [landed], lambda i, j, p: (j, p[2] ^ i, 0),
                inner, chips, rows,
            )

        def sum_by_chip(kept, sent, block_rows):
            place_of = lambda i, j, p: (p[0] ^ i, 0)
            return next_sums(kept, place_of, sent, place_of, chips, 1, block_rows)

        x_late, active_late = lax.optimization_barrier((x_all, active, hidden_low))[:2]
        grad_expand = dot_tn(x_late, grad_gate_up).astype(LOW)
        expand_cuts = grad_expand.reshape(chips, 2, inner, rows, FF)
        cut = pick(expand_cuts, 1, core ^ 1)
        other_sent = [swap_grp(pick(cut, 1, mine ^ t), t) for t in range(1, inner)]
        grad_shrink = dot_tn(active_late, c_all).astype(LOW)
        ff_rows = FF // (n * inner)
        shrink_cuts = grad_shrink.reshape(chips, inner, ff_rows, D)
        shrink_sent = [swap_grp(pick(shrink_cuts, 1, mine ^ t), t) for t in range(1, inner)]
        cut = pick(expand_cuts, 1, core)

        def own_rows(t, s):
            return pick(pick(cut, 0, chip ^ s), 0, mine ^ t)

        far_sent = [
            [swap_chip(after(own_rows(t, s), grad_slots[-1]), s) for s in range(1, chips)]
            for t in range(1, inner)
        ]

        grad_out = dot_tn(attended, grad_all).astype(LOW)
        out_rows = out_weight.shape[0]
        out_cuts = grad_out.reshape(2, inner, out_rows, D)
        out_sent = swap_core(pick(out_cuts, 0, core ^ 1))
        attended = after(attended, out_cuts)
        grad_one, back_all, gains_one = back_part(0, attended, None)

        line[:] = [gains_one]
        first_cuts, first_landed = cut_qkv(grad_one)
        other_cut = send_x(
            next_sums(
                expand_cuts, lambda i, j, p: (p[0] ^ i, p[1] ^ 1, p[2], 0), other_sent,
                lambda i, j, p: (p[0] ^ i, 0), chips, 1, rows,
            )
        )
        own_sent = []
        for t in range(1, inner):
            sent = [value[None] for value in far_sent[t - 1]]
            (total,) = next_sums(
                expand_cuts, lambda i, j, p, t=t: (p[0], p[1], p[2] ^ t, 0), sent,
                lambda i, j, p: (j, 0), 1, 1, rows,
            )
            own_sent.append(swap_grp(total, t))
        near_sent = [swap_chip(after(own_rows(0, s), *line), s)[None] for s in range(1, chips)]
        out_cut = send_y(
            next_sums(
                out_cuts, lambda i, j, p: (p[1], p[2] ^ i, 0), [out_sent],
                lambda i, j, p: (p[2] ^ i, 0), inner, 1, out_rows,
            )
        )
        attended, back_all = lax.optimization_barrier((attended, back_all, first_cuts, *line))[:2]
        grad_two, back_all, gains_two = back_part(1, attended, back_all)

        line[:] = [gains_two]
        (own_cut,) = next_sums(
            expand_cuts, lambda i, j, p: (p[0], p[1], p[2], 0), near_sent, lambda i, j, p: (j, 0), 1, 1, rows
        )
        shrink_cut = send_x(
            next_sums(
                shrink_cuts, lambda i, j, p: (p[0] ^ i, p[2], 0), shrink_sent,
                lambda i, j, p: (p[0] ^ i, 0), chips, 1, ff_rows,
            )
        )
        other_cut = swap_core(next_sum(*other_cut))
        own = go(next_sum(own_cut, own_sent))
        first_cut = send_y(sum_qkv_core(first_cuts, first_landed))
        second_cuts, second_landed = cut_qkv(after(grad_two, *line))
        other_cut = after(other_cut, *line)
        line[:] = [other_cut]
        other = go(other_cut)
        second_cut = send_y(sum_qkv_core(second_cuts, second_landed))
        shares = []
        for s in range(1, chips):
            share = after(back_all[2 * s * block : 2 * (s + 1) * block], *line)
            shares.append(swap_chip(share, s))
        out = go(next_sum(*out_cut))
        shrink = go(next_sum(*shrink_cut))

        def stacked(on_the_way):
            kept, sent = on_the_way
            total = stack_parts([kept[0]] + [after(value, *line)[0] for value in sent])
            line[:] = [total]
            return total

        step_on(own)
        first_cut = send_x(sum_by_chip(*first_cut, rows))
        step_on(other)
        second_cut = send_x(sum_by_chip(*second_cut, rows))
        first = go(stacked(first_cut))
        step_on(own)

        shares = [back_all[: 2 * block]] + [after(value, *line) for value in shares]
        input_part, gain_part = norm_back(inputs, gain_one, sum_of(shares))
        gain_one_grad = jnp.sum(gain_part, axis=0)
        input_grad = (input_part + hidden_grad).astype(LOW)
        input_landed = swap_core(input_grad[block:])
        head_gains = gains_one + gains_two
        grad_gains = jnp.concatenate([gain_one_grad, gain_two_grad, head_gains[0], head_gains[1]])
        grad_gains = grad_gains.reshape(n, inner, 1, -1)
        gains_sent = [
            swap_plane(pick(pick(grad_gains, 0, me ^ s), 0, mine ^ t), s, t)
            for s in range(n)
            for t in range(inner)
            if s or t
        ]
        line[:] = [gain_one_grad]

        step_on(out)
        second = go(stacked(second_cut))
        step_on(other)
        step_on(own)
        gains_sent = lax.optimization_barrier((*gains_sent, *line))[:-1]
        total_gains = sum_of([pick(pick(grad_gains, 0, me), 0, mine), *gains_sent])
        gains_sent = gather_reps(total_gains)
        step_on(shrink)
        step_on(out)
        step_on(other)
        step_on(first)
        step_on(shrink)
        step_on(out)
        step_on(second)
        step_on(first)
        step_on(shrink)
        step_on(second)
        step_on(first)
        step_on(second)
        trips = (own, other, out, shrink, first, second)
        for _ in hops:
            for trip in trips:
                step_on(trip)
        own_cut, other_cut, total_out, total_shrink, *qkv_cuts = [trip[0] for trip in trips]
        total_shrink, total_out, other_cut, own_cut = (
            value[0] for value in (total_shrink, total_out, other_cut, own_cut)
        )
        total_gains = sum_of(lax.optimization_barrier((*gains_sent, *line))[:-1])[0]
        input_grad = by_sequence(input_grad[:block], input_landed)

        size = k_width // HALVES

        def qkv_column(i, s):
            per_half = width // HALVES // size
            half, i = i // per_half, i % per_half
            q_blocks = q_width // HALVES // size
            q_place = (s * HALVES + half) * q_blocks + i
            k_place = QUERY_FEATURES // size + s * HALVES + half
            v_place = k_place + KEY_FEATURES // size
            return jnp.where(i < q_blocks, q_place, jnp.where(i == q_blocks, k_place, v_place))

        key = chip.reshape(1).astype(jnp.int32)
        return (
            output,
            input_grad,
            *adam_cuts(key, qkv_cuts, qkv_weight, qkv_first, qkv_second, RATE_QKV, size, qkv_column),
            *adam_step(out_weight, out_first, out_second, total_out.astype(FULL), RATE_OUT),
            *adam_pair(
                place, own_cut, other_cut, expand_weight, expand_first, expand_second, RATE_EXPAND,
                FF // n,
            ),
            *adam_step(
                shrink_weight, shrink_first, shrink_second, total_shrink.astype(FULL), RATE_SHRINK
            ),
            *adam_step(norm_gains, gains_first, gains_second, total_gains, RATE_GAINS),
        )

    return on_device


def solution(mesh):
    token_rows = P(("grp", "rep"), "ctx", None)
    token_notes = P(("grp", "rep"), "ctx")
    weight_rows = P(("ctx", "grp"), None)
    gain_rows = P(("ctx", "grp"))
    states = (weight_rows,) * 12 + (gain_rows,) * 3
    return jax.shard_map(
        make(mesh.shape["ctx"], mesh.shape["grp"], mesh.shape["rep"]),
        mesh=mesh,
        in_specs=(token_rows, token_notes, token_notes, token_rows) + states,
        out_specs=(token_rows, token_rows) + states,
        check_vma=False,
    )
```

```python
import functools
import math

import jax
import jax.numpy as jnp
from jax import lax
from jax.experimental import pallas as pl
from jax.experimental.pallas import tpu as pltpu
from jax.sharding import PartitionSpec as P

D = 1024
QUERY_HEADS = 16
KEY_VALUE_HEADS = 8
HEAD_SIZE = 128
FF = 3072
STEP = 10
QUERY_FEATURES = 2048
KEY_FEATURES = 1024
GROUP = QUERY_HEADS // KEY_VALUE_HEADS

EPS_NORM = 1e-06
ROPE_BASE = 1000000.0
MASKED_SCORE = -1e30
BETA_ONE = 0.9
BETA_TWO = 0.95
ADAM_EPS = 1e-08
WEIGHT_DECAY = 0.1
RATE_QKV = 0.1
RATE_OUT = 0.5
RATE_EXPAND = 0.1
RATE_SHRINK = 0.06
RATE_GAINS = 0.6

SCALE = HEAD_SIZE**-0.5
EXP_SCALE = SCALE * math.log2(math.e)
LOW = jnp.bfloat16
FULL = jnp.float32
MIB = 1 << 20
HALVES = 2


def dot_nn(a, b):
    return jnp.dot(a, b, preferred_element_type=FULL)


def dot_nt(a, b):
    return lax.dot_general(a, b, (((1,), (1,)), ((), ())), preferred_element_type=FULL)


def dot_tn(a, b):
    return lax.dot_general(a, b, (((0,), (0,)), ((), ())), preferred_element_type=FULL)


def inverse_rms(values):
    return lax.rsqrt(jnp.mean(values * values, axis=-1, keepdims=True) + EPS_NORM)


def norm_back(values, gain, incoming):
    scale = inverse_rms(values)
    normed = values * scale
    scaled = incoming * gain
    grad = scale * (scaled - normed * jnp.mean(scaled * normed, axis=-1, keepdims=True))
    return grad, incoming * normed


def adam_step(weight, first_moment, second_moment, gradient, step_rate):
    first_moment = BETA_ONE * first_moment + (1.0 - BETA_ONE) * gradient
    second_moment = BETA_TWO * second_moment + (1.0 - BETA_TWO) * gradient * gradient
    fix_one = 1.0 - BETA_ONE**STEP
    fix_two = 1.0 - BETA_TWO**STEP
    step_dir = first_moment / fix_one / (jnp.sqrt(second_moment / fix_two) + ADAM_EPS)
    return (first_moment, second_moment, weight - step_rate * (step_dir + WEIGHT_DECAY * weight))


def assemble(parts, whole, blocks):
    rows = whole.shape[0] // len(parts)
    for part, block in zip(parts, blocks):
        whole[pl.ds(pl.multiple_of(block * rows, rows), rows), :] = part[...]


def all_rows(place_ref, n, inner):
    return [(place_ref[0] ^ s) * inner + (place_ref[1] ^ t) for s in range(n) for t in range(inner)]


def chip_rows(place_ref, inner):
    return [
        ((place_ref[0] & 1) ^ k) * inner + (place_ref[1] ^ t) for k in range(2) for t in range(inner)
    ]


ANYWHERE = pl.BlockSpec(memory_space=pl.ANY)


def resident(shape, column=0):
    return pl.BlockSpec(shape, lambda *_: (0, column), pipeline_mode=pl.Buffered(1))


def project_kernel(n, inner, place_ref, *refs):
    parts = refs[: n * inner]
    pieces = refs[n * inner : n * inner + n]
    gain_ref, gain_q_ref, gain_k_ref, cos_ref, sin_ref = refs[n * inner + n : n * inner + n + 5]
    normed_ref, q_ref, k_ref, v_ref, raw_ref = refs[n * inner + n + 5 : n * inner + n + 10]
    weight, token = refs[n * inner + n + 10 :]
    step = pl.program_id(0)

    @pl.when(step == 0)
    def _():
        assemble(parts, weight, all_rows(place_ref, n, inner))

    for s in range(n):

        @pl.when((place_ref[0] ^ step) == s)
        def _():
            token[...] = pieces[s][...]

    x = token[...].astype(FULL)
    normed = (x * inverse_rms(x) * gain_ref[...]).astype(LOW)
    normed_ref[...] = normed
    projected = dot_nn(normed, weight[...])
    q_half, k_half = q_ref.shape[1] // HALVES, k_ref.shape[1] // HALVES
    raw_half = q_half + k_half
    half = raw_half + k_half
    cos, sin = cos_ref[...], sin_ref[...]

    def turn(values, gain):
        values = values * inverse_rms(values) * gain
        return (values * cos + pltpu.roll(values, HEAD_SIZE // 2, 1) * sin).astype(LOW)

    for i in range(HALVES):
        first = i * half
        raw_ref[:, i * raw_half : (i + 1) * raw_half] = projected[:, first : first + raw_half].astype(LOW)
        v_ref[:, i * k_half : (i + 1) * k_half] = projected[:, first + raw_half : first + half].astype(LOW)
        for h in range(0, q_half, HEAD_SIZE):
            values = projected[:, first + h : first + h + HEAD_SIZE]
            q_ref[:, i * q_half + h : i * q_half + h + HEAD_SIZE] = turn(values, gain_q_ref[...])
        for h in range(0, k_half, HEAD_SIZE):
            values = projected[:, first + q_half + h : first + q_half + h + HEAD_SIZE]
            k_ref[:, i * k_half + h : i * k_half + h + HEAD_SIZE] = turn(values, gain_k_ref[...])


def project(place, parts, pieces, gain, gain_q, gain_k, cos, sin):
    n = len(pieces)
    inner = len(parts) // n
    block = pieces[0].shape[0]
    length = n * block
    width = parts[0].shape[1]
    q_width, k_width = width // 2, width // 4
    whole = lambda j, p: (0, 0)
    natural = lambda j, p: (j, 0)
    return pl.pallas_call(
        functools.partial(project_kernel, n, inner),
        out_shape=(
            jax.ShapeDtypeStruct((length, D), LOW),
            jax.ShapeDtypeStruct((length, q_width), LOW),
            jax.ShapeDtypeStruct((length, k_width), LOW),
            jax.ShapeDtypeStruct((length, k_width), LOW),
            jax.ShapeDtypeStruct((length, q_width + k_width), LOW),
        ),
        grid_spec=pltpu.PrefetchScalarGridSpec(
            num_scalar_prefetch=1,
            grid=(n,),
            in_specs=[resident(p.shape) for p in parts]
            + [resident((block, D))] * n
            + [
                pl.BlockSpec((1, D), whole),
                pl.BlockSpec((1, HEAD_SIZE), whole),
                pl.BlockSpec((1, HEAD_SIZE), whole),
                pl.BlockSpec((block, HEAD_SIZE), natural),
                pl.BlockSpec((block, HEAD_SIZE), natural),
            ],
            out_specs=(
                pl.BlockSpec((block, D), natural),
                pl.BlockSpec((block, q_width), natural),
                pl.BlockSpec((block, k_width), natural),
                pl.BlockSpec((block, k_width), natural),
                pl.BlockSpec((block, q_width + k_width), natural),
            ),
            scratch_shapes=[
                pltpu.VMEM((D, width), LOW),
                pltpu.VMEM((block, D), LOW),
            ],
        ),
        compiler_params=pltpu.CompilerParams(vmem_limit_bytes=40 * MIB),
        cost_estimate=pl.CostEstimate(
            flops=2 * length * D * width, bytes_accessed=16 * MIB, transcendentals=0
        ),
        name="project",
    )(place, *parts, *pieces, gain, gain_q, gain_k, cos, sin)


def attend_kernel(n, inner, first, has_base, place_ref, *refs):
    parts = refs[: 2 * inner]
    q_ref, k_ref, v_ref, seg_col_ref, seg_row_ref = refs[2 * inner : 2 * inner + 5]
    rest = refs[2 * inner + 5 + (2 if has_base else 0) :]
    attended_ref, total_ref, share_ref, weight = rest
    block = q_ref.shape[0]
    heads = k_ref.shape[1] // HEAD_SIZE
    step = pl.program_id(0)

    @pl.when(step == 0)
    def _():
        assemble(parts, weight, chip_rows(place_ref, inner))

    def work(j):
        size = (j + 1) * block
        same = seg_col_ref[...] == seg_row_ref[:, :size]
        own = lax.broadcasted_iota(jnp.int32, (block, size), 0) + j * block
        key = lax.broadcasted_iota(jnp.int32, (block, size), 1)
        allowed = same & (own >= key)
        allowed = jnp.concatenate([allowed] * GROUP, axis=0)
        outs, totals = [], []
        for h in range(heads):
            lanes = slice(h * HEAD_SIZE, (h + 1) * HEAD_SIZE)
            q = jnp.concatenate(
                [
                    q_ref[:, (h * GROUP + g) * HEAD_SIZE : (h * GROUP + g + 1) * HEAD_SIZE]
                    for g in range(GROUP)
                ],
                axis=0,
            )
            scores = jnp.where(allowed, dot_nt(q, k_ref[:size, lanes]), MASKED_SCORE)
            top = jnp.max(scores, axis=-1, keepdims=True)
            weights = jnp.exp2((scores - top) * EXP_SCALE)
            total = jnp.sum(weights, axis=-1, keepdims=True)
            out = dot_nn(weights.astype(LOW), v_ref[:size, lanes]) / total
            log_total = top * EXP_SCALE + jnp.log2(total)
            for g in range(GROUP):
                outs.append(out[g * block : (g + 1) * block].astype(LOW))
                totals.append(log_total[g * block : (g + 1) * block])
        attended = jnp.concatenate(outs, axis=1)
        attended_ref[...] = attended
        share_ref[...] = dot_nn(attended, weight[...]).astype(LOW)
        lane = lax.broadcasted_iota(jnp.int32, (block, HEAD_SIZE), 1)
        packed = jnp.zeros((block, HEAD_SIZE), FULL)
        for i, column in enumerate(totals):
            packed = jnp.where(lane == i, column, packed)
        total_ref[...] = packed

    place = place_ref[0] ^ (first + step)
    for j in range(n):
        pl.when(place == j)(functools.partial(work, j))


def attend(place, parts, q, k, v, seg_col, seg_row, n, chip, base):
    inner = len(parts) // 2
    length, q_width = q.shape
    k_width = k.shape[1]
    block = length // n
    first = 2 * chip
    whole = lambda i, p: (0, 0)
    natural = lambda i, p: (p[0] ^ (first + i), 0)
    slot = lambda i, p: (first + i, 0)
    plain = lambda i, p: (i, 0)
    base = list(base or ())
    before = 1 + len(parts) + 5
    return pl.pallas_call(
        functools.partial(attend_kernel, n, inner, first, bool(base)),
        out_shape=(
            jax.ShapeDtypeStruct((length, q_width), LOW),
            jax.ShapeDtypeStruct((length, HEAD_SIZE), FULL),
            jax.ShapeDtypeStruct((2 * block, D), LOW),
        ),
        grid_spec=pltpu.PrefetchScalarGridSpec(
            num_scalar_prefetch=1,
            grid=(2,),
            in_specs=[resident(p.shape) for p in parts]
            + [
                pl.BlockSpec((block, q_width), natural),
                resident((length, k_width)),
                resident((length, k_width)),
                pl.BlockSpec((block, 1), natural),
                pl.BlockSpec((1, length), whole),
            ]
            + [ANYWHERE] * len(base),
            out_specs=(
                pl.BlockSpec((block, q_width), slot),
                pl.BlockSpec((block, HEAD_SIZE), slot),
                pl.BlockSpec((block, D), plain),
            ),
            scratch_shapes=[pltpu.VMEM((q_width, D), LOW)],
        ),
        input_output_aliases={before: 0, before + 1: 1} if base else {},
        compiler_params=pltpu.CompilerParams(vmem_limit_bytes=48 * MIB),
        cost_estimate=pl.CostEstimate(
            flops=4 * block * q_width * (D + 2 * length), bytes_accessed=8 * MIB, transcendentals=0
        ),
        name="attend",
    )(place, *parts, q, k, v, seg_col, seg_row, *base)


def feed_kernel(chips, place_ref, *refs):
    gates, ups, shrinks = refs[:chips], refs[chips : 2 * chips], refs[2 * chips : 3 * chips]
    own_ref, other_ref, c_ref, c_other_ref = refs[3 * chips : 3 * chips + 4]
    x_out, c_out, active_ref, grad_ref, share_ref, share_other, back_ref, back_other = refs[3 * chips + 4 :]
    mine = pl.program_id(0) == 0
    x = jnp.where(mine, own_ref[...], other_ref[...])
    c_near, c_far = c_ref[0], c_other_ref[0]
    c = jnp.concatenate([jnp.where(mine, c_near, c_far), jnp.where(mine, c_far, c_near)], axis=0)
    x_out[...] = x
    c_out[...] = c
    size = gates[0].shape[1]
    share, back = 0.0, 0.0
    for s in range(chips):
        here = slice(s * size, (s + 1) * size)
        there = slice((chips + s) * size, (chips + s + 1) * size)
        gate = dot_nn(x, gates[s][...])
        up = dot_nn(x, ups[s][...])
        grad_active = dot_nt(c, shrinks[s][...]).astype(LOW).astype(FULL)
        gated = jax.nn.sigmoid(gate)
        silu = gate * gated
        active = (silu * up).astype(LOW)
        grad_gate = (grad_active * up * gated * (1.0 + gate * (1.0 - gated))).astype(LOW)
        grad_up = (grad_active * silu).astype(LOW)
        active_ref[:, here] = active
        grad_ref[:, here] = grad_gate
        grad_ref[:, there] = grad_up
        share = share + dot_nn(active, shrinks[s][...])
        back = back + dot_nt(grad_gate, gates[s][...]) + dot_nt(grad_up, ups[s][...])
    share = share.astype(LOW)
    back = back.astype(LOW)

    @pl.when(mine)
    def _():
        share_ref[...] = share
        back_ref[...] = back

    @pl.when(jnp.logical_not(mine))
    def _():
        share_other[...] = share
        back_other[...] = back


def feed(place, n, expand, shrink, own, other, c, c_other):
    chips = n // 2
    rows = own.shape[0]
    size = FF // n
    whole = lambda i, p: (0, 0)
    flat = lambda i, p: (i, 0)
    core = lambda i, p: ((p[0] & 1) ^ i, 0, 0)
    once = pl.Buffered(1)
    gates = [
        pl.BlockSpec((D, size), lambda i, p, s=s: (0, 2 * s + (p[0] & 1)), pipeline_mode=once)
        for s in range(chips)
    ]
    ups = [
        pl.BlockSpec((D, size), lambda i, p, s=s: (0, n + 2 * s + (p[0] & 1)), pipeline_mode=once)
        for s in range(chips)
    ]
    shrinks = [
        pl.BlockSpec((size, D), lambda i, p, s=s: (2 * s + (p[0] & 1), 0), pipeline_mode=once)
        for s in range(chips)
    ]
    wide = lambda w: jax.ShapeDtypeStruct((2 * rows, w), LOW)
    part = jax.ShapeDtypeStruct((rows, D), LOW)
    return pl.pallas_call(
        functools.partial(feed_kernel, chips),
        out_shape=(wide(D), wide(D), wide(FF // 2), wide(FF), part, part, part, part),
        grid_spec=pltpu.PrefetchScalarGridSpec(
            num_scalar_prefetch=1,
            grid=(2,),
            in_specs=gates
            + ups
            + shrinks
            + [
                resident((rows, D)),
                resident((rows, D)),
                pl.BlockSpec((1, rows // 2, D), core),
                pl.BlockSpec((1, rows // 2, D), core),
            ],
            out_specs=(
                pl.BlockSpec((rows, D), flat),
                pl.BlockSpec((rows, D), flat),
                pl.BlockSpec((rows, FF // 2), flat),
                pl.BlockSpec((rows, FF), flat),
                pl.BlockSpec((rows, D), whole),
                pl.BlockSpec((rows, D), whole),
                pl.BlockSpec((rows, D), whole),
                pl.BlockSpec((rows, D), whole),
            ),
        ),
        compiler_params=pltpu.CompilerParams(vmem_limit_bytes=56 * MIB),
        cost_estimate=pl.CostEstimate(
            flops=12 * rows * D * FF, bytes_accessed=30 * MIB, transcendentals=0
        ),
        name="feed",
    )(place, *[expand] * (2 * chips), *[shrink] * chips, own, other, c, c_other)


def back_kernel(n, inner, half, place_ref, *refs):
    qkv_parts = refs[: n * inner]
    out_parts = refs[n * inner : (n + 2) * inner]
    refs = refs[(n + 2) * inner :]
    (
        h_ref,
        attended_ref,
        total_ref,
        q_ref,
        k_ref,
        v_ref,
        raw_ref,
        cos_ref,
        sin_ref,
        seg_col_ref,
        seg_row_ref,
        gain_q_ref,
        gain_k_ref,
    ) = refs[:13]
    refs = refs[13:]
    if half:
        base_ref, refs = refs[0], refs[1:]
    grad_ref, share_ref, gains_ref, qkv, out, key_sum, value_sum = refs
    block = q_ref.shape[0]
    heads = k_ref.shape[1] // HEAD_SIZE
    step = pl.program_id(0)

    @pl.when(step == 0)
    def _():
        assemble(qkv_parts, qkv, all_rows(place_ref, n, inner))
        rows = out_parts[0].shape[0]
        size = out.shape[0] // rows
        for part, spot in zip(out_parts, chip_rows(place_ref, inner)):

            @pl.when(spot // size == half)
            def _():
                out[pl.ds(pl.multiple_of((spot % size) * rows, rows), rows), :] = part[...]

        key_sum[...] = jnp.zeros_like(key_sum)
        value_sum[...] = jnp.zeros_like(value_sum)
        gains_ref[...] = jnp.zeros_like(gains_ref)

    def work(j):
        size = (j + 1) * block
        grad_attended = dot_nt(h_ref[...], out[...]).astype(LOW)
        attended = attended_ref[...]
        totals = total_ref[...].T
        same = seg_col_ref[:size, :] == seg_row_ref[:, j * block : size]
        key = lax.broadcasted_iota(jnp.int32, (size, block), 0)
        own = lax.broadcasted_iota(jnp.int32, (size, block), 1) + j * block
        allowed = same & (own >= key)
        allowed = jnp.concatenate([allowed] * GROUP, axis=1)
        cos, sin = cos_ref[...], sin_ref[...]
        gains = gains_ref[...]
        kind = lax.broadcasted_iota(jnp.int32, gains.shape, 0)

        def head_back(grad, values, gain):
            grad = grad * cos + pltpu.roll(grad * sin, HEAD_SIZE // 2, 1)
            grad, gain_part = norm_back(values.astype(FULL), gain, grad)
            return grad.astype(LOW), jnp.sum(gain_part, axis=0, keepdims=True)

        query_grads, key_grads, value_grads = [], [], []
        for h in range(heads):
            lanes = slice(h * HEAD_SIZE, (h + 1) * HEAD_SIZE)
            k, v = k_ref[:size, lanes], v_ref[:size, lanes]
            head_lanes = [
                slice((h * GROUP + g) * HEAD_SIZE, (h * GROUP + g + 1) * HEAD_SIZE)
                for g in range(GROUP)
            ]
            q = jnp.concatenate([q_ref[:, s] for s in head_lanes], axis=0)
            up = jnp.concatenate([grad_attended[:, s] for s in head_lanes], axis=0)
            seen = jnp.concatenate([attended[:, s] for s in head_lanes], axis=0)
            log_total = jnp.concatenate(
                [totals[(half * heads + h) * GROUP + g : (half * heads + h) * GROUP + g + 1, :] for g in range(GROUP)], axis=1
            )
            row = jnp.sum(up.astype(FULL) * seen.astype(FULL), axis=1, keepdims=True)
            row = jnp.broadcast_to(row, (GROUP * block, HEAD_SIZE)).T[:1, :]
            probs = jnp.where(allowed, jnp.exp2(dot_nt(k, q) * EXP_SCALE - log_total), 0.0)
            grad_probs = dot_nt(v, up)
            grad_scores = (probs * (grad_probs - row)).astype(LOW)
            value_sum[:size, lanes] += dot_nn(probs.astype(LOW), up)
            key_sum[:size, lanes] += dot_nn(grad_scores, q)
            query_grad = dot_tn(grad_scores, k) * SCALE
            for g in range(GROUP):
                grad, gain_part = head_back(
                    query_grad[g * block : (g + 1) * block], raw_ref[:, head_lanes[g]], gain_q_ref[...]
                )
                query_grads.append(grad)
                gains = jnp.where(kind == 0, gains + gain_part, gains)
        own_rows = slice(j * block, size)
        for h in range(heads):
            lanes = slice(h * HEAD_SIZE, (h + 1) * HEAD_SIZE)
            first = (heads * GROUP + h) * HEAD_SIZE
            grad, gain_part = head_back(
                key_sum[own_rows, lanes] * SCALE, raw_ref[:, first : first + HEAD_SIZE], gain_k_ref[...]
            )
            key_grads.append(grad)
            gains = jnp.where(kind == 1, gains + gain_part, gains)
            value_grads.append(value_sum[own_rows, lanes].astype(LOW))
        gains_ref[...] = gains
        grad = jnp.concatenate(query_grads + key_grads + value_grads, axis=1)
        grad_ref[...] = grad
        share = dot_nt(grad, qkv[...])
        if half:
            share = share + base_ref[...].astype(FULL)
        share_ref[...] = share.astype(LOW)

    for j in range(n):
        pl.when(step == n - 1 - j)(functools.partial(work, j))


def back(
    place, qkv_parts, out_parts, hidden_grad, attended, totals, q, k, v, raw, cos, sin, seg_col,
    seg_row, gain_q, gain_k, half, base,
):
    inner = len(out_parts) // 2
    n = len(qkv_parts) // inner
    length = q.shape[0]
    q_width, k_width = q.shape[1] // HALVES, k.shape[1] // HALVES
    block = length // n
    width = q_width + 2 * k_width
    whole = lambda i, p: (0, 0)
    natural = lambda i, p: (n - 1 - i, 0)
    slot = lambda i, p: (p[0] ^ (n - 1 - i), 0)
    natural_half = lambda i, p: (n - 1 - i, half)
    slot_half = lambda i, p: (p[0] ^ (n - 1 - i), half)
    base = [] if base is None else [base]
    return pl.pallas_call(
        functools.partial(back_kernel, n, inner, half),
        out_shape=(
            jax.ShapeDtypeStruct((length, width), LOW),
            jax.ShapeDtypeStruct((length, D), LOW),
            jax.ShapeDtypeStruct((8, HEAD_SIZE), FULL),
        ),
        grid_spec=pltpu.PrefetchScalarGridSpec(
            num_scalar_prefetch=1,
            grid=(n,),
            in_specs=[resident((p.shape[0], width), half) for p in qkv_parts]
            + [resident(p.shape) for p in out_parts]
            + [
                pl.BlockSpec((block, D), slot),
                pl.BlockSpec((block, q_width), slot_half),
                pl.BlockSpec((block, HEAD_SIZE), slot),
                pl.BlockSpec((block, q_width), natural_half),
                resident((length, k_width), half),
                resident((length, k_width), half),
                pl.BlockSpec((block, q_width + k_width), natural_half),
                pl.BlockSpec((block, HEAD_SIZE), natural),
                pl.BlockSpec((block, HEAD_SIZE), natural),
                pl.BlockSpec((length, 1), whole),
                pl.BlockSpec((1, length), whole),
                pl.BlockSpec((1, HEAD_SIZE), whole),
                pl.BlockSpec((1, HEAD_SIZE), whole),
            ]
            + [pl.BlockSpec((block, D), slot)] * len(base),
            out_specs=(
                pl.BlockSpec((block, width), natural),
                pl.BlockSpec((block, D), slot),
                pl.BlockSpec((8, HEAD_SIZE), whole),
            ),
            scratch_shapes=[
                pltpu.VMEM((D, width), LOW),
                pltpu.VMEM((q_width, D), LOW),
                pltpu.VMEM((length, k_width), FULL),
                pltpu.VMEM((length, k_width), FULL),
            ],
        ),
        compiler_params=pltpu.CompilerParams(vmem_limit_bytes=56 * MIB),
        cost_estimate=pl.CostEstimate(
            flops=2 * length * D * (q_width + width) + 5 * length * length * q_width,
            bytes_accessed=30 * MIB,
            transcendentals=0,
        ),
        name="back",
    )(
        place, *qkv_parts, *out_parts, hidden_grad, attended, totals, q, k, v, raw, cos, sin,
        seg_col, seg_row, gain_q, gain_k, *base,
    )


def adam_kernel(rate, blocks, key_ref, *refs):
    cuts = refs[:HALVES]
    weight_ref, first_ref, second_ref, new_first, new_second, new_weight, grad = refs[HALVES:]
    for i in range(HALVES):

        @pl.when(pl.program_id(0) // blocks == i)
        def _():
            grad[...] = cuts[i][0].astype(FULL)

    results = adam_step(weight_ref[...], first_ref[...], second_ref[...], grad[...], rate)
    new_first[...], new_second[...], new_weight[...] = results


def adam_cuts(key, cuts, weight, first, second, rate, size, column):
    chips, rows, columns = cuts[0].shape
    blocks = columns // size
    place = lambda i, s, p: (0, column(i, s))
    slot = lambda i, s, p: (p[0] ^ s, 0, i % blocks)
    spec = pl.BlockSpec((rows, size), place)
    shape = jax.ShapeDtypeStruct(weight.shape, FULL)
    return pl.pallas_call(
        functools.partial(adam_kernel, rate, blocks),
        out_shape=(shape, shape, shape),
        grid_spec=pltpu.PrefetchScalarGridSpec(
            num_scalar_prefetch=1,
            grid=(HALVES * blocks, chips),
            in_specs=[pl.BlockSpec((1, rows, size), slot)] * HALVES + [spec] * 3,
            out_specs=(spec,) * 3,
            scratch_shapes=[pltpu.VMEM((rows, size), FULL)],
        ),
        cost_estimate=pl.CostEstimate(
            flops=20 * weight.size, bytes_accessed=26 * weight.size, transcendentals=weight.size
        ),
        compiler_params=pltpu.CompilerParams(vmem_limit_bytes=24 * MIB),
        name="adam_cuts",
    )(key, *cuts, weight, first, second)


def adam_pair_kernel(rate, place_ref, own_ref, other_ref, weight_ref, first_ref, second_ref, *outs):
    mine = pl.program_id(1) == (place_ref[0] & 1)
    grad = jnp.where(mine, own_ref[...].astype(FULL), other_ref[...].astype(FULL))
    results = adam_step(weight_ref[...], first_ref[...], second_ref[...], grad, rate)
    outs[0][...], outs[1][...], outs[2][...] = results


def adam_pair(place, own, other, weight, first, second, rate, size):
    rows, width = own.shape
    cut = pl.BlockSpec((rows, size), lambda i, c, p: (0, i))
    spec = pl.BlockSpec((rows, size), lambda i, c, p: (0, 2 * i + c))
    shape = jax.ShapeDtypeStruct(weight.shape, FULL)
    return pl.pallas_call(
        functools.partial(adam_pair_kernel, rate),
        out_shape=(shape, shape, shape),
        grid_spec=pltpu.PrefetchScalarGridSpec(
            num_scalar_prefetch=1,
            grid=(width // size, 2),
            in_specs=[cut, cut] + [spec] * 3,
            out_specs=(spec,) * 3,
        ),
        cost_estimate=pl.CostEstimate(
            flops=20 * weight.size, bytes_accessed=26 * weight.size, transcendentals=weight.size
        ),
        compiler_params=pltpu.CompilerParams(vmem_limit_bytes=24 * MIB),
        name="adam_pair",
    )(place, own, other, weight, first, second)


def after(value, *others):
    return lax.optimization_barrier((value, *others))[0]


def make(n, inner, reps):
    chips = n // 2

    def swap_ctx(value, s):
        return lax.ppermute(value, "ctx", [(i, i ^ s) for i in range(n)])

    def swap_core(value):
        return swap_ctx(value, 1)

    def swap_chip(value, s):
        return swap_ctx(value, 2 * s)

    def swap_grp(value, t):
        return lax.ppermute(value, "grp", [(i, i ^ t) for i in range(inner)])

    def swap_rep(value, r):
        return lax.ppermute(value, "rep", [(i, i ^ r) for i in range(reps)])

    def over_chips(value):
        return [value] + [swap_chip(value, s) for s in range(1, chips)]

    def over_grp(value):
        return [value] + [swap_grp(value, t) for t in range(1, inner)]

    def sum_of(parts):
        total = parts[0].astype(FULL)
        for part in parts[1:]:
            total = total + part.astype(FULL)
        return total

    def swap_plane(value, s, t):
        pairs = [(c * inner + g, (c ^ s) * inner + (g ^ t)) for c in range(n) for g in range(inner)]
        return lax.ppermute(value, ("ctx", "grp"), pairs)

    def pick(value, axis, index):
        return lax.dynamic_index_in_dim(value, index, axis, False)

    middle = reps // 2
    hops = [([(k, k + 1), (reps - 1 - k, reps - 2 - k)], None) for k in range(middle - 1)]
    hops.append(([(middle - 1, middle), (middle, middle - 1)], None))
    hops += [
        ([(k, k - 1), (reps - 1 - k, reps - k)], (k - 1, reps - k)) for k in range(middle - 1, 0, -1)
    ]

    def gather_reps(value):
        return [value] + [swap_rep(value, r) for r in range(1, reps)]

    def on_device(
        tokens,
        segment_ids,
        positions,
        cotangent,
        qkv_weight,
        qkv_first,
        qkv_second,
        out_weight,
        out_first,
        out_second,
        expand_weight,
        expand_first,
        expand_second,
        shrink_weight,
        shrink_first,
        shrink_second,
        norm_gains,
        gains_first,
        gains_second,
    ):
        seqs, block, _ = tokens.shape
        length = n * block
        me = lax.axis_index("ctx")
        core = me & 1
        chip = me >> 1
        mine = lax.axis_index("grp")
        place = jnp.stack([me, mine]).astype(jnp.int32)
        order = me ^ jnp.arange(n)
        q_width = QUERY_FEATURES // chips
        k_width = KEY_FEATURES // chips
        width = q_width + 2 * k_width
        rows = qkv_weight.shape[0]

        rep = lax.axis_index("rep")

        def qkv_piece(s):
            to = chip ^ s
            parts = []
            for i in range(HALVES):
                for first, size in ((0, q_width), (QUERY_FEATURES, k_width), (QUERY_FEATURES + KEY_FEATURES, k_width)):
                    start = first + to * size + i * (size // HALVES)
                    parts.append(lax.dynamic_slice_in_dim(qkv_weight, start, size // HALVES, 1))
            return jnp.concatenate(parts, axis=1).astype(LOW)

        small = jnp.concatenate(
            [
                segment_ids.reshape(-1).astype(FULL),
                positions.reshape(-1).astype(FULL),
                norm_gains.astype(LOW).astype(FULL),
            ]
        ).reshape(1, -1)
        small = [
            swap_plane(small, s, t) if s or t else small for s in range(n) for t in range(inner)
        ]
        tokens, qkv_low, other_tokens, *small = lax.optimization_barrier(
            (tokens, [qkv_piece(s) for s in range(chips)], pick(tokens, 0, core ^ 1), *small)
        )
        small = jnp.stack(small)
        small = small.reshape(n, inner, -1)[order]
        notes = small[:, 0, : 2 * seqs * block].reshape(n, 2, seqs, block)
        notes = pick(notes, 2, core)
        notes = jnp.moveaxis(notes, 0, 1).reshape(2, length)
        gains = small[:, mine ^ jnp.arange(inner), 2 * seqs * block :].reshape(1, -1)
        gain_one, gain_two = gains[:, :D], gains[:, D : 2 * D]
        gain_query = gains[:, 2 * D : 2 * D + HEAD_SIZE]
        gain_key = gains[:, 2 * D + HEAD_SIZE :]

        token_slots = [pick(tokens, 0, core), swap_core(other_tokens)]
        for s in range(1, chips):
            token_slots += [swap_chip(part, s) for part in token_slots[:2]]

        landed = [qkv_low[0]] + [swap_chip(qkv_low[s], s) for s in range(1, chips)]
        qkv_parts = []
        for part in landed:
            near = over_grp(part)
            qkv_parts += near + [swap_core(p) for p in near]

        near = over_grp(out_weight.astype(LOW))
        out_parts = near + [swap_core(p) for p in near]
        def gather_all(weight):
            share = weight.shape[0] // reps
            low = lax.dynamic_slice_in_dim(weight, rep * share, share, 0).astype(LOW)
            return lax.all_gather(low, ("ctx", "grp", "rep"), axis=0, tiled=True)

        expand_full = gather_all(expand_weight)
        shrink_full = gather_all(shrink_weight)
        other_cotangent = swap_core(cotangent)

        ladder = jnp.arange(HEAD_SIZE) % (HEAD_SIZE // 2)
        frequency = jnp.exp(ladder.astype(FULL) * (-2.0 * math.log(ROPE_BASE) / HEAD_SIZE))
        angles = notes[1][:, None] * frequency[None, :]
        sign = jnp.where(jnp.arange(HEAD_SIZE) < HEAD_SIZE // 2, -1.0, 1.0)
        cos, sin = jnp.cos(angles), jnp.sin(angles) * sign
        seg_col, seg_row = notes[0][:, None], notes[0][None, :]

        normed, q, k, v, raw = project(
            place, qkv_parts, token_slots, gain_one, gain_query, gain_key, cos, sin
        )
        base, shares = None, []
        for s in range(chips - 1, -1, -1):
            *base, share = attend(place, out_parts, q, k, v, seg_col, seg_row, n, s, base)
            shares.append(swap_chip(share, s) if s else share)
        attended, totals = base
        inputs = jnp.concatenate(token_slots[:2]).astype(FULL)
        hidden = inputs + sum_of(shares)
        normed_two = (hidden * inverse_rms(hidden) * gain_two).astype(LOW)

        x_all, c_all, active, grad_gate_up, share, share_other, back_share, back_other = feed(
            place, n, expand_full, shrink_full, normed_two, swap_core(normed_two), cotangent,
            other_cotangent,
        )
        normed_grad = sum_of([back_share, swap_core(back_other)])
        hidden_grad, gain_part = norm_back(hidden, gain_two, normed_grad)
        gain_two_grad = jnp.sum(gain_part, axis=0)
        hidden_grad = hidden_grad + c_all[: 2 * block].astype(FULL)
        hidden_low = hidden_grad.astype(LOW)
        grad_slots = over_chips(hidden_low)
        grad_all = jnp.concatenate(grad_slots)

        def by_sequence(kept, landed):
            return jnp.where(core == 0, jnp.stack([kept, landed]), jnp.stack([landed, kept]))

        output = (hidden + sum_of([share, swap_core(share_other)])).astype(LOW)
        output = by_sequence(output[:block], swap_core(output[block:]))

        line = []

        def next_sum(kept, sent):
            if line:
                sent = lax.optimization_barrier((*sent, *line))[: len(sent)]
            total = sum_of([kept, *sent]).astype(LOW)
            line[:] = [total]
            return total

        def next_cut(kept, sent, axis, place, count):
            sent = lax.optimization_barrier((*sent, *line))[: len(sent)]
            pieces = [
                sum_of([pick(value, axis, place ^ s) for value in (kept, *sent)]).astype(LOW)
                for s in range(count)
            ]
            line[:] = pieces
            return pieces

        def go(value, step=0):
            return [value, lax.ppermute(value, "rep", hops[step][0]), step]

        def step_on(trip):
            value, landed, step = trip
            if step == len(hops):
                return
            takes = hops[step][1]
            if takes is None:
                value = next_sum(value, [landed])
            else:
                landed = after(landed, *line)
                value = jnp.where((rep == takes[0]) | (rep == takes[1]), landed, value)
                line[:] = [value]
            step += 1
            trip[:] = go(value, step) if step < len(hops) else [value, None, step]

        def send_x(parts):
            return parts[0], [swap_chip(parts[s], s) for s in range(1, chips)]

        def send_y(parts):
            return parts[0], [swap_grp(parts[t], t) for t in range(1, inner)]

        def back_part(half, attended, back_all):
            return back(
                place, qkv_parts, out_parts, grad_all, attended, totals, q, k, v, raw, cos, sin,
                seg_col, seg_row, gain_query, gain_key, half, back_all,
            )

        def cut_qkv(grad):
            grad_qkv = dot_tn(normed, grad).astype(LOW)
            cuts = grad_qkv.reshape(chips, 2, inner, rows, width // HALVES)
            return pick(cuts, 1, core), [swap_core(pick(cuts, 1, core ^ 1))]

        x_late, active_late = lax.optimization_barrier((x_all, active, hidden_low))[:2]
        grad_expand = dot_tn(x_late, grad_gate_up).astype(LOW)
        expand_cuts = grad_expand.reshape(chips, 2, inner, rows, FF)
        other_rows = pick(expand_cuts, 1, core ^ 1)
        other_sent = [swap_grp(pick(other_rows, 1, mine ^ t), t) for t in range(1, inner)]
        grad_shrink = dot_tn(active_late, c_all).astype(LOW)
        shrink_cuts = grad_shrink.reshape(chips, inner, FF // (n * inner), D)
        own_cuts = pick(expand_cuts, 1, core)

        def first_over_x(cuts, t, *gates):
            cut = after(cuts, *gates)
            sent = [swap_chip(pick(pick(cut, 0, chip ^ s), 0, mine ^ t), s) for s in range(1, chips)]
            return pick(pick(cuts, 0, chip), 0, mine ^ t), sent

        own_far = [first_over_x(own_cuts, t, grad_slots[-1]) for t in range(1, inner)]
        own_near = first_over_x(own_cuts, 0, grad_slots[-1])

        grad_out = dot_tn(attended, grad_all).astype(LOW)
        out_cuts = grad_out.reshape(2, inner, out_weight.shape[0], D)
        out_sent = swap_core(pick(out_cuts, 0, core ^ 1))
        attended = after(attended, out_cuts)
        grad_one, back_all, gains_one = back_part(0, attended, None)

        line[:] = [gains_one]
        own_sent = [swap_grp(next_sum(*own_far[t - 1]), t) for t in range(1, inner)]
        other_cut = send_x(next_cut(pick(other_rows, 1, mine), other_sent, 0, chip, chips))
        own_cut = next_sum(*own_near)
        first_cuts, first_sent = cut_qkv(grad_one)
        shrink_far = [first_over_x(shrink_cuts, t, *line) for t in range(1, inner)]
        shrink_near = first_over_x(shrink_cuts, 0, *line)
        out_cut = send_y(next_cut(pick(out_cuts, 0, core), [out_sent], 0, mine, inner))
        attended, back_all = lax.optimization_barrier((attended, back_all, first_cuts, *line))[:2]
        grad_two, back_all, gains_two = back_part(1, attended, back_all)

        line[:] = [gains_two]
        shrink_sent = [swap_grp(next_sum(*shrink_far[t - 1]), t) for t in range(1, inner)]
        shrink_cut = next_sum(*shrink_near)
        own_cut = next_sum(own_cut, own_sent)
        first_cut = send_y(next_cut(first_cuts, first_sent, 1, mine, inner))
        second_cuts, second_sent = cut_qkv(after(grad_two, *line))
        other_cut = swap_core(next_sum(*other_cut))
        second_cut = send_y(next_cut(second_cuts, second_sent, 1, mine, inner))
        shares = []
        for s in range(1, chips):
            share = after(back_all[2 * s * block : 2 * (s + 1) * block], *line)
            shares.append(swap_chip(share, s))
        out = go(next_sum(*out_cut))
        shrink_cut = next_sum(shrink_cut, shrink_sent)
        own_cut, other_cut, shrink_cut = lax.optimization_barrier((own_cut, other_cut, shrink_cut, *line))[:3]
        line[:] = [own_cut]
        own_cut, other_cut, total_shrink = lax.psum((own_cut, other_cut, shrink_cut), "rep")
        first_cut = send_x(next_cut(*first_cut, 0, chip, chips))
        second_cut = send_x(next_cut(*second_cut, 0, chip, chips))

        def stacked(on_the_way):
            kept, sent = on_the_way
            total = jnp.stack([kept, *lax.optimization_barrier((*sent, *line))[: len(sent)]])
            line[:] = [total]
            return total

        step_on(out)
        first = go(stacked(first_cut))
        second = go(stacked(second_cut))
        shares = [back_all[: 2 * block]] + [after(value, *line) for value in shares]
        input_part, gain_part = norm_back(inputs, gain_one, sum_of(shares))
        gain_one_grad = jnp.sum(gain_part, axis=0)
        input_grad = (input_part + hidden_grad).astype(LOW)
        input_landed = swap_core(input_grad[block:])
        head_gains = gains_one + gains_two
        grad_gains = jnp.concatenate([gain_one_grad, gain_two_grad, head_gains[0], head_gains[1]])
        grad_gains = grad_gains.reshape(n, inner, 1, -1)
        gains_sent = [
            swap_plane(pick(pick(grad_gains, 0, me ^ s), 0, mine ^ t), s, t)
            for s in range(n)
            for t in range(inner)
            if s or t
        ]
        line[:] = [gain_one_grad]

        step_on(out)
        step_on(first)
        step_on(second)
        gains_sent = lax.optimization_barrier((*gains_sent, *line))[:-1]
        total_gains = sum_of([pick(pick(grad_gains, 0, me), 0, mine), *gains_sent])
        gains_sent = gather_reps(total_gains)
        step_on(first)
        step_on(out)
        step_on(second)
        trips = (out, first, second)
        for _ in hops:
            for trip in trips:
                step_on(trip)
        total_out, *qkv_cuts = [trip[0] for trip in trips]
        total_gains = sum_of(lax.optimization_barrier((*gains_sent, *line))[:-1])[0]
        input_grad = by_sequence(input_grad[:block], input_landed)

        size = k_width // HALVES

        def qkv_column(i, s):
            per_half = width // HALVES // size
            half, i = i // per_half, i % per_half
            q_blocks = q_width // HALVES // size
            q_place = (s * HALVES + half) * q_blocks + i
            k_place = QUERY_FEATURES // size + s * HALVES + half
            v_place = k_place + KEY_FEATURES // size
            return jnp.where(i < q_blocks, q_place, jnp.where(i == q_blocks, k_place, v_place))

        key = chip.reshape(1).astype(jnp.int32)
        return (
            output,
            input_grad,
            *adam_cuts(key, qkv_cuts, qkv_weight, qkv_first, qkv_second, RATE_QKV, size, qkv_column),
            *adam_step(out_weight, out_first, out_second, total_out.astype(FULL), RATE_OUT),
            *adam_pair(
                place, own_cut, other_cut, expand_weight, expand_first, expand_second, RATE_EXPAND,
                FF // n,
            ),
            *adam_step(
                shrink_weight, shrink_first, shrink_second, total_shrink.astype(FULL), RATE_SHRINK
            ),
            *adam_step(norm_gains, gains_first, gains_second, total_gains, RATE_GAINS),
        )

    return on_device


def solution(mesh):
    token_rows = P(("grp", "rep"), "ctx", None)
    token_notes = P(("grp", "rep"), "ctx")
    weight_rows = P(("ctx", "grp"), None)
    gain_rows = P(("ctx", "grp"))
    states = (weight_rows,) * 12 + (gain_rows,) * 3
    return jax.shard_map(
        make(mesh.shape["ctx"], mesh.shape["grp"], mesh.shape["rep"]),
        mesh=mesh,
        in_specs=(token_rows, token_notes, token_notes, token_rows) + states,
        out_specs=(token_rows, token_rows) + states,
        check_vma=False,
    )
```

```python
import functools
import math

import jax
import jax.numpy as jnp
from jax import lax
from jax.experimental import pallas as pl
from jax.experimental.pallas import tpu as pltpu
from jax.sharding import PartitionSpec as P

D = 1024
QUERY_HEADS = 16
KEY_VALUE_HEADS = 8
HEAD_SIZE = 128
FF = 3072
STEP = 10
QUERY_FEATURES = 2048
KEY_FEATURES = 1024
GROUP = QUERY_HEADS // KEY_VALUE_HEADS

EPS_NORM = 1e-06
ROPE_BASE = 1000000.0
MASKED_SCORE = -1e30
BETA_ONE = 0.9
BETA_TWO = 0.95
ADAM_EPS = 1e-08
WEIGHT_DECAY = 0.1
RATE_QKV = 0.1
RATE_OUT = 0.5
RATE_EXPAND = 0.1
RATE_SHRINK = 0.06
RATE_GAINS = 0.6

SCALE = HEAD_SIZE**-0.5
EXP_SCALE = SCALE * math.log2(math.e)
LOW = jnp.bfloat16
FULL = jnp.float32
MIB = 1 << 20
HALVES = 1


def dot_nn(a, b):
    return jnp.dot(a, b, preferred_element_type=FULL)


def dot_nt(a, b):
    return lax.dot_general(a, b, (((1,), (1,)), ((), ())), preferred_element_type=FULL)


def dot_tn(a, b):
    return lax.dot_general(a, b, (((0,), (0,)), ((), ())), preferred_element_type=FULL)


def inverse_rms(values):
    return lax.rsqrt(jnp.mean(values * values, axis=-1, keepdims=True) + EPS_NORM)


def norm_back(values, gain, incoming):
    scale = inverse_rms(values)
    normed = values * scale
    scaled = incoming * gain
    grad = scale * (scaled - normed * jnp.mean(scaled * normed, axis=-1, keepdims=True))
    return grad, incoming * normed


def adam_step(weight, first_moment, second_moment, gradient, step_rate):
    first_moment = BETA_ONE * first_moment + (1.0 - BETA_ONE) * gradient
    second_moment = BETA_TWO * second_moment + (1.0 - BETA_TWO) * gradient * gradient
    fix_one = 1.0 - BETA_ONE**STEP
    fix_two = 1.0 - BETA_TWO**STEP
    step_dir = first_moment / fix_one / (jnp.sqrt(second_moment / fix_two) + ADAM_EPS)
    return (first_moment, second_moment, weight - step_rate * (step_dir + WEIGHT_DECAY * weight))


def assemble(parts, whole, blocks):
    rows = whole.shape[0] // len(parts)
    for part, block in zip(parts, blocks):
        whole[pl.ds(pl.multiple_of(block * rows, rows), rows), :] = part[...]


def all_rows(place_ref, n, inner):
    return [(place_ref[0] ^ s) * inner + (place_ref[1] ^ t) for s in range(n) for t in range(inner)]


def chip_rows(place_ref, inner):
    return [
        ((place_ref[0] & 1) ^ k) * inner + (place_ref[1] ^ t) for k in range(2) for t in range(inner)
    ]


ANYWHERE = pl.BlockSpec(memory_space=pl.ANY)


def resident(shape, column=0):
    return pl.BlockSpec(shape, lambda *_: (0, column), pipeline_mode=pl.Buffered(1))


def project_kernel(n, inner, place_ref, *refs):
    parts = refs[: n * inner]
    pieces = refs[n * inner : n * inner + n]
    gain_ref, gain_q_ref, gain_k_ref, cos_ref, sin_ref = refs[n * inner + n : n * inner + n + 5]
    normed_ref, q_ref, k_ref, v_ref, raw_ref = refs[n * inner + n + 5 : n * inner + n + 10]
    weight, token = refs[n * inner + n + 10 :]
    step = pl.program_id(0)

    @pl.when(step == 0)
    def _():
        assemble(parts, weight, all_rows(place_ref, n, inner))

    for s in range(n):

        @pl.when((place_ref[0] ^ step) == s)
        def _():
            token[...] = pieces[s][...]

    x = token[...].astype(FULL)
    normed = (x * inverse_rms(x) * gain_ref[...]).astype(LOW)
    normed_ref[...] = normed
    projected = dot_nn(normed, weight[...])
    q_half, k_half = q_ref.shape[1] // HALVES, k_ref.shape[1] // HALVES
    raw_half = q_half + k_half
    half = raw_half + k_half
    cos, sin = cos_ref[...], sin_ref[...]

    def turn(values, gain):
        values = values * inverse_rms(values) * gain
        return (values * cos + pltpu.roll(values, HEAD_SIZE // 2, 1) * sin).astype(LOW)

    for i in range(HALVES):
        first = i * half
        raw_ref[:, i * raw_half : (i + 1) * raw_half] = projected[:, first : first + raw_half].astype(LOW)
        v_ref[:, i * k_half : (i + 1) * k_half] = projected[:, first + raw_half : first + half].astype(LOW)
        for h in range(0, q_half, HEAD_SIZE):
            values = projected[:, first + h : first + h + HEAD_SIZE]
            q_ref[:, i * q_half + h : i * q_half + h + HEAD_SIZE] = turn(values, gain_q_ref[...])
        for h in range(0, k_half, HEAD_SIZE):
            values = projected[:, first + q_half + h : first + q_half + h + HEAD_SIZE]
            k_ref[:, i * k_half + h : i * k_half + h + HEAD_SIZE] = turn(values, gain_k_ref[...])


def project(place, parts, pieces, gain, gain_q, gain_k, cos, sin):
    n = len(pieces)
    inner = len(parts) // n
    block = pieces[0].shape[0]
    length = n * block
    width = parts[0].shape[1]
    q_width, k_width = width // 2, width // 4
    whole = lambda j, p: (0, 0)
    natural = lambda j, p: (j, 0)
    return pl.pallas_call(
        functools.partial(project_kernel, n, inner),
        out_shape=(
            jax.ShapeDtypeStruct((length, D), LOW),
            jax.ShapeDtypeStruct((length, q_width), LOW),
            jax.ShapeDtypeStruct((length, k_width), LOW),
            jax.ShapeDtypeStruct((length, k_width), LOW),
            jax.ShapeDtypeStruct((length, q_width + k_width), LOW),
        ),
        grid_spec=pltpu.PrefetchScalarGridSpec(
            num_scalar_prefetch=1,
            grid=(n,),
            in_specs=[resident(p.shape) for p in parts]
            + [resident((block, D))] * n
            + [
                pl.BlockSpec((1, D), whole),
                pl.BlockSpec((1, HEAD_SIZE), whole),
                pl.BlockSpec((1, HEAD_SIZE), whole),
                pl.BlockSpec((block, HEAD_SIZE), natural),
                pl.BlockSpec((block, HEAD_SIZE), natural),
            ],
            out_specs=(
                pl.BlockSpec((block, D), natural),
                pl.BlockSpec((block, q_width), natural),
                pl.BlockSpec((block, k_width), natural),
                pl.BlockSpec((block, k_width), natural),
                pl.BlockSpec((block, q_width + k_width), natural),
            ),
            scratch_shapes=[
                pltpu.VMEM((D, width), LOW),
                pltpu.VMEM((block, D), LOW),
            ],
        ),
        compiler_params=pltpu.CompilerParams(vmem_limit_bytes=40 * MIB),
        cost_estimate=pl.CostEstimate(
            flops=2 * length * D * width, bytes_accessed=16 * MIB, transcendentals=0
        ),
        name="project",
    )(place, *parts, *pieces, gain, gain_q, gain_k, cos, sin)


def attend_kernel(n, inner, first, has_base, place_ref, *refs):
    parts = refs[: 2 * inner]
    q_ref, k_ref, v_ref, seg_col_ref, seg_row_ref = refs[2 * inner : 2 * inner + 5]
    rest = refs[2 * inner + 5 + (2 if has_base else 0) :]
    attended_ref, total_ref, share_ref, weight = rest
    block = q_ref.shape[0]
    heads = k_ref.shape[1] // HEAD_SIZE
    step = pl.program_id(0)

    @pl.when(step == 0)
    def _():
        assemble(parts, weight, chip_rows(place_ref, inner))

    def work(j):
        size = (j + 1) * block
        same = seg_col_ref[...] == seg_row_ref[:, :size]
        own = lax.broadcasted_iota(jnp.int32, (block, size), 0) + j * block
        key = lax.broadcasted_iota(jnp.int32, (block, size), 1)
        allowed = same & (own >= key)
        allowed = jnp.concatenate([allowed] * GROUP, axis=0)
        outs, totals = [], []
        for h in range(heads):
            lanes = slice(h * HEAD_SIZE, (h + 1) * HEAD_SIZE)
            q = jnp.concatenate(
                [
                    q_ref[:, (h * GROUP + g) * HEAD_SIZE : (h * GROUP + g + 1) * HEAD_SIZE]
                    for g in range(GROUP)
                ],
                axis=0,
            )
            scores = jnp.where(allowed, dot_nt(q, k_ref[:size, lanes]), MASKED_SCORE)
            top = jnp.max(scores, axis=-1, keepdims=True)
            weights = jnp.exp2((scores - top) * EXP_SCALE)
            total = jnp.sum(weights, axis=-1, keepdims=True)
            out = dot_nn(weights.astype(LOW), v_ref[:size, lanes]) / total
            log_total = top * EXP_SCALE + jnp.log2(total)
            for g in range(GROUP):
                outs.append(out[g * block : (g + 1) * block].astype(LOW))
                totals.append(log_total[g * block : (g + 1) * block])
        attended = jnp.concatenate(outs, axis=1)
        attended_ref[...] = attended
        share_ref[...] = dot_nn(attended, weight[...]).astype(LOW)
        lane = lax.broadcasted_iota(jnp.int32, (block, HEAD_SIZE), 1)
        packed = jnp.zeros((block, HEAD_SIZE), FULL)
        for i, column in enumerate(totals):
            packed = jnp.where(lane == i, column, packed)
        total_ref[...] = packed

    place = place_ref[0] ^ (first + step)
    for j in range(n):
        pl.when(place == j)(functools.partial(work, j))


def attend(place, parts, q, k, v, seg_col, seg_row, n, chip, base):
    inner = len(parts) // 2
    length, q_width = q.shape
    k_width = k.shape[1]
    block = length // n
    first = 2 * chip
    whole = lambda i, p: (0, 0)
    natural = lambda i, p: (p[0] ^ (first + i), 0)
    slot = lambda i, p: (first + i, 0)
    plain = lambda i, p: (i, 0)
    base = list(base or ())
    before = 1 + len(parts) + 5
    return pl.pallas_call(
        functools.partial(attend_kernel, n, inner, first, bool(base)),
        out_shape=(
            jax.ShapeDtypeStruct((length, q_width), LOW),
            jax.ShapeDtypeStruct((length, HEAD_SIZE), FULL),
            jax.ShapeDtypeStruct((2 * block, D), LOW),
        ),
        grid_spec=pltpu.PrefetchScalarGridSpec(
            num_scalar_prefetch=1,
            grid=(2,),
            in_specs=[resident(p.shape) for p in parts]
            + [
                pl.BlockSpec((block, q_width), natural),
                resident((length, k_width)),
                resident((length, k_width)),
                pl.BlockSpec((block, 1), natural),
                pl.BlockSpec((1, length), whole),
            ]
            + [ANYWHERE] * len(base),
            out_specs=(
                pl.BlockSpec((block, q_width), slot),
                pl.BlockSpec((block, HEAD_SIZE), slot),
                pl.BlockSpec((block, D), plain),
            ),
            scratch_shapes=[pltpu.VMEM((q_width, D), LOW)],
        ),
        input_output_aliases={before: 0, before + 1: 1} if base else {},
        compiler_params=pltpu.CompilerParams(vmem_limit_bytes=48 * MIB),
        cost_estimate=pl.CostEstimate(
            flops=4 * block * q_width * (D + 2 * length), bytes_accessed=8 * MIB, transcendentals=0
        ),
        name="attend",
    )(place, *parts, q, k, v, seg_col, seg_row, *base)


def feed_kernel(chips, place_ref, *refs):
    gates, ups, shrinks = refs[:chips], refs[chips : 2 * chips], refs[2 * chips : 3 * chips]
    own_ref, other_ref, c_ref, c_other_ref = refs[3 * chips : 3 * chips + 4]
    x_out, c_out, active_ref, grad_ref, share_ref, share_other, back_ref, back_other = refs[3 * chips + 4 :]
    step = pl.program_id(0)
    mine = step < 2
    x = jnp.where(mine, own_ref[...], other_ref[...])
    c = jnp.where((step == 0) | (step == 3), c_ref[0], c_other_ref[0])
    x_out[...] = x
    c_out[...] = c
    size = gates[0].shape[1]
    share, back = 0.0, 0.0
    for s in range(chips):
        here = slice(s * size, (s + 1) * size)
        there = slice((chips + s) * size, (chips + s + 1) * size)
        gate = dot_nn(x, gates[s][...])
        up = dot_nn(x, ups[s][...])
        grad_active = dot_nt(c, shrinks[s][...]).astype(LOW).astype(FULL)
        gated = jax.nn.sigmoid(gate)
        silu = gate * gated
        active = (silu * up).astype(LOW)
        grad_gate = (grad_active * up * gated * (1.0 + gate * (1.0 - gated))).astype(LOW)
        grad_up = (grad_active * silu).astype(LOW)
        active_ref[:, here] = active
        grad_ref[:, here] = grad_gate
        grad_ref[:, there] = grad_up
        share = share + dot_nn(active, shrinks[s][...])
        back = back + dot_nt(grad_gate, gates[s][...]) + dot_nt(grad_up, ups[s][...])
    share = share.astype(LOW)
    back = back.astype(LOW)

    @pl.when(mine)
    def _():
        share_ref[...] = share
        back_ref[...] = back

    @pl.when(jnp.logical_not(mine))
    def _():
        share_other[...] = share
        back_other[...] = back


def feed(place, n, expand, shrink, own, other, c, c_other):
    chips = n // 2
    rows = own.shape[0]
    size = FF // n
    near = lambda i, p: (jnp.minimum(i, 1), 0)
    far = lambda i, p: (jnp.maximum(i - 2, 0), 0)
    flat = lambda i, p: (i, 0)
    core = lambda i, p: ((p[0] & 1) ^ (i // 2), 0, 0)
    block = rows // 2
    once = pl.Buffered(1)
    gates = [
        pl.BlockSpec((D, size), lambda i, p, s=s: (0, 2 * s + (p[0] & 1)), pipeline_mode=once)
        for s in range(chips)
    ]
    ups = [
        pl.BlockSpec((D, size), lambda i, p, s=s: (0, n + 2 * s + (p[0] & 1)), pipeline_mode=once)
        for s in range(chips)
    ]
    shrinks = [
        pl.BlockSpec((size, D), lambda i, p, s=s: (2 * s + (p[0] & 1), 0), pipeline_mode=once)
        for s in range(chips)
    ]
    wide = lambda w: jax.ShapeDtypeStruct((2 * rows, w), LOW)
    part = jax.ShapeDtypeStruct((rows, D), LOW)
    return pl.pallas_call(
        functools.partial(feed_kernel, chips),
        out_shape=(wide(D), wide(D), wide(FF // 2), wide(FF), part, part, part, part),
        grid_spec=pltpu.PrefetchScalarGridSpec(
            num_scalar_prefetch=1,
            grid=(4,),
            in_specs=gates
            + ups
            + shrinks
            + [
                pl.BlockSpec((block, D), near),
                pl.BlockSpec((block, D), far),
                pl.BlockSpec((1, block, D), core),
                pl.BlockSpec((1, block, D), core),
            ],
            out_specs=(
                pl.BlockSpec((block, D), flat),
                pl.BlockSpec((block, D), flat),
                pl.BlockSpec((block, FF // 2), flat),
                pl.BlockSpec((block, FF), flat),
                pl.BlockSpec((block, D), near),
                pl.BlockSpec((block, D), far),
                pl.BlockSpec((block, D), near),
                pl.BlockSpec((block, D), far),
            ),
        ),
        compiler_params=pltpu.CompilerParams(vmem_limit_bytes=56 * MIB),
        cost_estimate=pl.CostEstimate(
            flops=12 * rows * D * FF, bytes_accessed=30 * MIB, transcendentals=0
        ),
        name="feed",
    )(place, *[expand] * (2 * chips), *[shrink] * chips, own, other, c, c_other)


def back_kernel(n, inner, half, place_ref, *refs):
    qkv_parts = refs[: n * inner]
    out_parts = refs[n * inner : (n + 2) * inner]
    refs = refs[(n + 2) * inner :]
    (
        h_ref,
        attended_ref,
        total_ref,
        q_ref,
        k_ref,
        v_ref,
        raw_ref,
        cos_ref,
        sin_ref,
        seg_col_ref,
        seg_row_ref,
        gain_q_ref,
        gain_k_ref,
    ) = refs[:13]
    refs = refs[13:]
    if half:
        base_ref, refs = refs[0], refs[1:]
    grad_ref, share_ref, gains_ref, qkv, out, key_sum, value_sum = refs
    block = q_ref.shape[0]
    heads = k_ref.shape[1] // HEAD_SIZE
    step = pl.program_id(0)

    @pl.when(step == 0)
    def _():
        assemble(qkv_parts, qkv, all_rows(place_ref, n, inner))
        rows = out_parts[0].shape[0]
        size = out.shape[0] // rows
        for part, spot in zip(out_parts, chip_rows(place_ref, inner)):

            @pl.when(spot // size == half)
            def _():
                out[pl.ds(pl.multiple_of((spot % size) * rows, rows), rows), :] = part[...]

        key_sum[...] = jnp.zeros_like(key_sum)
        value_sum[...] = jnp.zeros_like(value_sum)
        gains_ref[...] = jnp.zeros_like(gains_ref)

    def work(j):
        size = (j + 1) * block
        grad_attended = dot_nt(h_ref[...], out[...]).astype(LOW)
        attended = attended_ref[...]
        totals = total_ref[...].T
        same = seg_col_ref[:size, :] == seg_row_ref[:, j * block : size]
        key = lax.broadcasted_iota(jnp.int32, (size, block), 0)
        own = lax.broadcasted_iota(jnp.int32, (size, block), 1) + j * block
        allowed = same & (own >= key)
        allowed = jnp.concatenate([allowed] * GROUP, axis=1)
        cos, sin = cos_ref[...], sin_ref[...]
        gains = gains_ref[...]
        kind = lax.broadcasted_iota(jnp.int32, gains.shape, 0)

        def head_back(grad, values, gain):
            grad = grad * cos + pltpu.roll(grad * sin, HEAD_SIZE // 2, 1)
            grad, gain_part = norm_back(values.astype(FULL), gain, grad)
            return grad.astype(LOW), jnp.sum(gain_part, axis=0, keepdims=True)

        query_grads, key_grads, value_grads = [], [], []
        for h in range(heads):
            lanes = slice(h * HEAD_SIZE, (h + 1) * HEAD_SIZE)
            k, v = k_ref[:size, lanes], v_ref[:size, lanes]
            head_lanes = [
                slice((h * GROUP + g) * HEAD_SIZE, (h * GROUP + g + 1) * HEAD_SIZE)
                for g in range(GROUP)
            ]
            q = jnp.concatenate([q_ref[:, s] for s in head_lanes], axis=0)
            up = jnp.concatenate([grad_attended[:, s] for s in head_lanes], axis=0)
            seen = jnp.concatenate([attended[:, s] for s in head_lanes], axis=0)
            log_total = jnp.concatenate(
                [totals[(half * heads + h) * GROUP + g : (half * heads + h) * GROUP + g + 1, :] for g in range(GROUP)], axis=1
            )
            row = jnp.sum(up.astype(FULL) * seen.astype(FULL), axis=1, keepdims=True)
            row = jnp.broadcast_to(row, (GROUP * block, HEAD_SIZE)).T[:1, :]
            probs = jnp.where(allowed, jnp.exp2(dot_nt(k, q) * EXP_SCALE - log_total), 0.0)
            grad_probs = dot_nt(v, up)
            grad_scores = (probs * (grad_probs - row)).astype(LOW)
            value_sum[:size, lanes] += dot_nn(probs.astype(LOW), up)
            key_sum[:size, lanes] += dot_nn(grad_scores, q)
            query_grad = dot_tn(grad_scores, k) * SCALE
            for g in range(GROUP):
                grad, gain_part = head_back(
                    query_grad[g * block : (g + 1) * block], raw_ref[:, head_lanes[g]], gain_q_ref[...]
                )
                query_grads.append(grad)
                gains = jnp.where(kind == 0, gains + gain_part, gains)
        own_rows = slice(j * block, size)
        for h in range(heads):
            lanes = slice(h * HEAD_SIZE, (h + 1) * HEAD_SIZE)
            first = (heads * GROUP + h) * HEAD_SIZE
            grad, gain_part = head_back(
                key_sum[own_rows, lanes] * SCALE, raw_ref[:, first : first + HEAD_SIZE], gain_k_ref[...]
            )
            key_grads.append(grad)
            gains = jnp.where(kind == 1, gains + gain_part, gains)
            value_grads.append(value_sum[own_rows, lanes].astype(LOW))
        gains_ref[...] = gains
        grad = jnp.concatenate(query_grads + key_grads + value_grads, axis=1)
        grad_ref[...] = grad
        share = dot_nt(grad, qkv[...])
        if half:
            share = share + base_ref[...].astype(FULL)
        share_ref[...] = share.astype(LOW)

    for j in range(n):
        pl.when(step == n - 1 - j)(functools.partial(work, j))


def back(
    place, qkv_parts, out_parts, hidden_grad, attended, totals, q, k, v, raw, cos, sin, seg_col,
    seg_row, gain_q, gain_k, half, base,
):
    inner = len(out_parts) // 2
    n = len(qkv_parts) // inner
    length = q.shape[0]
    q_width, k_width = q.shape[1] // HALVES, k.shape[1] // HALVES
    block = length // n
    width = q_width + 2 * k_width
    whole = lambda i, p: (0, 0)
    natural = lambda i, p: (n - 1 - i, 0)
    slot = lambda i, p: (p[0] ^ (n - 1 - i), 0)
    natural_half = lambda i, p: (n - 1 - i, half)
    slot_half = lambda i, p: (p[0] ^ (n - 1 - i), half)
    base = [] if base is None else [base]
    return pl.pallas_call(
        functools.partial(back_kernel, n, inner, half),
        out_shape=(
            jax.ShapeDtypeStruct((length, width), LOW),
            jax.ShapeDtypeStruct((length, D), LOW),
            jax.ShapeDtypeStruct((8, HEAD_SIZE), FULL),
        ),
        grid_spec=pltpu.PrefetchScalarGridSpec(
            num_scalar_prefetch=1,
            grid=(n,),
            in_specs=[resident((p.shape[0], width), half) for p in qkv_parts]
            + [resident(p.shape) for p in out_parts]
            + [
                pl.BlockSpec((block, D), slot),
                pl.BlockSpec((block, q_width), slot_half),
                pl.BlockSpec((block, HEAD_SIZE), slot),
                pl.BlockSpec((block, q_width), natural_half),
                resident((length, k_width), half),
                resident((length, k_width), half),
                pl.BlockSpec((block, q_width + k_width), natural_half),
                pl.BlockSpec((block, HEAD_SIZE), natural),
                pl.BlockSpec((block, HEAD_SIZE), natural),
                pl.BlockSpec((length, 1), whole),
                pl.BlockSpec((1, length), whole),
                pl.BlockSpec((1, HEAD_SIZE), whole),
                pl.BlockSpec((1, HEAD_SIZE), whole),
            ]
            + [pl.BlockSpec((block, D), slot)] * len(base),
            out_specs=(
                pl.BlockSpec((block, width), natural),
                pl.BlockSpec((block, D), slot),
                pl.BlockSpec((8, HEAD_SIZE), whole),
            ),
            scratch_shapes=[
                pltpu.VMEM((D, width), LOW),
                pltpu.VMEM((q_width, D), LOW),
                pltpu.VMEM((length, k_width), FULL),
                pltpu.VMEM((length, k_width), FULL),
            ],
        ),
        compiler_params=pltpu.CompilerParams(vmem_limit_bytes=56 * MIB),
        cost_estimate=pl.CostEstimate(
            flops=2 * length * D * (q_width + width) + 5 * length * length * q_width,
            bytes_accessed=30 * MIB,
            transcendentals=0,
        ),
        name="back",
    )(
        place, *qkv_parts, *out_parts, hidden_grad, attended, totals, q, k, v, raw, cos, sin,
        seg_col, seg_row, gain_q, gain_k, *base,
    )


def adam_kernel(rate, key_ref, *refs):
    cuts = refs[:-7]
    weight_ref, first_ref, second_ref, new_first, new_second, new_weight, grad = refs[-7:]
    for s, cut in enumerate(cuts):

        @pl.when((pl.program_id(1) ^ key_ref[0]) == s)
        def _():
            grad[...] = cut[...].astype(FULL)

    results = adam_step(weight_ref[...], first_ref[...], second_ref[...], grad[...], rate)
    new_first[...], new_second[...], new_weight[...] = results


def adam_cuts(key, cuts, weight, first, second, rate, size, column):
    rows, columns = cuts[0].shape
    cut = pl.BlockSpec((rows, size), lambda i, s, p: (0, i))
    spec = pl.BlockSpec((rows, size), lambda i, s, p: (0, column(i, s)))
    shape = jax.ShapeDtypeStruct(weight.shape, FULL)
    return pl.pallas_call(
        functools.partial(adam_kernel, rate),
        out_shape=(shape, shape, shape),
        grid_spec=pltpu.PrefetchScalarGridSpec(
            num_scalar_prefetch=1,
            grid=(columns // size, len(cuts)),
            in_specs=[cut] * len(cuts) + [spec] * 3,
            out_specs=(spec,) * 3,
            scratch_shapes=[pltpu.VMEM((rows, size), FULL)],
        ),
        cost_estimate=pl.CostEstimate(
            flops=20 * weight.size, bytes_accessed=26 * weight.size, transcendentals=weight.size
        ),
        compiler_params=pltpu.CompilerParams(vmem_limit_bytes=24 * MIB),
        name="adam_cuts",
    )(key, *cuts, weight, first, second)


def adam_pair_kernel(rate, place_ref, own_ref, other_ref, weight_ref, first_ref, second_ref, *outs):
    mine = pl.program_id(1) == (place_ref[0] & 1)
    grad = jnp.where(mine, own_ref[...].astype(FULL), other_ref[...].astype(FULL))
    results = adam_step(weight_ref[...], first_ref[...], second_ref[...], grad, rate)
    outs[0][...], outs[1][...], outs[2][...] = results


def adam_pair(place, own, other, weight, first, second, rate, size):
    rows, width = own.shape
    cut = pl.BlockSpec((rows, size), lambda i, c, p: (0, i))
    spec = pl.BlockSpec((rows, size), lambda i, c, p: (0, 2 * i + c))
    shape = jax.ShapeDtypeStruct(weight.shape, FULL)
    return pl.pallas_call(
        functools.partial(adam_pair_kernel, rate),
        out_shape=(shape, shape, shape),
        grid_spec=pltpu.PrefetchScalarGridSpec(
            num_scalar_prefetch=1,
            grid=(width // size, 2),
            in_specs=[cut, cut] + [spec] * 3,
            out_specs=(spec,) * 3,
        ),
        cost_estimate=pl.CostEstimate(
            flops=20 * weight.size, bytes_accessed=26 * weight.size, transcendentals=weight.size
        ),
        compiler_params=pltpu.CompilerParams(vmem_limit_bytes=24 * MIB),
        name="adam_pair",
    )(place, own, other, weight, first, second)


def after(value, *others):
    return lax.optimization_barrier((value, *others))[0]


def make(n, inner, reps):
    chips = n // 2

    def swap_ctx(value, s):
        return lax.ppermute(value, "ctx", [(i, i ^ s) for i in range(n)])

    def swap_core(value):
        return swap_ctx(value, 1)

    def swap_chip(value, s):
        return swap_ctx(value, 2 * s)

    def swap_grp(value, t):
        return lax.ppermute(value, "grp", [(i, i ^ t) for i in range(inner)])

    def over_chips(value):
        return [value] + [swap_chip(value, s) for s in range(1, chips)]

    def over_grp(value):
        return [value] + [swap_grp(value, t) for t in range(1, inner)]

    def sum_of(parts):
        total = parts[0].astype(FULL)
        for part in parts[1:]:
            total = total + part.astype(FULL)
        return total

    def swap_plane(value, s, t):
        pairs = [(c * inner + g, (c ^ s) * inner + (g ^ t)) for c in range(n) for g in range(inner)]
        return lax.ppermute(value, ("ctx", "grp"), pairs)

    def pick(value, axis, index):
        return lax.dynamic_index_in_dim(value, index, axis, False)

    middle = reps // 2
    hops = [([(k, k + 1), (reps - 1 - k, reps - 2 - k)], None) for k in range(middle - 1)]
    hops.append(([(middle - 1, middle), (middle, middle - 1)], None))
    hops += [
        ([(k, k - 1), (reps - 1 - k, reps - k)], (k - 1, reps - k)) for k in range(middle - 1, 0, -1)
    ]

    def on_device(
        tokens,
        segment_ids,
        positions,
        cotangent,
        qkv_weight,
        qkv_first,
        qkv_second,
        out_weight,
        out_first,
        out_second,
        expand_weight,
        expand_first,
        expand_second,
        shrink_weight,
        shrink_first,
        shrink_second,
        norm_gains,
        gains_first,
        gains_second,
    ):
        seqs, block, _ = tokens.shape
        length = n * block
        me = lax.axis_index("ctx")
        core = me & 1
        chip = me >> 1
        mine = lax.axis_index("grp")
        place = jnp.stack([me, mine]).astype(jnp.int32)
        order = me ^ jnp.arange(n)
        q_width = QUERY_FEATURES // chips
        k_width = KEY_FEATURES // chips
        width = q_width + 2 * k_width
        rows = qkv_weight.shape[0]

        rep = lax.axis_index("rep")

        def qkv_piece(s):
            to = chip ^ s
            parts = []
            for i in range(HALVES):
                for first, size in ((0, q_width), (QUERY_FEATURES, k_width), (QUERY_FEATURES + KEY_FEATURES, k_width)):
                    start = first + to * size + i * (size // HALVES)
                    parts.append(lax.dynamic_slice_in_dim(qkv_weight, start, size // HALVES, 1))
            return jnp.concatenate(parts, axis=1).astype(LOW)

        small = jnp.concatenate(
            [
                segment_ids.reshape(-1).astype(FULL),
                positions.reshape(-1).astype(FULL),
                norm_gains.astype(LOW).astype(FULL),
            ]
        ).reshape(1, -1)
        small = [
            swap_plane(small, s, t) if s or t else small for s in range(n) for t in range(inner)
        ]
        tokens, qkv_low, other_tokens, *small = lax.optimization_barrier(
            (tokens, [qkv_piece(s) for s in range(chips)], pick(tokens, 0, core ^ 1), *small)
        )
        small = jnp.stack(small)
        small = small.reshape(n, inner, -1)[order]
        notes = small[:, 0, : 2 * seqs * block].reshape(n, 2, seqs, block)
        notes = pick(notes, 2, core)
        notes = jnp.moveaxis(notes, 0, 1).reshape(2, length)
        gains = small[:, mine ^ jnp.arange(inner), 2 * seqs * block :].reshape(1, -1)
        gain_one, gain_two = gains[:, :D], gains[:, D : 2 * D]
        gain_query = gains[:, 2 * D : 2 * D + HEAD_SIZE]
        gain_key = gains[:, 2 * D + HEAD_SIZE :]

        token_slots = [pick(tokens, 0, core), swap_core(other_tokens)]
        for s in range(1, chips):
            token_slots += [swap_chip(part, s) for part in token_slots[:2]]

        landed = [qkv_low[0]] + [swap_chip(qkv_low[s], s) for s in range(1, chips)]
        qkv_parts = []
        for part in landed:
            near = over_grp(part)
            qkv_parts += near + [swap_core(p) for p in near]

        near = over_grp(out_weight.astype(LOW))
        out_parts = near + [swap_core(p) for p in near]
        def gather_all(weight):
            return lax.all_gather(weight.astype(LOW), ("ctx", "grp"), axis=0, tiled=True)

        expand_full = gather_all(expand_weight)
        shrink_full = gather_all(shrink_weight)
        other_cotangent = swap_core(cotangent)

        ladder = jnp.arange(HEAD_SIZE) % (HEAD_SIZE // 2)
        frequency = jnp.exp(ladder.astype(FULL) * (-2.0 * math.log(ROPE_BASE) / HEAD_SIZE))
        angles = notes[1][:, None] * frequency[None, :]
        sign = jnp.where(jnp.arange(HEAD_SIZE) < HEAD_SIZE // 2, -1.0, 1.0)
        cos, sin = jnp.cos(angles), jnp.sin(angles) * sign
        seg_col, seg_row = notes[0][:, None], notes[0][None, :]

        normed, q, k, v, raw = project(
            place, qkv_parts, token_slots, gain_one, gain_query, gain_key, cos, sin
        )
        base, shares = None, []
        for s in range(chips - 1, -1, -1):
            *base, share = attend(place, out_parts, q, k, v, seg_col, seg_row, n, s, base)
            shares.append(swap_chip(share, s) if s else share)
        attended, totals = base
        inputs = jnp.concatenate(token_slots[:2]).astype(FULL)
        hidden = inputs + sum_of(shares)
        normed_two = (hidden * inverse_rms(hidden) * gain_two).astype(LOW)

        x_all, c_all, active, grad_gate_up, share, share_other, back_share, back_other = feed(
            place, n, expand_full, shrink_full, normed_two, swap_core(normed_two), cotangent,
            other_cotangent,
        )
        normed_grad = sum_of([back_share, swap_core(back_other)])
        hidden_grad, gain_part = norm_back(hidden, gain_two, normed_grad)
        gain_two_grad = jnp.sum(gain_part, axis=0)
        hidden_grad = hidden_grad + c_all[: 2 * block].astype(FULL)
        hidden_low = hidden_grad.astype(LOW)
        grad_slots = over_chips(hidden_low)
        grad_all = jnp.concatenate(grad_slots)

        def by_sequence(kept, landed):
            return jnp.where(core == 0, jnp.stack([kept, landed]), jnp.stack([landed, kept]))

        output = (hidden + sum_of([share, swap_core(share_other)])).astype(LOW)
        output = by_sequence(output[:block], swap_core(output[block:]))

        line = []

        def next_sum(kept, sent):
            if line:
                sent = lax.optimization_barrier((*sent, *line))[: len(sent)]
            total = sum_of([kept, *sent]).astype(LOW)
            line[:] = [total]
            return total

        def next_cut(kept, sent, axis, place, count):
            sent = lax.optimization_barrier((*sent, *line))[: len(sent)]
            pieces = [
                sum_of([pick(value, axis, place ^ s) for value in (kept, *sent)]).astype(LOW)
                for s in range(count)
            ]
            line[:] = pieces
            return pieces

        def go(value, step=0):
            return [value, lax.ppermute(value, "rep", hops[step][0]), step]

        def step_on(trip):
            value, landed, step = trip
            if step == len(hops):
                return
            takes = hops[step][1]
            if takes is None:
                value = next_sum(value, [landed])
            else:
                landed = after(landed, *line)
                value = jnp.where((rep == takes[0]) | (rep == takes[1]), landed, value)
                line[:] = [value]
            step += 1
            trip[:] = go(value, step) if step < len(hops) else [value, None, step]

        def send_x(parts):
            return parts[0], [swap_chip(parts[s], s) for s in range(1, chips)]

        def send_y(parts):
            return parts[0], [swap_grp(parts[t], t) for t in range(1, inner)]

        def cut_qkv(grad):
            grad_qkv = dot_tn(normed, grad).astype(LOW)
            cuts = grad_qkv.reshape(chips, 2, inner, rows, width // HALVES)
            return pick(cuts, 1, core), [swap_core(pick(cuts, 1, core ^ 1))]

        x_late, active_late = lax.optimization_barrier((x_all, active, hidden_low))[:2]
        grad_expand = dot_tn(x_late, grad_gate_up).astype(LOW)
        expand_cuts = grad_expand.reshape(chips, 2, inner, rows, FF)
        other_rows = pick(expand_cuts, 1, core ^ 1)
        other_sent = [swap_grp(pick(other_rows, 1, mine ^ t), t) for t in range(1, inner)]
        grad_shrink = dot_tn(active_late, c_all).astype(LOW)
        shrink_cuts = grad_shrink.reshape(chips, inner, FF // (n * inner), D)
        shrink_sent = [swap_grp(pick(shrink_cuts, 1, mine ^ t), t) for t in range(1, inner)]
        own_rows = pick(expand_cuts, 1, core)
        late_rows = after(own_rows, grad_slots[-1])
        own_sent = [swap_chip(pick(late_rows, 0, chip ^ s), s) for s in range(1, chips)]
        grad, back_all, head_gains = back(
            place, qkv_parts, out_parts, grad_all, attended, totals, q, k, v, raw, cos, sin, seg_col,
            seg_row, gain_query, gain_key, 0, None,
        )

        line[:] = [head_gains]
        own_cut = send_y(next_cut(pick(own_rows, 0, chip), own_sent, 0, mine, inner))
        other_cut = send_x(next_cut(pick(other_rows, 1, mine), other_sent, 0, chip, chips))
        qkv_cuts, qkv_sent = cut_qkv(after(grad, *line))
        shrink_cut = send_x(next_cut(pick(shrink_cuts, 1, mine), shrink_sent, 0, chip, chips))
        grad_out = dot_tn(after(attended, *line), grad_all).astype(LOW)
        out_cuts = grad_out.reshape(2, inner, out_weight.shape[0], D)
        out_sent = [swap_core(pick(out_cuts, 0, core ^ 1))]
        qkv_cut = send_y(next_cut(qkv_cuts, qkv_sent, 1, mine, inner))
        other_cut = swap_core(next_sum(*other_cut))
        out_cut = send_y(next_cut(pick(out_cuts, 0, core), out_sent, 0, mine, inner))
        shares = []
        for s in range(1, chips):
            share = after(back_all[2 * s * block : 2 * (s + 1) * block], *line)
            shares.append(swap_chip(share, s))
        other_cut = after(other_cut, *line)
        line[:] = [other_cut]
        other = go(other_cut)
        own = go(next_sum(*own_cut))
        shrink = go(next_sum(*shrink_cut))
        step_on(other)
        kept, sent = send_x(next_cut(*qkv_cut, 0, chip, chips))
        qkv = [go(kept)]
        out = go(next_sum(*out_cut))
        step_on(own)
        step_on(other)
        for value in sent:
            value = after(value, *line)
            line[:] = [value]
            qkv.append(go(value))
        step_on(shrink)
        step_on(own)

        shares = [back_all[: 2 * block]] + [after(value, *line) for value in shares]
        input_part, gain_part = norm_back(inputs, gain_one, sum_of(shares))
        gain_one_grad = jnp.sum(gain_part, axis=0)
        input_grad = (input_part + hidden_grad).astype(LOW)
        input_landed = swap_core(input_grad[block:])
        line[:] = [gain_one_grad]

        step_on(qkv[0])
        step_on(other)
        step_on(shrink)
        step_on(out)
        step_on(own)
        step_on(qkv[0])
        for trip in qkv[1:]:
            step_on(trip)
        step_on(out)
        grad_gains = jnp.concatenate([gain_one_grad, gain_two_grad, head_gains[0], head_gains[1]])
        total_gains = lax.psum(after(grad_gains, *line), ("ctx", "grp", "rep"))
        line[:] = [total_gains]
        total_gains = lax.dynamic_slice_in_dim(
            total_gains, (me * inner + mine) * norm_gains.shape[0], norm_gains.shape[0], 0
        )
        step_on(shrink)
        for trip in qkv[1:]:
            step_on(trip)
        trips = (other, own, shrink, out, *qkv)
        for _ in hops:
            for trip in trips:
                step_on(trip)
        other_cut, own_cut, total_shrink, total_out, *qkv_cuts = [trip[0] for trip in trips]
        input_grad = by_sequence(input_grad[:block], input_landed)

        def qkv_column(i, s):
            q_blocks = q_width // k_width
            k_place = QUERY_FEATURES // k_width + s
            v_place = k_place + chips
            return jnp.where(i < q_blocks, s * q_blocks + i, jnp.where(i == q_blocks, k_place, v_place))

        key = chip.reshape(1).astype(jnp.int32)
        return (
            output,
            input_grad,
            *adam_cuts(
                key, qkv_cuts, qkv_weight, qkv_first, qkv_second, RATE_QKV, k_width, qkv_column
            ),
            *adam_step(out_weight, out_first, out_second, total_out.astype(FULL), RATE_OUT),
            *adam_pair(
                place, own_cut, other_cut, expand_weight, expand_first, expand_second, RATE_EXPAND,
                FF // n,
            ),
            *adam_step(
                shrink_weight, shrink_first, shrink_second, total_shrink.astype(FULL), RATE_SHRINK
            ),
            *adam_step(norm_gains, gains_first, gains_second, total_gains, RATE_GAINS),
        )

    return on_device


def solution(mesh):
    token_rows = P(("grp", "rep"), "ctx", None)
    token_notes = P(("grp", "rep"), "ctx")
    weight_rows = P(("ctx", "grp"), None)
    gain_rows = P(("ctx", "grp"))
    states = (weight_rows,) * 12 + (gain_rows,) * 3
    return jax.shard_map(
        make(mesh.shape["ctx"], mesh.shape["grp"], mesh.shape["rep"]),
        mesh=mesh,
        in_specs=(token_rows, token_notes, token_notes, token_rows) + states,
        out_specs=(token_rows, token_rows) + states,
        check_vma=False,
    )
```

```python
import functools
import math

import jax
import jax.numpy as jnp
from jax import lax
from jax.experimental import pallas as pl
from jax.experimental.pallas import tpu as pltpu
from jax.sharding import PartitionSpec as P

D = 1024
QUERY_HEADS = 16
KEY_VALUE_HEADS = 8
HEAD_SIZE = 128
FF = 3072
STEP = 10
QUERY_FEATURES = 2048
KEY_FEATURES = 1024
GROUP = QUERY_HEADS // KEY_VALUE_HEADS

EPS_NORM = 1e-06
ROPE_BASE = 1000000.0
MASKED_SCORE = -1e30
BETA_ONE = 0.9
BETA_TWO = 0.95
ADAM_EPS = 1e-08
WEIGHT_DECAY = 0.1
RATE_QKV = 0.1
RATE_OUT = 0.5
RATE_EXPAND = 0.1
RATE_SHRINK = 0.06
RATE_GAINS = 0.6

SCALE = HEAD_SIZE**-0.5
EXP_SCALE = SCALE * math.log2(math.e)
LOW = jnp.bfloat16
FULL = jnp.float32
MIB = 1 << 20
HALVES = 2


def dot_nn(a, b):
    return jnp.dot(a, b, preferred_element_type=FULL)


def dot_nt(a, b):
    return lax.dot_general(a, b, (((1,), (1,)), ((), ())), preferred_element_type=FULL)


def dot_tn(a, b):
    return lax.dot_general(a, b, (((0,), (0,)), ((), ())), preferred_element_type=FULL)


def inverse_rms(values):
    return lax.rsqrt(jnp.mean(values * values, axis=-1, keepdims=True) + EPS_NORM)


def norm_back(values, gain, incoming):
    scale = inverse_rms(values)
    normed = values * scale
    scaled = incoming * gain
    grad = scale * (scaled - normed * jnp.mean(scaled * normed, axis=-1, keepdims=True))
    return grad, incoming * normed


def adam_step(weight, first_moment, second_moment, gradient, step_rate):
    first_moment = BETA_ONE * first_moment + (1.0 - BETA_ONE) * gradient
    second_moment = BETA_TWO * second_moment + (1.0 - BETA_TWO) * gradient * gradient
    fix_one = 1.0 - BETA_ONE**STEP
    fix_two = 1.0 - BETA_TWO**STEP
    step_dir = first_moment / fix_one / (jnp.sqrt(second_moment / fix_two) + ADAM_EPS)
    return (first_moment, second_moment, weight - step_rate * (step_dir + WEIGHT_DECAY * weight))


def assemble(parts, whole, blocks):
    rows = whole.shape[0] // len(parts)
    for part, block in zip(parts, blocks):
        whole[pl.ds(pl.multiple_of(block * rows, rows), rows), :] = part[...]


def all_rows(place_ref, n, inner):
    return [(place_ref[0] ^ s) * inner + (place_ref[1] ^ t) for s in range(n) for t in range(inner)]


def chip_rows(place_ref, inner):
    return [
        ((place_ref[0] & 1) ^ k) * inner + (place_ref[1] ^ t) for k in range(2) for t in range(inner)
    ]


ANYWHERE = pl.BlockSpec(memory_space=pl.ANY)


def resident(shape, column=0):
    return pl.BlockSpec(shape, lambda *_: (0, column), pipeline_mode=pl.Buffered(1))


def project_kernel(n, inner, place_ref, *refs):
    parts = refs[: n * inner]
    pieces = refs[n * inner : n * inner + n]
    gain_ref, gain_q_ref, gain_k_ref, cos_ref, sin_ref = refs[n * inner + n : n * inner + n + 5]
    normed_ref, q_ref, k_ref, v_ref, raw_ref = refs[n * inner + n + 5 : n * inner + n + 10]
    weight, token = refs[n * inner + n + 10 :]
    step = pl.program_id(0)

    @pl.when(step == 0)
    def _():
        assemble(parts, weight, all_rows(place_ref, n, inner))

    for s in range(n):

        @pl.when((place_ref[0] ^ step) == s)
        def _():
            token[...] = pieces[s][...]

    x = token[...].astype(FULL)
    normed = (x * inverse_rms(x) * gain_ref[...]).astype(LOW)
    normed_ref[...] = normed
    projected = dot_nn(normed, weight[...])
    q_half, k_half = q_ref.shape[1] // HALVES, k_ref.shape[1] // HALVES
    raw_half = q_half + k_half
    half = raw_half + k_half
    cos, sin = cos_ref[...], sin_ref[...]

    def turn(values, gain):
        values = values * inverse_rms(values) * gain
        return (values * cos + pltpu.roll(values, HEAD_SIZE // 2, 1) * sin).astype(LOW)

    for i in range(HALVES):
        first = i * half
        raw_ref[:, i * raw_half : (i + 1) * raw_half] = projected[:, first : first + raw_half].astype(LOW)
        v_ref[:, i * k_half : (i + 1) * k_half] = projected[:, first + raw_half : first + half].astype(LOW)
        for h in range(0, q_half, HEAD_SIZE):
            values = projected[:, first + h : first + h + HEAD_SIZE]
            q_ref[:, i * q_half + h : i * q_half + h + HEAD_SIZE] = turn(values, gain_q_ref[...])
        for h in range(0, k_half, HEAD_SIZE):
            values = projected[:, first + q_half + h : first + q_half + h + HEAD_SIZE]
            k_ref[:, i * k_half + h : i * k_half + h + HEAD_SIZE] = turn(values, gain_k_ref[...])


def project(place, parts, pieces, gain, gain_q, gain_k, cos, sin):
    n = len(pieces)
    inner = len(parts) // n
    block = pieces[0].shape[0]
    length = n * block
    width = parts[0].shape[1]
    q_width, k_width = width // 2, width // 4
    whole = lambda j, p: (0, 0)
    natural = lambda j, p: (j, 0)
    return pl.pallas_call(
        functools.partial(project_kernel, n, inner),
        out_shape=(
            jax.ShapeDtypeStruct((length, D), LOW),
            jax.ShapeDtypeStruct((length, q_width), LOW),
            jax.ShapeDtypeStruct((length, k_width), LOW),
            jax.ShapeDtypeStruct((length, k_width), LOW),
            jax.ShapeDtypeStruct((length, q_width + k_width), LOW),
        ),
        grid_spec=pltpu.PrefetchScalarGridSpec(
            num_scalar_prefetch=1,
            grid=(n,),
            in_specs=[resident(p.shape) for p in parts]
            + [resident((block, D))] * n
            + [
                pl.BlockSpec((1, D), whole),
                pl.BlockSpec((1, HEAD_SIZE), whole),
                pl.BlockSpec((1, HEAD_SIZE), whole),
                pl.BlockSpec((block, HEAD_SIZE), natural),
                pl.BlockSpec((block, HEAD_SIZE), natural),
            ],
            out_specs=(
                pl.BlockSpec((block, D), natural),
                pl.BlockSpec((block, q_width), natural),
                pl.BlockSpec((block, k_width), natural),
                pl.BlockSpec((block, k_width), natural),
                pl.BlockSpec((block, q_width + k_width), natural),
            ),
            scratch_shapes=[
                pltpu.VMEM((D, width), LOW),
                pltpu.VMEM((block, D), LOW),
            ],
        ),
        compiler_params=pltpu.CompilerParams(vmem_limit_bytes=40 * MIB),
        cost_estimate=pl.CostEstimate(
            flops=2 * length * D * width, bytes_accessed=16 * MIB, transcendentals=0
        ),
        name="project",
    )(place, *parts, *pieces, gain, gain_q, gain_k, cos, sin)


def attend_kernel(n, inner, first, has_base, place_ref, *refs):
    parts = refs[: 2 * inner]
    q_ref, k_ref, v_ref, seg_col_ref, seg_row_ref = refs[2 * inner : 2 * inner + 5]
    rest = refs[2 * inner + 5 + (2 if has_base else 0) :]
    attended_ref, total_ref, share_ref, weight = rest
    block = q_ref.shape[0]
    heads = k_ref.shape[1] // HEAD_SIZE
    step = pl.program_id(0)

    @pl.when(step == 0)
    def _():
        assemble(parts, weight, chip_rows(place_ref, inner))

    def work(j):
        size = (j + 1) * block
        same = seg_col_ref[...] == seg_row_ref[:, :size]
        own = lax.broadcasted_iota(jnp.int32, (block, size), 0) + j * block
        key = lax.broadcasted_iota(jnp.int32, (block, size), 1)
        allowed = same & (own >= key)
        allowed = jnp.concatenate([allowed] * GROUP, axis=0)
        outs, totals = [], []
        for h in range(heads):
            lanes = slice(h * HEAD_SIZE, (h + 1) * HEAD_SIZE)
            q = jnp.concatenate(
                [
                    q_ref[:, (h * GROUP + g) * HEAD_SIZE : (h * GROUP + g + 1) * HEAD_SIZE]
                    for g in range(GROUP)
                ],
                axis=0,
            )
            scores = jnp.where(allowed, dot_nt(q, k_ref[:size, lanes]), MASKED_SCORE)
            top = jnp.max(scores, axis=-1, keepdims=True)
            weights = jnp.exp2((scores - top) * EXP_SCALE)
            total = jnp.sum(weights, axis=-1, keepdims=True)
            out = dot_nn(weights.astype(LOW), v_ref[:size, lanes]) / total
            log_total = top * EXP_SCALE + jnp.log2(total)
            for g in range(GROUP):
                outs.append(out[g * block : (g + 1) * block].astype(LOW))
                totals.append(log_total[g * block : (g + 1) * block])
        attended = jnp.concatenate(outs, axis=1)
        attended_ref[...] = attended
        share_ref[...] = dot_nn(attended, weight[...]).astype(LOW)
        lane = lax.broadcasted_iota(jnp.int32, (block, HEAD_SIZE), 1)
        count = len(totals) // HALVES
        for half in range(HALVES):
            packed = jnp.zeros((block, HEAD_SIZE), FULL)
            for i, column in enumerate(totals[half * count : (half + 1) * count]):
                packed = jnp.where(lane == i, column, packed)
            total_ref[:, half * HEAD_SIZE : (half + 1) * HEAD_SIZE] = packed

    place = place_ref[0] ^ (first + step)
    for j in range(n):
        pl.when(place == j)(functools.partial(work, j))


def attend(place, parts, q, k, v, seg_col, seg_row, n, chip, base):
    inner = len(parts) // 2
    length, q_width = q.shape
    k_width = k.shape[1]
    block = length // n
    first = 2 * chip
    whole = lambda i, p: (0, 0)
    natural = lambda i, p: (p[0] ^ (first + i), 0)
    slot = lambda i, p: (first + i, 0)
    plain = lambda i, p: (i, 0)
    base = list(base or ())
    before = 1 + len(parts) + 5
    return pl.pallas_call(
        functools.partial(attend_kernel, n, inner, first, bool(base)),
        out_shape=(
            jax.ShapeDtypeStruct((length, q_width), LOW),
            jax.ShapeDtypeStruct((length, HALVES * HEAD_SIZE), FULL),
            jax.ShapeDtypeStruct((2 * block, D), LOW),
        ),
        grid_spec=pltpu.PrefetchScalarGridSpec(
            num_scalar_prefetch=1,
            grid=(2,),
            in_specs=[resident(p.shape) for p in parts]
            + [
                pl.BlockSpec((block, q_width), natural),
                resident((length, k_width)),
                resident((length, k_width)),
                pl.BlockSpec((block, 1), natural),
                pl.BlockSpec((1, length), whole),
            ]
            + [ANYWHERE] * len(base),
            out_specs=(
                pl.BlockSpec((block, q_width), slot),
                pl.BlockSpec((block, HALVES * HEAD_SIZE), slot),
                pl.BlockSpec((block, D), plain),
            ),
            scratch_shapes=[pltpu.VMEM((q_width, D), LOW)],
        ),
        input_output_aliases={before: 0, before + 1: 1} if base else {},
        compiler_params=pltpu.CompilerParams(vmem_limit_bytes=48 * MIB),
        cost_estimate=pl.CostEstimate(
            flops=4 * block * q_width * (D + 2 * length), bytes_accessed=8 * MIB, transcendentals=0
        ),
        name="attend",
    )(place, *parts, q, k, v, seg_col, seg_row, *base)


def feed_kernel(chips, place_ref, *refs):
    gates, ups, shrinks = refs[:chips], refs[chips : 2 * chips], refs[2 * chips : 3 * chips]
    own_ref, other_ref, c_ref, c_other_ref = refs[3 * chips : 3 * chips + 4]
    x_out, c_out, active_ref, grad_ref, share_ref, share_other, back_ref, back_other = refs[3 * chips + 4 :]
    step = pl.program_id(0)
    mine = step < 2
    x = jnp.where(mine, own_ref[...], other_ref[...])
    c = jnp.where((step == 0) | (step == 3), c_ref[0], c_other_ref[0])
    x_out[...] = x
    c_out[...] = c
    size = gates[0].shape[1]
    share, back = 0.0, 0.0
    for s in range(chips):
        here = slice(s * size, (s + 1) * size)
        there = slice((chips + s) * size, (chips + s + 1) * size)
        gate = dot_nn(x, gates[s][...])
        up = dot_nn(x, ups[s][...])
        grad_active = dot_nt(c, shrinks[s][...]).astype(LOW).astype(FULL)
        gated = jax.nn.sigmoid(gate)
        silu = gate * gated
        active = (silu * up).astype(LOW)
        grad_gate = (grad_active * up * gated * (1.0 + gate * (1.0 - gated))).astype(LOW)
        grad_up = (grad_active * silu).astype(LOW)
        active_ref[:, here] = active
        grad_ref[:, here] = grad_gate
        grad_ref[:, there] = grad_up
        share = share + dot_nn(active, shrinks[s][...])
        back = back + dot_nt(grad_gate, gates[s][...]) + dot_nt(grad_up, ups[s][...])
    share = share.astype(LOW)
    back = back.astype(LOW)

    @pl.when(mine)
    def _():
        share_ref[...] = share
        back_ref[...] = back

    @pl.when(jnp.logical_not(mine))
    def _():
        share_other[...] = share
        back_other[...] = back


def feed(place, n, expand, shrink, own, other, c, c_other):
    chips = n // 2
    rows = own.shape[0]
    size = FF // n
    near = lambda i, p: (jnp.minimum(i, 1), 0)
    far = lambda i, p: (jnp.maximum(i - 2, 0), 0)
    flat = lambda i, p: (i, 0)
    core = lambda i, p: ((p[0] & 1) ^ (i // 2), 0, 0)
    block = rows // 2
    once = pl.Buffered(1)
    gates = [
        pl.BlockSpec((D, size), lambda i, p, s=s: (0, 2 * s + (p[0] & 1)), pipeline_mode=once)
        for s in range(chips)
    ]
    ups = [
        pl.BlockSpec((D, size), lambda i, p, s=s: (0, n + 2 * s + (p[0] & 1)), pipeline_mode=once)
        for s in range(chips)
    ]
    shrinks = [
        pl.BlockSpec((size, D), lambda i, p, s=s: (2 * s + (p[0] & 1), 0), pipeline_mode=once)
        for s in range(chips)
    ]
    wide = lambda w: jax.ShapeDtypeStruct((2 * rows, w), LOW)
    part = jax.ShapeDtypeStruct((rows, D), LOW)
    return pl.pallas_call(
        functools.partial(feed_kernel, chips),
        out_shape=(wide(D), wide(D), wide(FF // 2), wide(FF), part, part, part, part),
        grid_spec=pltpu.PrefetchScalarGridSpec(
            num_scalar_prefetch=1,
            grid=(4,),
            in_specs=gates
            + ups
            + shrinks
            + [
                pl.BlockSpec((block, D), near),
                pl.BlockSpec((block, D), far),
                pl.BlockSpec((1, block, D), core),
                pl.BlockSpec((1, block, D), core),
            ],
            out_specs=(
                pl.BlockSpec((block, D), flat),
                pl.BlockSpec((block, D), flat),
                pl.BlockSpec((block, FF // 2), flat),
                pl.BlockSpec((block, FF), flat),
                pl.BlockSpec((block, D), near),
                pl.BlockSpec((block, D), far),
                pl.BlockSpec((block, D), near),
                pl.BlockSpec((block, D), far),
            ),
        ),
        compiler_params=pltpu.CompilerParams(vmem_limit_bytes=56 * MIB),
        cost_estimate=pl.CostEstimate(
            flops=12 * rows * D * FF, bytes_accessed=30 * MIB, transcendentals=0
        ),
        name="feed",
    )(place, *[expand] * (2 * chips), *[shrink] * chips, own, other, c, c_other)


def back_kernel(n, inner, place_ref, *refs):
    qkv_parts = refs[: n * inner]
    out_parts = refs[n * inner : (n + 2) * inner]
    refs = refs[(n + 2) * inner :]
    (
        h_ref,
        attended_ref,
        total_ref,
        q_ref,
        k_ref,
        v_ref,
        raw_ref,
        cos_ref,
        sin_ref,
        seg_col_ref,
        seg_row_ref,
        gain_q_ref,
        gain_k_ref,
    ) = refs[:13]
    grad_ref, share_ref, gains_ref, qkv, out, key_sum, value_sum, share_sum = refs[13:]
    block = q_ref.shape[0]
    heads = k_ref.shape[1] // HEAD_SIZE
    half, step = pl.program_id(0), pl.program_id(1)

    @pl.when((half == 0) & (step == 0))
    def _():
        gains_ref[...] = jnp.zeros_like(gains_ref)

    @pl.when(step == 0)
    def _():
        assemble(qkv_parts, qkv, all_rows(place_ref, n, inner))
        rows = out_parts[0].shape[0]
        size = out.shape[0] // rows
        for part, spot in zip(out_parts, chip_rows(place_ref, inner)):

            @pl.when(spot // size == half)
            def _():
                out[pl.ds(pl.multiple_of((spot % size) * rows, rows), rows), :] = part[...]

        key_sum[...] = jnp.zeros_like(key_sum)
        value_sum[...] = jnp.zeros_like(value_sum)

    def work(j):
        size = (j + 1) * block
        grad_attended = dot_nt(h_ref[...], out[...]).astype(LOW)
        attended = attended_ref[...]
        totals = total_ref[...].T
        same = seg_col_ref[:size, :] == seg_row_ref[:, j * block : size]
        key = lax.broadcasted_iota(jnp.int32, (size, block), 0)
        own = lax.broadcasted_iota(jnp.int32, (size, block), 1) + j * block
        allowed = same & (own >= key)
        allowed = jnp.concatenate([allowed] * GROUP, axis=1)
        cos, sin = cos_ref[...], sin_ref[...]
        gains = gains_ref[...]
        kind = lax.broadcasted_iota(jnp.int32, gains.shape, 0)

        def head_back(grad, values, gain):
            grad = grad * cos + pltpu.roll(grad * sin, HEAD_SIZE // 2, 1)
            grad, gain_part = norm_back(values.astype(FULL), gain, grad)
            return grad.astype(LOW), jnp.sum(gain_part, axis=0, keepdims=True)

        query_grads, key_grads, value_grads = [], [], []
        for h in range(heads):
            lanes = slice(h * HEAD_SIZE, (h + 1) * HEAD_SIZE)
            k, v = k_ref[:size, lanes], v_ref[:size, lanes]
            head_lanes = [
                slice((h * GROUP + g) * HEAD_SIZE, (h * GROUP + g + 1) * HEAD_SIZE)
                for g in range(GROUP)
            ]
            q = jnp.concatenate([q_ref[:, s] for s in head_lanes], axis=0)
            up = jnp.concatenate([grad_attended[:, s] for s in head_lanes], axis=0)
            seen = jnp.concatenate([attended[:, s] for s in head_lanes], axis=0)
            log_total = jnp.concatenate(
                [totals[h * GROUP + g : h * GROUP + g + 1, :] for g in range(GROUP)], axis=1
            )
            row = jnp.sum(up.astype(FULL) * seen.astype(FULL), axis=1, keepdims=True)
            row = jnp.broadcast_to(row, (GROUP * block, HEAD_SIZE)).T[:1, :]
            probs = jnp.where(allowed, jnp.exp2(dot_nt(k, q) * EXP_SCALE - log_total), 0.0)
            grad_probs = dot_nt(v, up)
            grad_scores = (probs * (grad_probs - row)).astype(LOW)
            value_sum[:size, lanes] += dot_nn(probs.astype(LOW), up)
            key_sum[:size, lanes] += dot_nn(grad_scores, q)
            query_grad = dot_tn(grad_scores, k) * SCALE
            for g in range(GROUP):
                grad, gain_part = head_back(
                    query_grad[g * block : (g + 1) * block], raw_ref[:, head_lanes[g]], gain_q_ref[...]
                )
                query_grads.append(grad)
                gains = jnp.where(kind == 0, gains + gain_part, gains)
        own_rows = slice(j * block, size)
        for h in range(heads):
            lanes = slice(h * HEAD_SIZE, (h + 1) * HEAD_SIZE)
            first = (heads * GROUP + h) * HEAD_SIZE
            grad, gain_part = head_back(
                key_sum[own_rows, lanes] * SCALE, raw_ref[:, first : first + HEAD_SIZE], gain_k_ref[...]
            )
            key_grads.append(grad)
            gains = jnp.where(kind == 1, gains + gain_part, gains)
            value_grads.append(value_sum[own_rows, lanes].astype(LOW))
        gains_ref[...] = gains
        grad = jnp.concatenate(query_grads + key_grads + value_grads, axis=1)
        grad_ref[...] = grad
        share = dot_nt(grad, qkv[...])

        @pl.when(half == 0)
        def _():
            share_sum[j] = share

        @pl.when((half > 0) & (half < HALVES - 1))
        def _():
            share_sum[j] += share

        @pl.when(half == HALVES - 1)
        def _():
            share_ref[...] = (share_sum[j] + share).astype(LOW)

    for j in range(n):
        pl.when(step == n - 1 - j)(functools.partial(work, j))


def back(
    place, qkv_parts, out_parts, hidden_grad, attended, totals, q, k, v, raw, cos, sin, seg_col,
    seg_row, gain_q, gain_k,
):
    inner = len(out_parts) // 2
    n = len(qkv_parts) // inner
    length = q.shape[0]
    q_width, k_width = q.shape[1] // HALVES, k.shape[1] // HALVES
    block = length // n
    width = q_width + 2 * k_width
    whole = lambda h, i, p: (0, 0)
    natural = lambda h, i, p: (n - 1 - i, 0)
    slot = lambda h, i, p: (p[0] ^ (n - 1 - i), 0)
    last_slot = lambda h, i, p: (p[0] ^ (n - 1 - jnp.where(h == HALVES - 1, i, 0)), 0)
    of_half = lambda h, i, p: (0, h)
    natural_half = lambda h, i, p: (n - 1 - i, h)
    slot_half = lambda h, i, p: (p[0] ^ (n - 1 - i), h)
    return pl.pallas_call(
        functools.partial(back_kernel, n, inner),
        out_shape=(
            jax.ShapeDtypeStruct((length, HALVES * width), LOW),
            jax.ShapeDtypeStruct((length, D), LOW),
            jax.ShapeDtypeStruct((8, HEAD_SIZE), FULL),
        ),
        grid_spec=pltpu.PrefetchScalarGridSpec(
            num_scalar_prefetch=1,
            grid=(HALVES, n),
            in_specs=[pl.BlockSpec((p.shape[0], width), of_half) for p in qkv_parts]
            + [resident(p.shape) for p in out_parts]
            + [
                pl.BlockSpec((block, D), slot),
                pl.BlockSpec((block, q_width), slot_half),
                pl.BlockSpec((block, HEAD_SIZE), slot_half),
                pl.BlockSpec((block, q_width), natural_half),
                pl.BlockSpec((length, k_width), of_half),
                pl.BlockSpec((length, k_width), of_half),
                pl.BlockSpec((block, q_width + k_width), natural_half),
                pl.BlockSpec((block, HEAD_SIZE), natural),
                pl.BlockSpec((block, HEAD_SIZE), natural),
                pl.BlockSpec((length, 1), whole),
                pl.BlockSpec((1, length), whole),
                pl.BlockSpec((1, HEAD_SIZE), whole),
                pl.BlockSpec((1, HEAD_SIZE), whole),
            ],
            out_specs=(
                pl.BlockSpec((block, width), natural_half),
                pl.BlockSpec((block, D), last_slot),
                pl.BlockSpec((8, HEAD_SIZE), whole),
            ),
            scratch_shapes=[
                pltpu.VMEM((D, width), LOW),
                pltpu.VMEM((q_width, D), LOW),
                pltpu.VMEM((length, k_width), FULL),
                pltpu.VMEM((length, k_width), FULL),
                pltpu.VMEM((n, block, D), FULL),
            ],
        ),
        compiler_params=pltpu.CompilerParams(vmem_limit_bytes=56 * MIB),
        cost_estimate=pl.CostEstimate(
            flops=2 * length * D * (q_width + width) + 5 * length * length * q_width,
            bytes_accessed=30 * MIB,
            transcendentals=0,
        ),
        name="back",
    )(
        place, *qkv_parts, *out_parts, hidden_grad, attended, totals, q, k, v, raw, cos, sin,
        seg_col, seg_row, gain_q, gain_k,
    )


def adam_kernel(rate, key_ref, *refs):
    cuts = refs[:-7]
    weight_ref, first_ref, second_ref, new_first, new_second, new_weight, grad = refs[-7:]
    for s, cut in enumerate(cuts):

        @pl.when((pl.program_id(1) ^ key_ref[0]) == s)
        def _():
            grad[...] = cut[...].astype(FULL)

    results = adam_step(weight_ref[...], first_ref[...], second_ref[...], grad[...], rate)
    new_first[...], new_second[...], new_weight[...] = results


def adam_cuts(key, cuts, weight, first, second, rate, size, column):
    rows, columns = cuts[0].shape
    cut = pl.BlockSpec((rows, size), lambda i, s, p: (0, i))
    spec = pl.BlockSpec((rows, size), lambda i, s, p: (0, column(i, s)))
    shape = jax.ShapeDtypeStruct(weight.shape, FULL)
    return pl.pallas_call(
        functools.partial(adam_kernel, rate),
        out_shape=(shape, shape, shape),
        grid_spec=pltpu.PrefetchScalarGridSpec(
            num_scalar_prefetch=1,
            grid=(columns // size, len(cuts)),
            in_specs=[cut] * len(cuts) + [spec] * 3,
            out_specs=(spec,) * 3,
            scratch_shapes=[pltpu.VMEM((rows, size), FULL)],
        ),
        cost_estimate=pl.CostEstimate(
            flops=20 * weight.size, bytes_accessed=26 * weight.size, transcendentals=weight.size
        ),
        compiler_params=pltpu.CompilerParams(vmem_limit_bytes=24 * MIB),
        name="adam_cuts",
    )(key, *cuts, weight, first, second)


def adam_pair_kernel(rate, place_ref, own_ref, other_ref, weight_ref, first_ref, second_ref, *outs):
    mine = pl.program_id(1) == (place_ref[0] & 1)
    grad = jnp.where(mine, own_ref[...].astype(FULL), other_ref[...].astype(FULL))
    results = adam_step(weight_ref[...], first_ref[...], second_ref[...], grad, rate)
    outs[0][...], outs[1][...], outs[2][...] = results


def adam_pair(place, own, other, weight, first, second, rate, size):
    rows, width = own.shape
    cut = pl.BlockSpec((rows, size), lambda i, c, p: (0, i))
    spec = pl.BlockSpec((rows, size), lambda i, c, p: (0, 2 * i + c))
    shape = jax.ShapeDtypeStruct(weight.shape, FULL)
    return pl.pallas_call(
        functools.partial(adam_pair_kernel, rate),
        out_shape=(shape, shape, shape),
        grid_spec=pltpu.PrefetchScalarGridSpec(
            num_scalar_prefetch=1,
            grid=(width // size, 2),
            in_specs=[cut, cut] + [spec] * 3,
            out_specs=(spec,) * 3,
        ),
        cost_estimate=pl.CostEstimate(
            flops=20 * weight.size, bytes_accessed=26 * weight.size, transcendentals=weight.size
        ),
        compiler_params=pltpu.CompilerParams(vmem_limit_bytes=24 * MIB),
        name="adam_pair",
    )(place, own, other, weight, first, second)


def after(value, *others):
    return lax.optimization_barrier((value, *others))[0]


def make(n, inner, reps):
    chips = n // 2

    def swap_ctx(value, s):
        return lax.ppermute(value, "ctx", [(i, i ^ s) for i in range(n)])

    def swap_core(value):
        return swap_ctx(value, 1)

    def swap_chip(value, s):
        return swap_ctx(value, 2 * s)

    def swap_grp(value, t):
        return lax.ppermute(value, "grp", [(i, i ^ t) for i in range(inner)])

    def over_chips(value):
        return [value] + [swap_chip(value, s) for s in range(1, chips)]

    def over_grp(value):
        return [value] + [swap_grp(value, t) for t in range(1, inner)]

    def sum_of(parts):
        total = parts[0].astype(FULL)
        for part in parts[1:]:
            total = total + part.astype(FULL)
        return total

    def swap_plane(value, s, t):
        pairs = [(c * inner + g, (c ^ s) * inner + (g ^ t)) for c in range(n) for g in range(inner)]
        return lax.ppermute(value, ("ctx", "grp"), pairs)

    def pick(value, axis, index):
        return lax.dynamic_index_in_dim(value, index, axis, False)

    def on_device(
        tokens,
        segment_ids,
        positions,
        cotangent,
        qkv_weight,
        qkv_first,
        qkv_second,
        out_weight,
        out_first,
        out_second,
        expand_weight,
        expand_first,
        expand_second,
        shrink_weight,
        shrink_first,
        shrink_second,
        norm_gains,
        gains_first,
        gains_second,
    ):
        seqs, block, _ = tokens.shape
        length = n * block
        me = lax.axis_index("ctx")
        core = me & 1
        chip = me >> 1
        mine = lax.axis_index("grp")
        place = jnp.stack([me, mine]).astype(jnp.int32)
        order = me ^ jnp.arange(n)
        q_width = QUERY_FEATURES // chips
        k_width = KEY_FEATURES // chips
        width = q_width + 2 * k_width
        rows = qkv_weight.shape[0]

        rep = lax.axis_index("rep")

        def qkv_piece(s):
            to = chip ^ s
            parts = []
            for i in range(HALVES):
                for first, size in ((0, q_width), (QUERY_FEATURES, k_width), (QUERY_FEATURES + KEY_FEATURES, k_width)):
                    start = first + to * size + i * (size // HALVES)
                    parts.append(lax.dynamic_slice_in_dim(qkv_weight, start, size // HALVES, 1))
            return jnp.concatenate(parts, axis=1).astype(LOW)

        small = jnp.concatenate(
            [
                segment_ids.reshape(-1).astype(FULL),
                positions.reshape(-1).astype(FULL),
                norm_gains.astype(LOW).astype(FULL),
            ]
        ).reshape(1, -1)
        small = [
            swap_plane(small, s, t) if s or t else small for s in range(n) for t in range(inner)
        ]
        tokens, qkv_low, other_tokens, *small = lax.optimization_barrier(
            (tokens, [qkv_piece(s) for s in range(chips)], pick(tokens, 0, core ^ 1), *small)
        )
        small = jnp.stack(small)
        small = small.reshape(n, inner, -1)[order]
        notes = small[:, 0, : 2 * seqs * block].reshape(n, 2, seqs, block)
        notes = pick(notes, 2, core)
        notes = jnp.moveaxis(notes, 0, 1).reshape(2, length)
        gains = small[:, mine ^ jnp.arange(inner), 2 * seqs * block :].reshape(1, -1)
        gain_one, gain_two = gains[:, :D], gains[:, D : 2 * D]
        gain_query = gains[:, 2 * D : 2 * D + HEAD_SIZE]
        gain_key = gains[:, 2 * D + HEAD_SIZE :]

        token_slots = [pick(tokens, 0, core), swap_core(other_tokens)]
        for s in range(1, chips):
            token_slots += [swap_chip(part, s) for part in token_slots[:2]]

        landed = [qkv_low[0]] + [swap_chip(qkv_low[s], s) for s in range(1, chips)]
        qkv_parts = []
        for part in landed:
            near = over_grp(part)
            qkv_parts += near + [swap_core(p) for p in near]

        near = over_grp(out_weight.astype(LOW))
        out_parts = near + [swap_core(p) for p in near]
        def gather_all(weight):
            return lax.all_gather(weight.astype(LOW), ("ctx", "grp"), axis=0, tiled=True)

        expand_full = gather_all(expand_weight)
        shrink_full = gather_all(shrink_weight)
        other_cotangent = swap_core(cotangent)

        ladder = jnp.arange(HEAD_SIZE) % (HEAD_SIZE // 2)
        frequency = jnp.exp(ladder.astype(FULL) * (-2.0 * math.log(ROPE_BASE) / HEAD_SIZE))
        angles = notes[1][:, None] * frequency[None, :]
        sign = jnp.where(jnp.arange(HEAD_SIZE) < HEAD_SIZE // 2, -1.0, 1.0)
        cos, sin = jnp.cos(angles), jnp.sin(angles) * sign
        seg_col, seg_row = notes[0][:, None], notes[0][None, :]

        normed, q, k, v, raw = project(
            place, qkv_parts, token_slots, gain_one, gain_query, gain_key, cos, sin
        )
        base, shares = None, []
        for s in range(chips - 1, -1, -1):
            *base, share = attend(place, out_parts, q, k, v, seg_col, seg_row, n, s, base)
            shares.append(swap_chip(share, s) if s else share)
        attended, totals = base
        inputs = jnp.concatenate(token_slots[:2]).astype(FULL)
        hidden = inputs + sum_of(shares)
        normed_two = (hidden * inverse_rms(hidden) * gain_two).astype(LOW)

        x_all, c_all, active, grad_gate_up, share, share_other, back_share, back_other = feed(
            place, n, expand_full, shrink_full, normed_two, swap_core(normed_two), cotangent,
            other_cotangent,
        )
        normed_grad = sum_of([back_share, swap_core(back_other)])
        hidden_grad, gain_part = norm_back(hidden, gain_two, normed_grad)
        gain_two_grad = jnp.sum(gain_part, axis=0)
        hidden_grad = hidden_grad + c_all[: 2 * block].astype(FULL)
        hidden_low = hidden_grad.astype(LOW)
        grad_slots = over_chips(hidden_low)

        def by_sequence(kept, landed):
            return jnp.where(core == 0, jnp.stack([kept, landed]), jnp.stack([landed, kept]))

        output = (hidden + sum_of([share, swap_core(share_other)])).astype(LOW)
        output = by_sequence(output[:block], swap_core(output[block:]))

        line = []

        def next_sum(kept, sent):
            if line:
                sent = lax.optimization_barrier((*sent, *line))[: len(sent)]
            total = sum_of([kept, *sent]).astype(LOW)
            line[:] = [total]
            return total

        def next_cut(kept, sent, axis, place, count):
            sent = lax.optimization_barrier((*sent, *line))[: len(sent)]
            pieces = [
                sum_of([pick(value, axis, place ^ s) for value in (kept, *sent)]).astype(LOW)
                for s in range(count)
            ]
            line[:] = pieces
            return pieces

        def send_x(parts):
            return parts[0], [swap_chip(parts[s], s) for s in range(1, chips)]

        def send_y(parts):
            return parts[0], [swap_grp(parts[t], t) for t in range(1, inner)]

        def cut_qkv(grad):
            grad_qkv = dot_tn(normed, grad).astype(LOW)
            cuts = grad_qkv.reshape(chips, 2, inner, rows, width)
            return pick(cuts, 1, core), [swap_core(pick(cuts, 1, core ^ 1))]

        x_late, active_late = lax.optimization_barrier((x_all, active, hidden_low))[:2]
        grad_expand = dot_tn(x_late, grad_gate_up).astype(LOW)
        expand_cuts = grad_expand.reshape(chips, 2, inner, rows, FF)
        other_rows = pick(expand_cuts, 1, core ^ 1)
        other_sent = [swap_grp(pick(other_rows, 1, mine ^ t), t) for t in range(1, inner)]
        grad_shrink = dot_tn(active_late, c_all).astype(LOW)
        shrink_cuts = grad_shrink.reshape(chips, inner, FF // (n * inner), D)
        shrink_sent = [swap_grp(pick(shrink_cuts, 1, mine ^ t), t) for t in range(1, inner)]
        own_rows = pick(expand_cuts, 1, core)
        late_rows = after(own_rows, grad_slots[-1])
        own_sent = [swap_chip(pick(late_rows, 0, chip ^ s), s) for s in range(1, chips)]
        grad_slots = lax.optimization_barrier((*grad_slots, grad_shrink))[:-1]
        grad_all = jnp.concatenate(grad_slots)
        grad, back_all, head_gains = back(
            place, qkv_parts, out_parts, grad_all, attended, totals, q, k, v, raw, cos, sin, seg_col,
            seg_row, gain_query, gain_key,
        )

        line[:] = [head_gains]
        own_cut = send_y(next_cut(pick(own_rows, 0, chip), own_sent, 0, mine, inner))
        other_cut = send_x(next_cut(pick(other_rows, 1, mine), other_sent, 0, chip, chips))
        qkv_cuts, qkv_sent = cut_qkv(after(grad, *line))
        shrink_cut = send_x(next_cut(pick(shrink_cuts, 1, mine), shrink_sent, 0, chip, chips))
        grad_out = dot_tn(after(attended, *line), grad_all).astype(LOW)
        out_cuts = grad_out.reshape(2, inner, out_weight.shape[0], D)
        out_sent = [swap_core(pick(out_cuts, 0, core ^ 1))]
        qkv_cut = send_y(next_cut(qkv_cuts, qkv_sent, 1, mine, inner))
        other_cut = swap_core(next_sum(*other_cut))
        out_cut = send_y(next_cut(pick(out_cuts, 0, core), out_sent, 0, mine, inner))
        own_cut = next_sum(*own_cut)
        own_cut, other_cut = lax.optimization_barrier((own_cut, other_cut, *line))[:2]
        line[:] = [other_cut]
        own_cut, other_cut = lax.psum((own_cut, other_cut), "rep")
        shrink_cut = next_sum(*shrink_cut)
        kept, sent = send_x(next_cut(*qkv_cut, 0, chip, chips))
        shares = []
        for s in range(1, chips):
            share = after(back_all[2 * s * block : 2 * (s + 1) * block], kept)
            shares.append(swap_chip(share, s))
        out_cut = next_sum(*out_cut)
        *qkv_cuts, shrink_cut, out_cut, own_cut, other_cut = lax.optimization_barrier(
            (kept, *sent, shrink_cut, out_cut, own_cut, other_cut, *line)
        )[: 4 + chips]
        total_shrink, total_out, *qkv_cuts = lax.psum((shrink_cut, out_cut, *qkv_cuts), "rep")

        shares = [back_all[: 2 * block]] + [after(value, *line) for value in shares]
        input_part, gain_part = norm_back(inputs, gain_one, sum_of(shares))
        gain_one_grad = jnp.sum(gain_part, axis=0)
        input_grad = (input_part + hidden_grad).astype(LOW)
        input_landed = swap_core(input_grad[block:])
        grad_gains = jnp.concatenate([gain_one_grad, gain_two_grad, head_gains[0], head_gains[1]])
        grad_gains = grad_gains.reshape(n, inner, 1, -1)
        gains_of = lambda s, t: pick(pick(grad_gains, 0, me ^ s), 0, mine ^ t)
        gains_sent = [
            swap_plane(gains_of(s, t), s, t) for s in range(n) for t in range(inner) if s or t
        ]
        gains_sent = lax.optimization_barrier(tuple(gains_sent))
        total_gains = sum_of([gains_of(0, 0), *gains_sent])
        gains_sent = [
            lax.ppermute(total_gains, "rep", [(i, i ^ r) for i in range(reps)]) for r in range(1, reps)
        ]
        total_gains = sum_of([total_gains, *lax.optimization_barrier(tuple(gains_sent))])[0]
        input_grad = by_sequence(input_grad[:block], input_landed)

        size = k_width // HALVES

        def qkv_column(i, s):
            q_blocks = q_width // HALVES // size
            half, i = i // (q_blocks + 2), i % (q_blocks + 2)
            q_place = (s * HALVES + half) * q_blocks + i
            k_place = QUERY_FEATURES // size + s * HALVES + half
            v_place = k_place + KEY_FEATURES // size
            return jnp.where(i < q_blocks, q_place, jnp.where(i == q_blocks, k_place, v_place))

        key = chip.reshape(1).astype(jnp.int32)
        return (
            output,
            input_grad,
            *adam_cuts(
                key, qkv_cuts, qkv_weight, qkv_first, qkv_second, RATE_QKV, size, qkv_column
            ),
            *adam_step(out_weight, out_first, out_second, total_out.astype(FULL), RATE_OUT),
            *adam_pair(
                place, own_cut, other_cut, expand_weight, expand_first, expand_second, RATE_EXPAND,
                FF // n,
            ),
            *adam_step(
                shrink_weight, shrink_first, shrink_second, total_shrink.astype(FULL), RATE_SHRINK
            ),
            *adam_step(norm_gains, gains_first, gains_second, total_gains, RATE_GAINS),
        )

    return on_device


def solution(mesh):
    token_rows = P(("grp", "rep"), "ctx", None)
    token_notes = P(("grp", "rep"), "ctx")
    weight_rows = P(("ctx", "grp"), None)
    gain_rows = P(("ctx", "grp"))
    states = (weight_rows,) * 12 + (gain_rows,) * 3
    return jax.shard_map(
        make(mesh.shape["ctx"], mesh.shape["grp"], mesh.shape["rep"]),
        mesh=mesh,
        in_specs=(token_rows, token_notes, token_notes, token_rows) + states,
        out_specs=(token_rows, token_rows) + states,
        check_vma=False,
    )
```

```python
import functools
import math

import jax
import jax.numpy as jnp
from jax import lax
from jax.experimental import pallas as pl
from jax.experimental.pallas import tpu as pltpu
from jax.sharding import PartitionSpec as P

D = 1024
QUERY_HEADS = 16
KEY_VALUE_HEADS = 8
HEAD_SIZE = 128
FF = 3072
STEP = 10
QUERY_FEATURES = 2048
KEY_FEATURES = 1024
GROUP = QUERY_HEADS // KEY_VALUE_HEADS

EPS_NORM = 1e-06
ROPE_BASE = 1000000.0
MASKED_SCORE = -1e30
BETA_ONE = 0.9
BETA_TWO = 0.95
ADAM_EPS = 1e-08
WEIGHT_DECAY = 0.1
RATE_QKV = 0.1
RATE_OUT = 0.5
RATE_EXPAND = 0.1
RATE_SHRINK = 0.06
RATE_GAINS = 0.6

SCALE = HEAD_SIZE**-0.5
EXP_SCALE = SCALE * math.log2(math.e)
LOW = jnp.bfloat16
FULL = jnp.float32
MIB = 1 << 20
HALVES = 2


def dot_nn(a, b):
    return jnp.dot(a, b, preferred_element_type=FULL)


def dot_nt(a, b):
    return lax.dot_general(a, b, (((1,), (1,)), ((), ())), preferred_element_type=FULL)


def dot_tn(a, b):
    return lax.dot_general(a, b, (((0,), (0,)), ((), ())), preferred_element_type=FULL)


def inverse_rms(values):
    return lax.rsqrt(jnp.mean(values * values, axis=-1, keepdims=True) + EPS_NORM)


def norm_back(values, gain, incoming):
    scale = inverse_rms(values)
    normed = values * scale
    scaled = incoming * gain
    grad = scale * (scaled - normed * jnp.mean(scaled * normed, axis=-1, keepdims=True))
    return grad, incoming * normed


def adam_step(weight, first_moment, second_moment, gradient, step_rate):
    first_moment = BETA_ONE * first_moment + (1.0 - BETA_ONE) * gradient
    second_moment = BETA_TWO * second_moment + (1.0 - BETA_TWO) * gradient * gradient
    fix_one = 1.0 - BETA_ONE**STEP
    fix_two = 1.0 - BETA_TWO**STEP
    step_dir = first_moment / fix_one / (jnp.sqrt(second_moment / fix_two) + ADAM_EPS)
    return (first_moment, second_moment, weight - step_rate * (step_dir + WEIGHT_DECAY * weight))


def assemble(parts, whole, blocks):
    rows = whole.shape[0] // len(parts)
    for part, block in zip(parts, blocks):
        whole[pl.ds(pl.multiple_of(block * rows, rows), rows), :] = part[...]


def all_rows(place_ref, n, inner):
    return [(place_ref[0] ^ s) * inner + (place_ref[1] ^ t) for s in range(n) for t in range(inner)]


def chip_rows(place_ref, inner):
    return [
        ((place_ref[0] & 1) ^ k) * inner + (place_ref[1] ^ t) for k in range(2) for t in range(inner)
    ]


ANYWHERE = pl.BlockSpec(memory_space=pl.ANY)


def resident(shape, column=0):
    return pl.BlockSpec(shape, lambda *_: (0, column), pipeline_mode=pl.Buffered(1))


def project_kernel(n, inner, place_ref, *refs):
    parts = refs[: n * inner]
    pieces = refs[n * inner : n * inner + n]
    gain_ref, gain_q_ref, gain_k_ref, cos_ref, sin_ref = refs[n * inner + n : n * inner + n + 5]
    normed_ref, q_ref, k_ref, v_ref, raw_ref = refs[n * inner + n + 5 : n * inner + n + 10]
    weight, token = refs[n * inner + n + 10 :]
    step = pl.program_id(0)

    @pl.when(step == 0)
    def _():
        assemble(parts, weight, all_rows(place_ref, n, inner))

    for s in range(n):

        @pl.when((place_ref[0] ^ step) == s)
        def _():
            token[...] = pieces[s][...]

    x = token[...].astype(FULL)
    normed = (x * inverse_rms(x) * gain_ref[...]).astype(LOW)
    normed_ref[...] = normed
    projected = dot_nn(normed, weight[...])
    q_half, k_half = q_ref.shape[1] // HALVES, k_ref.shape[1] // HALVES
    raw_half = q_half + k_half
    half = raw_half + k_half
    cos, sin = cos_ref[...], sin_ref[...]

    def turn(values, gain):
        values = values * inverse_rms(values) * gain
        return (values * cos + pltpu.roll(values, HEAD_SIZE // 2, 1) * sin).astype(LOW)

    for i in range(HALVES):
        first = i * half
        raw_ref[:, i * raw_half : (i + 1) * raw_half] = projected[:, first : first + raw_half].astype(LOW)
        v_ref[:, i * k_half : (i + 1) * k_half] = projected[:, first + raw_half : first + half].astype(LOW)
        for h in range(0, q_half, HEAD_SIZE):
            values = projected[:, first + h : first + h + HEAD_SIZE]
            q_ref[:, i * q_half + h : i * q_half + h + HEAD_SIZE] = turn(values, gain_q_ref[...])
        for h in range(0, k_half, HEAD_SIZE):
            values = projected[:, first + q_half + h : first + q_half + h + HEAD_SIZE]
            k_ref[:, i * k_half + h : i * k_half + h + HEAD_SIZE] = turn(values, gain_k_ref[...])


def project(place, parts, pieces, gain, gain_q, gain_k, cos, sin):
    n = len(pieces)
    inner = len(parts) // n
    block = pieces[0].shape[0]
    length = n * block
    width = parts[0].shape[1]
    q_width, k_width = width // 2, width // 4
    whole = lambda j, p: (0, 0)
    natural = lambda j, p: (j, 0)
    return pl.pallas_call(
        functools.partial(project_kernel, n, inner),
        out_shape=(
            jax.ShapeDtypeStruct((length, D), LOW),
            jax.ShapeDtypeStruct((length, q_width), LOW),
            jax.ShapeDtypeStruct((length, k_width), LOW),
            jax.ShapeDtypeStruct((length, k_width), LOW),
            jax.ShapeDtypeStruct((length, q_width + k_width), LOW),
        ),
        grid_spec=pltpu.PrefetchScalarGridSpec(
            num_scalar_prefetch=1,
            grid=(n,),
            in_specs=[resident(p.shape) for p in parts]
            + [resident((block, D))] * n
            + [
                pl.BlockSpec((1, D), whole),
                pl.BlockSpec((1, HEAD_SIZE), whole),
                pl.BlockSpec((1, HEAD_SIZE), whole),
                pl.BlockSpec((block, HEAD_SIZE), natural),
                pl.BlockSpec((block, HEAD_SIZE), natural),
            ],
            out_specs=(
                pl.BlockSpec((block, D), natural),
                pl.BlockSpec((block, q_width), natural),
                pl.BlockSpec((block, k_width), natural),
                pl.BlockSpec((block, k_width), natural),
                pl.BlockSpec((block, q_width + k_width), natural),
            ),
            scratch_shapes=[
                pltpu.VMEM((D, width), LOW),
                pltpu.VMEM((block, D), LOW),
            ],
        ),
        compiler_params=pltpu.CompilerParams(vmem_limit_bytes=40 * MIB),
        cost_estimate=pl.CostEstimate(
            flops=2 * length * D * width, bytes_accessed=16 * MIB, transcendentals=0
        ),
        name="project",
    )(place, *parts, *pieces, gain, gain_q, gain_k, cos, sin)


def attend_kernel(n, inner, first, has_base, place_ref, *refs):
    parts = refs[: 2 * inner]
    q_ref, k_ref, v_ref, seg_col_ref, seg_row_ref = refs[2 * inner : 2 * inner + 5]
    rest = refs[2 * inner + 5 + (2 if has_base else 0) :]
    attended_ref, total_ref, share_ref, weight = rest
    block = q_ref.shape[0]
    heads = k_ref.shape[1] // HEAD_SIZE
    step = pl.program_id(0)

    @pl.when(step == 0)
    def _():
        assemble(parts, weight, chip_rows(place_ref, inner))

    def work(j):
        size = (j + 1) * block
        same = seg_col_ref[...] == seg_row_ref[:, :size]
        own = lax.broadcasted_iota(jnp.int32, (block, size), 0) + j * block
        key = lax.broadcasted_iota(jnp.int32, (block, size), 1)
        allowed = same & (own >= key)
        allowed = jnp.concatenate([allowed] * GROUP, axis=0)
        outs, totals = [], []
        for h in range(heads):
            lanes = slice(h * HEAD_SIZE, (h + 1) * HEAD_SIZE)
            q = jnp.concatenate(
                [
                    q_ref[:, (h * GROUP + g) * HEAD_SIZE : (h * GROUP + g + 1) * HEAD_SIZE]
                    for g in range(GROUP)
                ],
                axis=0,
            )
            scores = jnp.where(allowed, dot_nt(q, k_ref[:size, lanes]), MASKED_SCORE)
            top = jnp.max(scores, axis=-1, keepdims=True)
            weights = jnp.exp2((scores - top) * EXP_SCALE)
            total = jnp.sum(weights, axis=-1, keepdims=True)
            out = dot_nn(weights.astype(LOW), v_ref[:size, lanes]) / total
            log_total = top * EXP_SCALE + jnp.log2(total)
            for g in range(GROUP):
                outs.append(out[g * block : (g + 1) * block].astype(LOW))
                totals.append(log_total[g * block : (g + 1) * block])
        attended = jnp.concatenate(outs, axis=1)
        attended_ref[...] = attended
        share_ref[...] = dot_nn(attended, weight[...]).astype(LOW)
        lane = lax.broadcasted_iota(jnp.int32, (block, HEAD_SIZE), 1)
        count = len(totals) // HALVES
        for half in range(HALVES):
            packed = jnp.zeros((block, HEAD_SIZE), FULL)
            for i, column in enumerate(totals[half * count : (half + 1) * count]):
                packed = jnp.where(lane == i, column, packed)
            total_ref[:, half * HEAD_SIZE : (half + 1) * HEAD_SIZE] = packed

    place = place_ref[0] ^ (first + step)
    for j in range(n):
        pl.when(place == j)(functools.partial(work, j))


def attend(place, parts, q, k, v, seg_col, seg_row, n, chip, base):
    inner = len(parts) // 2
    length, q_width = q.shape
    k_width = k.shape[1]
    block = length // n
    first = 2 * chip
    whole = lambda i, p: (0, 0)
    natural = lambda i, p: (p[0] ^ (first + i), 0)
    slot = lambda i, p: (first + i, 0)
    plain = lambda i, p: (i, 0)
    base = list(base or ())
    before = 1 + len(parts) + 5
    return pl.pallas_call(
        functools.partial(attend_kernel, n, inner, first, bool(base)),
        out_shape=(
            jax.ShapeDtypeStruct((length, q_width), LOW),
            jax.ShapeDtypeStruct((length, HALVES * HEAD_SIZE), FULL),
            jax.ShapeDtypeStruct((2 * block, D), LOW),
        ),
        grid_spec=pltpu.PrefetchScalarGridSpec(
            num_scalar_prefetch=1,
            grid=(2,),
            in_specs=[resident(p.shape) for p in parts]
            + [
                pl.BlockSpec((block, q_width), natural),
                resident((length, k_width)),
                resident((length, k_width)),
                pl.BlockSpec((block, 1), natural),
                pl.BlockSpec((1, length), whole),
            ]
            + [ANYWHERE] * len(base),
            out_specs=(
                pl.BlockSpec((block, q_width), slot),
                pl.BlockSpec((block, HALVES * HEAD_SIZE), slot),
                pl.BlockSpec((block, D), plain),
            ),
            scratch_shapes=[pltpu.VMEM((q_width, D), LOW)],
        ),
        input_output_aliases={before: 0, before + 1: 1} if base else {},
        compiler_params=pltpu.CompilerParams(vmem_limit_bytes=48 * MIB),
        cost_estimate=pl.CostEstimate(
            flops=4 * block * q_width * (D + 2 * length), bytes_accessed=8 * MIB, transcendentals=0
        ),
        name="attend",
    )(place, *parts, q, k, v, seg_col, seg_row, *base)


def feed_kernel(chips, place_ref, *refs):
    gates, ups, shrinks = refs[:chips], refs[chips : 2 * chips], refs[2 * chips : 3 * chips]
    own_ref, other_ref, c_ref, c_other_ref = refs[3 * chips : 3 * chips + 4]
    refs = refs[3 * chips + 4 :]
    x_out, c_out, active_ref, grad_ref, share_ref, share_other, back_ref, back_other, expand, shrink = refs
    step = pl.program_id(0)
    mine = step < 2
    x = jnp.where(mine, own_ref[...], other_ref[...])
    c = jnp.where((step == 0) | (step == 3), c_ref[0], c_other_ref[0])
    x_out[...] = x
    c_out[...] = c
    size = gates[0].shape[1]
    half = chips * size

    @pl.when(step == 0)
    def _():
        for s in range(chips):
            here = slice(s * size, (s + 1) * size)
            expand[:, here] = gates[s][...]
            expand[:, half + s * size : half + (s + 1) * size] = ups[s][...]
            shrink[here, :] = shrinks[s][...]

    gate_up = dot_nn(x, expand[...])
    grad_active = dot_nt(c, shrink[...]).astype(LOW).astype(FULL)
    gate, up = gate_up[:, :half], gate_up[:, half:]
    gated = jax.nn.sigmoid(gate)
    silu = gate * gated
    active = (silu * up).astype(LOW)
    active_ref[...] = active
    grad_gate = (grad_active * up * gated * (1.0 + gate * (1.0 - gated))).astype(LOW)
    grad_up = (grad_active * silu).astype(LOW)
    grad = jnp.concatenate([grad_gate, grad_up], axis=1)
    grad_ref[...] = grad
    share = dot_nn(active, shrink[...]).astype(LOW)
    back = dot_nt(grad, expand[...]).astype(LOW)

    @pl.when(mine)
    def _():
        share_ref[...] = share
        back_ref[...] = back

    @pl.when(jnp.logical_not(mine))
    def _():
        share_other[...] = share
        back_other[...] = back


def feed(place, n, expand, shrink, own, other, c, c_other):
    chips = n // 2
    rows = own.shape[0]
    size = FF // n
    near = lambda i, p: (jnp.minimum(i, 1), 0)
    far = lambda i, p: (jnp.maximum(i - 2, 0), 0)
    flat = lambda i, p: (i, 0)
    core = lambda i, p: ((p[0] & 1) ^ (i // 2), 0, 0)
    block = rows // 2
    once = pl.Buffered(1)
    gates = [
        pl.BlockSpec((D, size), lambda i, p, s=s: (0, 2 * s + (p[0] & 1)), pipeline_mode=once)
        for s in range(chips)
    ]
    ups = [
        pl.BlockSpec((D, size), lambda i, p, s=s: (0, n + 2 * s + (p[0] & 1)), pipeline_mode=once)
        for s in range(chips)
    ]
    shrinks = [
        pl.BlockSpec((size, D), lambda i, p, s=s: (2 * s + (p[0] & 1), 0), pipeline_mode=once)
        for s in range(chips)
    ]
    wide = lambda w: jax.ShapeDtypeStruct((2 * rows, w), LOW)
    part = jax.ShapeDtypeStruct((rows, D), LOW)
    return pl.pallas_call(
        functools.partial(feed_kernel, chips),
        out_shape=(wide(D), wide(D), wide(FF // 2), wide(FF), part, part, part, part),
        grid_spec=pltpu.PrefetchScalarGridSpec(
            num_scalar_prefetch=1,
            grid=(4,),
            in_specs=gates
            + ups
            + shrinks
            + [
                pl.BlockSpec((block, D), near),
                pl.BlockSpec((block, D), far),
                pl.BlockSpec((1, block, D), core),
                pl.BlockSpec((1, block, D), core),
            ],
            out_specs=(
                pl.BlockSpec((block, D), flat),
                pl.BlockSpec((block, D), flat),
                pl.BlockSpec((block, FF // 2), flat),
                pl.BlockSpec((block, FF), flat),
                pl.BlockSpec((block, D), near),
                pl.BlockSpec((block, D), far),
                pl.BlockSpec((block, D), near),
                pl.BlockSpec((block, D), far),
            ),
            scratch_shapes=[pltpu.VMEM((D, FF), LOW), pltpu.VMEM((FF // 2, D), LOW)],
        ),
        compiler_params=pltpu.CompilerParams(vmem_limit_bytes=56 * MIB),
        cost_estimate=pl.CostEstimate(
            flops=12 * rows * D * FF, bytes_accessed=30 * MIB, transcendentals=0
        ),
        name="feed",
    )(place, *[expand] * (2 * chips), *[shrink] * chips, own, other, c, c_other)


def back_kernel(n, inner, place_ref, *refs):
    qkv_parts = refs[: n * inner]
    out_parts = refs[n * inner : (n + 2) * inner]
    refs = refs[(n + 2) * inner :]
    (
        h_ref,
        attended_ref,
        total_ref,
        q_ref,
        k_ref,
        v_ref,
        raw_ref,
        cos_ref,
        sin_ref,
        seg_col_ref,
        seg_row_ref,
        gain_q_ref,
        gain_k_ref,
    ) = refs[:13]
    grad_ref, share_ref, gains_ref, qkv, out, key_sum, value_sum, share_sum = refs[13:]
    block = q_ref.shape[0]
    heads = k_ref.shape[1] // HEAD_SIZE
    half, step = pl.program_id(0), pl.program_id(1)

    @pl.when((half == 0) & (step == 0))
    def _():
        gains_ref[...] = jnp.zeros_like(gains_ref)

    @pl.when(step == 0)
    def _():
        assemble(qkv_parts, qkv, all_rows(place_ref, n, inner))
        rows = out_parts[0].shape[0]
        size = out.shape[0] // rows
        for part, spot in zip(out_parts, chip_rows(place_ref, inner)):

            @pl.when(spot // size == half)
            def _():
                out[pl.ds(pl.multiple_of((spot % size) * rows, rows), rows), :] = part[...]

        key_sum[...] = jnp.zeros_like(key_sum)
        value_sum[...] = jnp.zeros_like(value_sum)

    def work(j):
        size = (j + 1) * block
        grad_attended = dot_nt(h_ref[...], out[...]).astype(LOW)
        attended = attended_ref[...]
        totals = total_ref[...].T
        same = seg_col_ref[:size, :] == seg_row_ref[:, j * block : size]
        key = lax.broadcasted_iota(jnp.int32, (size, block), 0)
        own = lax.broadcasted_iota(jnp.int32, (size, block), 1) + j * block
        allowed = same & (own >= key)
        allowed = jnp.concatenate([allowed] * GROUP, axis=1)
        cos, sin = cos_ref[...], sin_ref[...]
        gains = gains_ref[...]
        kind = lax.broadcasted_iota(jnp.int32, gains.shape, 0)

        def head_back(grad, values, gain):
            grad = grad * cos + pltpu.roll(grad * sin, HEAD_SIZE // 2, 1)
            grad, gain_part = norm_back(values.astype(FULL), gain, grad)
            return grad.astype(LOW), jnp.sum(gain_part, axis=0, keepdims=True)

        query_grads, key_grads, value_grads = [], [], []
        for h in range(heads):
            lanes = slice(h * HEAD_SIZE, (h + 1) * HEAD_SIZE)
            k, v = k_ref[:size, lanes], v_ref[:size, lanes]
            head_lanes = [
                slice((h * GROUP + g) * HEAD_SIZE, (h * GROUP + g + 1) * HEAD_SIZE)
                for g in range(GROUP)
            ]
            q = jnp.concatenate([q_ref[:, s] for s in head_lanes], axis=0)
            up = jnp.concatenate([grad_attended[:, s] for s in head_lanes], axis=0)
            seen = jnp.concatenate([attended[:, s] for s in head_lanes], axis=0)
            log_total = jnp.concatenate(
                [totals[h * GROUP + g : h * GROUP + g + 1, :] for g in range(GROUP)], axis=1
            )
            row = jnp.sum(up.astype(FULL) * seen.astype(FULL), axis=1, keepdims=True)
            row = jnp.broadcast_to(row, (GROUP * block, HEAD_SIZE)).T[:1, :]
            probs = jnp.where(allowed, jnp.exp2(dot_nt(k, q) * EXP_SCALE - log_total), 0.0)
            grad_probs = dot_nt(v, up)
            grad_scores = (probs * (grad_probs - row)).astype(LOW)
            value_sum[:size, lanes] += dot_nn(probs.astype(LOW), up)
            key_sum[:size, lanes] += dot_nn(grad_scores, q)
            query_grad = dot_tn(grad_scores, k) * SCALE
            for g in range(GROUP):
                grad, gain_part = head_back(
                    query_grad[g * block : (g + 1) * block], raw_ref[:, head_lanes[g]], gain_q_ref[...]
                )
                query_grads.append(grad)
                gains = jnp.where(kind == 0, gains + gain_part, gains)
        own_rows = slice(j * block, size)
        for h in range(heads):
            lanes = slice(h * HEAD_SIZE, (h + 1) * HEAD_SIZE)
            first = (heads * GROUP + h) * HEAD_SIZE
            grad, gain_part = head_back(
                key_sum[own_rows, lanes] * SCALE, raw_ref[:, first : first + HEAD_SIZE], gain_k_ref[...]
            )
            key_grads.append(grad)
            gains = jnp.where(kind == 1, gains + gain_part, gains)
            value_grads.append(value_sum[own_rows, lanes].astype(LOW))
        gains_ref[...] = gains
        grad = jnp.concatenate(query_grads + key_grads + value_grads, axis=1)
        grad_ref[...] = grad
        share = dot_nt(grad, qkv[...])

        @pl.when(half == 0)
        def _():
            share_sum[j] = share

        @pl.when((half > 0) & (half < HALVES - 1))
        def _():
            share_sum[j] += share

        @pl.when(half == HALVES - 1)
        def _():
            share_ref[...] = (share_sum[j] + share).astype(LOW)

    for j in range(n):
        pl.when(step == n - 1 - j)(functools.partial(work, j))


def back(
    place, qkv_parts, out_parts, hidden_grad, attended, totals, q, k, v, raw, cos, sin, seg_col,
    seg_row, gain_q, gain_k,
):
    inner = len(out_parts) // 2
    n = len(qkv_parts) // inner
    length = q.shape[0]
    q_width, k_width = q.shape[1] // HALVES, k.shape[1] // HALVES
    block = length // n
    width = q_width + 2 * k_width
    whole = lambda h, i, p: (0, 0)
    natural = lambda h, i, p: (n - 1 - i, 0)
    slot = lambda h, i, p: (p[0] ^ (n - 1 - i), 0)
    last_slot = lambda h, i, p: (p[0] ^ (n - 1 - jnp.where(h == HALVES - 1, i, 0)), 0)
    of_half = lambda h, i, p: (0, h)
    natural_half = lambda h, i, p: (n - 1 - i, h)
    slot_half = lambda h, i, p: (p[0] ^ (n - 1 - i), h)
    return pl.pallas_call(
        functools.partial(back_kernel, n, inner),
        out_shape=(
            jax.ShapeDtypeStruct((length, HALVES * width), LOW),
            jax.ShapeDtypeStruct((length, D), LOW),
            jax.ShapeDtypeStruct((8, HEAD_SIZE), FULL),
        ),
        grid_spec=pltpu.PrefetchScalarGridSpec(
            num_scalar_prefetch=1,
            grid=(HALVES, n),
            in_specs=[pl.BlockSpec((p.shape[0], width), of_half) for p in qkv_parts]
            + [resident(p.shape) for p in out_parts]
            + [
                pl.BlockSpec((block, D), slot),
                pl.BlockSpec((block, q_width), slot_half),
                pl.BlockSpec((block, HEAD_SIZE), slot_half),
                pl.BlockSpec((block, q_width), natural_half),
                pl.BlockSpec((length, k_width), of_half),
                pl.BlockSpec((length, k_width), of_half),
                pl.BlockSpec((block, q_width + k_width), natural_half),
                pl.BlockSpec((block, HEAD_SIZE), natural),
                pl.BlockSpec((block, HEAD_SIZE), natural),
                pl.BlockSpec((length, 1), whole),
                pl.BlockSpec((1, length), whole),
                pl.BlockSpec((1, HEAD_SIZE), whole),
                pl.BlockSpec((1, HEAD_SIZE), whole),
            ],
            out_specs=(
                pl.BlockSpec((block, width), natural_half),
                pl.BlockSpec((block, D), last_slot),
                pl.BlockSpec((8, HEAD_SIZE), whole),
            ),
            scratch_shapes=[
                pltpu.VMEM((D, width), LOW),
                pltpu.VMEM((q_width, D), LOW),
                pltpu.VMEM((length, k_width), FULL),
                pltpu.VMEM((length, k_width), FULL),
                pltpu.VMEM((n, block, D), FULL),
            ],
        ),
        compiler_params=pltpu.CompilerParams(vmem_limit_bytes=56 * MIB),
        cost_estimate=pl.CostEstimate(
            flops=2 * length * D * (q_width + width) + 5 * length * length * q_width,
            bytes_accessed=30 * MIB,
            transcendentals=0,
        ),
        name="back",
    )(
        place, *qkv_parts, *out_parts, hidden_grad, attended, totals, q, k, v, raw, cos, sin,
        seg_col, seg_row, gain_q, gain_k,
    )


def adam_kernel(rate, key_ref, *refs):
    cuts = refs[:-7]
    weight_ref, first_ref, second_ref, new_first, new_second, new_weight, grad = refs[-7:]
    for s, cut in enumerate(cuts):

        @pl.when((pl.program_id(1) ^ key_ref[0]) == s)
        def _():
            grad[...] = cut[...].astype(FULL)

    results = adam_step(weight_ref[...], first_ref[...], second_ref[...], grad[...], rate)
    new_first[...], new_second[...], new_weight[...] = results


def adam_cuts(key, cuts, weight, first, second, rate, size, column):
    rows, columns = cuts[0].shape
    cut = pl.BlockSpec((rows, size), lambda i, s, p: (0, i))
    spec = pl.BlockSpec((rows, size), lambda i, s, p: (0, column(i, s)))
    shape = jax.ShapeDtypeStruct(weight.shape, FULL)
    return pl.pallas_call(
        functools.partial(adam_kernel, rate),
        out_shape=(shape, shape, shape),
        grid_spec=pltpu.PrefetchScalarGridSpec(
            num_scalar_prefetch=1,
            grid=(columns // size, len(cuts)),
            in_specs=[cut] * len(cuts) + [spec] * 3,
            out_specs=(spec,) * 3,
            scratch_shapes=[pltpu.VMEM((rows, size), FULL)],
        ),
        cost_estimate=pl.CostEstimate(
            flops=20 * weight.size, bytes_accessed=26 * weight.size, transcendentals=weight.size
        ),
        compiler_params=pltpu.CompilerParams(vmem_limit_bytes=24 * MIB),
        name="adam_cuts",
    )(key, *cuts, weight, first, second)


def adam_pair_kernel(rate, place_ref, own_ref, other_ref, weight_ref, first_ref, second_ref, *outs):
    mine = pl.program_id(1) == (place_ref[0] & 1)
    grad = jnp.where(mine, own_ref[...].astype(FULL), other_ref[...].astype(FULL))
    results = adam_step(weight_ref[...], first_ref[...], second_ref[...], grad, rate)
    outs[0][...], outs[1][...], outs[2][...] = results


def adam_pair(place, own, other, weight, first, second, rate, size):
    rows, width = own.shape
    cut = pl.BlockSpec((rows, size), lambda i, c, p: (0, i))
    spec = pl.BlockSpec((rows, size), lambda i, c, p: (0, 2 * i + c))
    shape = jax.ShapeDtypeStruct(weight.shape, FULL)
    return pl.pallas_call(
        functools.partial(adam_pair_kernel, rate),
        out_shape=(shape, shape, shape),
        grid_spec=pltpu.PrefetchScalarGridSpec(
            num_scalar_prefetch=1,
            grid=(width // size, 2),
            in_specs=[cut, cut] + [spec] * 3,
            out_specs=(spec,) * 3,
        ),
        cost_estimate=pl.CostEstimate(
            flops=20 * weight.size, bytes_accessed=26 * weight.size, transcendentals=weight.size
        ),
        compiler_params=pltpu.CompilerParams(vmem_limit_bytes=24 * MIB),
        name="adam_pair",
    )(place, own, other, weight, first, second)


def after(value, *others):
    return lax.optimization_barrier((value, *others))[0]


def make(n, inner, reps):
    chips = n // 2

    def swap_ctx(value, s):
        return lax.ppermute(value, "ctx", [(i, i ^ s) for i in range(n)])

    def swap_core(value):
        return swap_ctx(value, 1)

    def swap_chip(value, s):
        return swap_ctx(value, 2 * s)

    def swap_grp(value, t):
        return lax.ppermute(value, "grp", [(i, i ^ t) for i in range(inner)])

    def over_chips(value):
        return [value] + [swap_chip(value, s) for s in range(1, chips)]

    def over_grp(value):
        return [value] + [swap_grp(value, t) for t in range(1, inner)]

    def sum_of(parts):
        total = parts[0].astype(FULL)
        for part in parts[1:]:
            total = total + part.astype(FULL)
        return total

    def swap_plane(value, s, t):
        pairs = [(c * inner + g, (c ^ s) * inner + (g ^ t)) for c in range(n) for g in range(inner)]
        return lax.ppermute(value, ("ctx", "grp"), pairs)

    def pick(value, axis, index):
        return lax.dynamic_index_in_dim(value, index, axis, False)

    def on_device(
        tokens,
        segment_ids,
        positions,
        cotangent,
        qkv_weight,
        qkv_first,
        qkv_second,
        out_weight,
        out_first,
        out_second,
        expand_weight,
        expand_first,
        expand_second,
        shrink_weight,
        shrink_first,
        shrink_second,
        norm_gains,
        gains_first,
        gains_second,
    ):
        seqs, block, _ = tokens.shape
        length = n * block
        me = lax.axis_index("ctx")
        core = me & 1
        chip = me >> 1
        mine = lax.axis_index("grp")
        place = jnp.stack([me, mine]).astype(jnp.int32)
        order = me ^ jnp.arange(n)
        q_width = QUERY_FEATURES // chips
        k_width = KEY_FEATURES // chips
        width = q_width + 2 * k_width
        rows = qkv_weight.shape[0]

        rep = lax.axis_index("rep")

        def qkv_piece(s):
            to = chip ^ s
            parts = []
            for i in range(HALVES):
                for first, size in ((0, q_width), (QUERY_FEATURES, k_width), (QUERY_FEATURES + KEY_FEATURES, k_width)):
                    start = first + to * size + i * (size // HALVES)
                    parts.append(lax.dynamic_slice_in_dim(qkv_weight, start, size // HALVES, 1))
            return jnp.concatenate(parts, axis=1).astype(LOW)

        small = jnp.concatenate(
            [
                segment_ids.reshape(-1).astype(FULL),
                positions.reshape(-1).astype(FULL),
                norm_gains.astype(LOW).astype(FULL),
            ]
        ).reshape(1, -1)
        small = [
            swap_plane(small, s, t) if s or t else small for s in range(n) for t in range(inner)
        ]
        tokens, qkv_low, other_tokens, *small = lax.optimization_barrier(
            (tokens, [qkv_piece(s) for s in range(chips)], pick(tokens, 0, core ^ 1), *small)
        )
        small = jnp.stack(small)
        small = small.reshape(n, inner, -1)[order]
        notes = small[:, 0, : 2 * seqs * block].reshape(n, 2, seqs, block)
        notes = pick(notes, 2, core)
        notes = jnp.moveaxis(notes, 0, 1).reshape(2, length)
        gains = small[:, mine ^ jnp.arange(inner), 2 * seqs * block :].reshape(1, -1)
        gain_one, gain_two = gains[:, :D], gains[:, D : 2 * D]
        gain_query = gains[:, 2 * D : 2 * D + HEAD_SIZE]
        gain_key = gains[:, 2 * D + HEAD_SIZE :]

        token_slots = [pick(tokens, 0, core), swap_core(other_tokens)]
        for s in range(1, chips):
            token_slots += [swap_chip(part, s) for part in token_slots[:2]]

        landed = [qkv_low[0]] + [swap_chip(qkv_low[s], s) for s in range(1, chips)]
        qkv_parts = []
        for part in landed:
            near = over_grp(part)
            qkv_parts += near + [swap_core(p) for p in near]

        near = over_grp(out_weight.astype(LOW))
        out_parts = near + [swap_core(p) for p in near]
        def gather_all(weight):
            return lax.all_gather(weight.astype(LOW), ("ctx", "grp"), axis=0, tiled=True)

        expand_full = gather_all(expand_weight)
        shrink_full = gather_all(shrink_weight)
        other_cotangent = swap_core(cotangent)

        ladder = jnp.arange(HEAD_SIZE) % (HEAD_SIZE // 2)
        frequency = jnp.exp(ladder.astype(FULL) * (-2.0 * math.log(ROPE_BASE) / HEAD_SIZE))
        angles = notes[1][:, None] * frequency[None, :]
        sign = jnp.where(jnp.arange(HEAD_SIZE) < HEAD_SIZE // 2, -1.0, 1.0)
        cos, sin = jnp.cos(angles), jnp.sin(angles) * sign
        seg_col, seg_row = notes[0][:, None], notes[0][None, :]

        normed, q, k, v, raw = project(
            place, qkv_parts, token_slots, gain_one, gain_query, gain_key, cos, sin
        )
        base, shares = None, []
        for s in range(chips - 1, -1, -1):
            *base, share = attend(place, out_parts, q, k, v, seg_col, seg_row, n, s, base)
            shares.append(swap_chip(share, s) if s else share)
        attended, totals = base
        inputs = jnp.concatenate(token_slots[:2]).astype(FULL)
        hidden = inputs + sum_of(shares)
        normed_two = (hidden * inverse_rms(hidden) * gain_two).astype(LOW)

        x_all, c_all, active, grad_gate_up, share, share_other, back_share, back_other = feed(
            place, n, expand_full, shrink_full, normed_two, swap_core(normed_two), cotangent,
            other_cotangent,
        )
        grad_shrink = dot_tn(active, c_all).astype(LOW)
        shrink_cuts = grad_shrink.reshape(chips, inner, FF // (n * inner), D)
        shrink_sent = [swap_grp(pick(shrink_cuts, 1, mine ^ t), t) for t in range(1, inner)]
        normed_grad = sum_of([after(back_share, grad_shrink), swap_core(back_other)])
        hidden_grad, gain_part = norm_back(hidden, gain_two, normed_grad)
        gain_two_grad = jnp.sum(gain_part, axis=0)
        hidden_grad = hidden_grad + c_all[: 2 * block].astype(FULL)
        hidden_low = hidden_grad.astype(LOW)
        grad_slots = over_chips(hidden_low)

        def by_sequence(kept, landed):
            return jnp.where(core == 0, jnp.stack([kept, landed]), jnp.stack([landed, kept]))

        output = (hidden + sum_of([share, swap_core(share_other)])).astype(LOW)
        output = by_sequence(output[:block], swap_core(output[block:]))

        line = []

        def next_sum(kept, sent):
            if line:
                sent = lax.optimization_barrier((*sent, *line))[: len(sent)]
            total = sum_of([kept, *sent]).astype(LOW)
            line[:] = [total]
            return total

        def next_cut(kept, sent, axis, place, count):
            sent = lax.optimization_barrier((*sent, *line))[: len(sent)]
            pieces = [
                sum_of([pick(value, axis, place ^ s) for value in (kept, *sent)]).astype(LOW)
                for s in range(count)
            ]
            line[:] = pieces
            return pieces

        def send_x(parts):
            return parts[0], [swap_chip(parts[s], s) for s in range(1, chips)]

        def send_y(parts):
            return parts[0], [swap_grp(parts[t], t) for t in range(1, inner)]

        def cut_qkv(grad):
            grad_qkv = dot_tn(normed, grad).astype(LOW)
            cuts = grad_qkv.reshape(chips, 2, inner, rows, width)
            return pick(cuts, 1, core), [swap_core(pick(cuts, 1, core ^ 1))]

        grad_expand = dot_tn(after(x_all, hidden_low), grad_gate_up).astype(LOW)
        expand_cuts = grad_expand.reshape(chips, 2, inner, rows, FF)
        other_rows = pick(expand_cuts, 1, core ^ 1)
        other_sent = [swap_grp(pick(other_rows, 1, mine ^ t), t) for t in range(1, inner)]
        own_rows = pick(expand_cuts, 1, core)
        late_rows = after(own_rows, grad_slots[-1])
        own_sent = [swap_chip(pick(late_rows, 0, chip ^ s), s) for s in range(1, chips)]
        line[:] = [grad_expand]
        shrink_cut = send_x(next_cut(pick(shrink_cuts, 1, mine), shrink_sent, 0, chip, chips))
        grad_slots = lax.optimization_barrier((*grad_slots, *line))[:chips]
        grad_all = jnp.concatenate(grad_slots)
        grad, back_all, head_gains = back(
            place, qkv_parts, out_parts, grad_all, attended, totals, q, k, v, raw, cos, sin, seg_col,
            seg_row, gain_query, gain_key,
        )

        line[:] = [head_gains]
        shrink_cut = next_sum(*shrink_cut)
        total_shrink = lax.psum(shrink_cut, "rep")
        own_cut = send_y(next_cut(pick(own_rows, 0, chip), own_sent, 0, mine, inner))
        other_cut = send_x(next_cut(pick(other_rows, 1, mine), other_sent, 0, chip, chips))
        grad_out = dot_tn(after(attended, *line), grad_all).astype(LOW)
        out_cuts = grad_out.reshape(2, inner, out_weight.shape[0], D)
        out_sent = [swap_core(pick(out_cuts, 0, core ^ 1))]
        line[:] = [grad_out]
        qkv_cuts, qkv_sent = cut_qkv(after(grad, *line))
        out_cut = send_y(next_cut(pick(out_cuts, 0, core), out_sent, 0, mine, inner))
        qkv_cut = send_y(next_cut(qkv_cuts, qkv_sent, 1, mine, inner))
        own_cut = next_sum(*own_cut)
        other_cut = swap_core(next_sum(*other_cut))
        out_cut = next_sum(*out_cut)
        own_cut, other_cut, out_cut, total_shrink = lax.optimization_barrier(
            (own_cut, other_cut, out_cut, total_shrink, *line)
        )[:4]
        line[:] = [out_cut]
        own_cut, other_cut, total_out = lax.psum((own_cut, other_cut, out_cut), "rep")
        kept, sent = send_x(next_cut(*qkv_cut, 0, chip, chips))
        shares = []
        for s in range(1, chips):
            share = after(back_all[2 * s * block : 2 * (s + 1) * block], kept)
            shares.append(swap_chip(share, s))
        *qkv_cuts, own_cut, other_cut, total_out = lax.optimization_barrier(
            (kept, *sent, own_cut, other_cut, total_out, *line)
        )[: 3 + chips]
        qkv_cuts = lax.psum(tuple(qkv_cuts), "rep")

        shares = [back_all[: 2 * block]] + [after(value, *line) for value in shares]
        input_part, gain_part = norm_back(inputs, gain_one, sum_of(shares))
        gain_one_grad = jnp.sum(gain_part, axis=0)
        input_grad = (input_part + hidden_grad).astype(LOW)
        input_landed = swap_core(input_grad[block:])
        grad_gains = jnp.concatenate([gain_one_grad, gain_two_grad, head_gains[0], head_gains[1]])
        grad_gains = grad_gains.reshape(n, inner, 1, -1)
        gains_of = lambda s, t: pick(pick(grad_gains, 0, me ^ s), 0, mine ^ t)
        gains_sent = [
            swap_plane(gains_of(s, t), s, t) for s in range(n) for t in range(inner) if s or t
        ]
        gains_sent = lax.optimization_barrier(tuple(gains_sent))
        total_gains = sum_of([gains_of(0, 0), *gains_sent])
        gains_sent = [
            lax.ppermute(total_gains, "rep", [(i, i ^ r) for i in range(reps)]) for r in range(1, reps)
        ]
        total_gains = sum_of([total_gains, *lax.optimization_barrier(tuple(gains_sent))])[0]
        input_grad = by_sequence(input_grad[:block], input_landed)

        size = k_width // HALVES

        def qkv_column(i, s):
            q_blocks = q_width // HALVES // size
            half, i = i // (q_blocks + 2), i % (q_blocks + 2)
            q_place = (s * HALVES + half) * q_blocks + i
            k_place = QUERY_FEATURES // size + s * HALVES + half
            v_place = k_place + KEY_FEATURES // size
            return jnp.where(i < q_blocks, q_place, jnp.where(i == q_blocks, k_place, v_place))

        key = chip.reshape(1).astype(jnp.int32)
        return (
            output,
            input_grad,
            *adam_cuts(
                key, qkv_cuts, qkv_weight, qkv_first, qkv_second, RATE_QKV, size, qkv_column
            ),
            *adam_step(out_weight, out_first, out_second, total_out.astype(FULL), RATE_OUT),
            *adam_pair(
                place, own_cut, other_cut, expand_weight, expand_first, expand_second, RATE_EXPAND,
                FF // n,
            ),
            *adam_step(
                shrink_weight, shrink_first, shrink_second, total_shrink.astype(FULL), RATE_SHRINK
            ),
            *adam_step(norm_gains, gains_first, gains_second, total_gains, RATE_GAINS),
        )

    return on_device


def solution(mesh):
    token_rows = P(("grp", "rep"), "ctx", None)
    token_notes = P(("grp", "rep"), "ctx")
    weight_rows = P(("ctx", "grp"), None)
    gain_rows = P(("ctx", "grp"))
    states = (weight_rows,) * 12 + (gain_rows,) * 3
    return jax.shard_map(
        make(mesh.shape["ctx"], mesh.shape["grp"], mesh.shape["rep"]),
        mesh=mesh,
        in_specs=(token_rows, token_notes, token_notes, token_rows) + states,
        out_specs=(token_rows, token_rows) + states,
        check_vma=False,
    )
```

```python
import functools
import math

import jax
import jax.numpy as jnp
from jax import lax
from jax.experimental import pallas as pl
from jax.experimental.pallas import tpu as pltpu
from jax.sharding import PartitionSpec as P

D = 1024
QUERY_HEADS = 16
KEY_VALUE_HEADS = 8
HEAD_SIZE = 128
FF = 3072
STEP = 10
QUERY_FEATURES = 2048
KEY_FEATURES = 1024
GROUP = QUERY_HEADS // KEY_VALUE_HEADS

EPS_NORM = 1e-06
ROPE_BASE = 1000000.0
MASKED_SCORE = -1e30
BETA_ONE = 0.9
BETA_TWO = 0.95
ADAM_EPS = 1e-08
WEIGHT_DECAY = 0.1
RATE_QKV = 0.1
RATE_OUT = 0.5
RATE_EXPAND = 0.1
RATE_SHRINK = 0.06
RATE_GAINS = 0.6

SCALE = HEAD_SIZE**-0.5
EXP_SCALE = SCALE * math.log2(math.e)
LOW = jnp.bfloat16
FULL = jnp.float32
MIB = 1 << 20
HALVES = 2


def dot_nn(a, b):
    return jnp.dot(a, b, preferred_element_type=FULL)


def dot_nt(a, b):
    return lax.dot_general(a, b, (((1,), (1,)), ((), ())), preferred_element_type=FULL)


def dot_tn(a, b):
    return lax.dot_general(a, b, (((0,), (0,)), ((), ())), preferred_element_type=FULL)


def inverse_rms(values):
    return lax.rsqrt(jnp.mean(values * values, axis=-1, keepdims=True) + EPS_NORM)


def norm_back(values, gain, incoming):
    scale = inverse_rms(values)
    normed = values * scale
    scaled = incoming * gain
    grad = scale * (scaled - normed * jnp.mean(scaled * normed, axis=-1, keepdims=True))
    return grad, incoming * normed


def adam_step(weight, first_moment, second_moment, gradient, step_rate):
    first_moment = BETA_ONE * first_moment + (1.0 - BETA_ONE) * gradient
    second_moment = BETA_TWO * second_moment + (1.0 - BETA_TWO) * gradient * gradient
    fix_one = 1.0 - BETA_ONE**STEP
    fix_two = 1.0 - BETA_TWO**STEP
    step_dir = first_moment / fix_one / (jnp.sqrt(second_moment / fix_two) + ADAM_EPS)
    return (first_moment, second_moment, weight - step_rate * (step_dir + WEIGHT_DECAY * weight))


def assemble(parts, whole, blocks):
    rows = whole.shape[0] // len(parts)
    for part, block in zip(parts, blocks):
        whole[pl.ds(pl.multiple_of(block * rows, rows), rows), :] = part[...]


def all_rows(place_ref, n, inner):
    return [(place_ref[0] ^ s) * inner + (place_ref[1] ^ t) for s in range(n) for t in range(inner)]


def chip_rows(place_ref, inner):
    return [
        ((place_ref[0] & 1) ^ k) * inner + (place_ref[1] ^ t) for k in range(2) for t in range(inner)
    ]


ANYWHERE = pl.BlockSpec(memory_space=pl.ANY)


def resident(shape, column=0):
    return pl.BlockSpec(shape, lambda *_: (0, column), pipeline_mode=pl.Buffered(1))


def project_kernel(n, inner, place_ref, *refs):
    parts = refs[: n * inner]
    pieces = refs[n * inner : n * inner + n]
    gain_ref, gain_q_ref, gain_k_ref, cos_ref, sin_ref = refs[n * inner + n : n * inner + n + 5]
    normed_ref, q_ref, k_ref, v_ref, raw_ref = refs[n * inner + n + 5 : n * inner + n + 10]
    weight, token = refs[n * inner + n + 10 :]
    step = pl.program_id(0)

    @pl.when(step == 0)
    def _():
        assemble(parts, weight, all_rows(place_ref, n, inner))

    for s in range(n):

        @pl.when((place_ref[0] ^ step) == s)
        def _():
            token[...] = pieces[s][...]

    x = token[...].astype(FULL)
    normed = (x * inverse_rms(x) * gain_ref[...]).astype(LOW)
    normed_ref[...] = normed
    projected = dot_nn(normed, weight[...])
    q_half, k_half = q_ref.shape[1] // HALVES, k_ref.shape[1] // HALVES
    raw_half = q_half + k_half
    half = raw_half + k_half
    cos, sin = cos_ref[...], sin_ref[...]

    def turn(values, gain):
        values = values * inverse_rms(values) * gain
        return (values * cos + pltpu.roll(values, HEAD_SIZE // 2, 1) * sin).astype(LOW)

    for i in range(HALVES):
        first = i * half
        raw_ref[:, i * raw_half : (i + 1) * raw_half] = projected[:, first : first + raw_half].astype(LOW)
        v_ref[:, i * k_half : (i + 1) * k_half] = projected[:, first + raw_half : first + half].astype(LOW)
        for h in range(0, q_half, HEAD_SIZE):
            values = projected[:, first + h : first + h + HEAD_SIZE]
            q_ref[:, i * q_half + h : i * q_half + h + HEAD_SIZE] = turn(values, gain_q_ref[...])
        for h in range(0, k_half, HEAD_SIZE):
            values = projected[:, first + q_half + h : first + q_half + h + HEAD_SIZE]
            k_ref[:, i * k_half + h : i * k_half + h + HEAD_SIZE] = turn(values, gain_k_ref[...])


def project(place, parts, pieces, gain, gain_q, gain_k, cos, sin):
    n = len(pieces)
    inner = len(parts) // n
    block = pieces[0].shape[0]
    length = n * block
    width = parts[0].shape[1]
    q_width, k_width = width // 2, width // 4
    whole = lambda j, p: (0, 0)
    natural = lambda j, p: (j, 0)
    return pl.pallas_call(
        functools.partial(project_kernel, n, inner),
        out_shape=(
            jax.ShapeDtypeStruct((length, D), LOW),
            jax.ShapeDtypeStruct((length, q_width), LOW),
            jax.ShapeDtypeStruct((length, k_width), LOW),
            jax.ShapeDtypeStruct((length, k_width), LOW),
            jax.ShapeDtypeStruct((length, q_width + k_width), LOW),
        ),
        grid_spec=pltpu.PrefetchScalarGridSpec(
            num_scalar_prefetch=1,
            grid=(n,),
            in_specs=[resident(p.shape) for p in parts]
            + [resident((block, D))] * n
            + [
                pl.BlockSpec((1, D), whole),
                pl.BlockSpec((1, HEAD_SIZE), whole),
                pl.BlockSpec((1, HEAD_SIZE), whole),
                pl.BlockSpec((block, HEAD_SIZE), natural),
                pl.BlockSpec((block, HEAD_SIZE), natural),
            ],
            out_specs=(
                pl.BlockSpec((block, D), natural),
                pl.BlockSpec((block, q_width), natural),
                pl.BlockSpec((block, k_width), natural),
                pl.BlockSpec((block, k_width), natural),
                pl.BlockSpec((block, q_width + k_width), natural),
            ),
            scratch_shapes=[
                pltpu.VMEM((D, width), LOW),
                pltpu.VMEM((block, D), LOW),
            ],
        ),
        compiler_params=pltpu.CompilerParams(vmem_limit_bytes=40 * MIB),
        cost_estimate=pl.CostEstimate(
            flops=2 * length * D * width, bytes_accessed=16 * MIB, transcendentals=0
        ),
        name="project",
    )(place, *parts, *pieces, gain, gain_q, gain_k, cos, sin)


def attend_kernel(n, inner, first, has_base, place_ref, *refs):
    parts = refs[: 2 * inner]
    q_ref, k_ref, v_ref, seg_col_ref, seg_row_ref = refs[2 * inner : 2 * inner + 5]
    rest = refs[2 * inner + 5 + (2 if has_base else 0) :]
    attended_ref, total_ref, share_ref, weight = rest
    block = q_ref.shape[0]
    heads = k_ref.shape[1] // HEAD_SIZE
    step = pl.program_id(0)

    @pl.when(step == 0)
    def _():
        assemble(parts, weight, chip_rows(place_ref, inner))

    def work(j):
        size = (j + 1) * block
        same = seg_col_ref[...] == seg_row_ref[:, :size]
        own = lax.broadcasted_iota(jnp.int32, (block, size), 0) + j * block
        key = lax.broadcasted_iota(jnp.int32, (block, size), 1)
        allowed = same & (own >= key)
        allowed = jnp.concatenate([allowed] * GROUP, axis=0)
        outs, totals = [], []
        for h in range(heads):
            lanes = slice(h * HEAD_SIZE, (h + 1) * HEAD_SIZE)
            q = jnp.concatenate(
                [
                    q_ref[:, (h * GROUP + g) * HEAD_SIZE : (h * GROUP + g + 1) * HEAD_SIZE]
                    for g in range(GROUP)
                ],
                axis=0,
            )
            scores = jnp.where(allowed, dot_nt(q, k_ref[:size, lanes]), MASKED_SCORE)
            top = jnp.max(scores, axis=-1, keepdims=True)
            weights = jnp.exp2((scores - top) * EXP_SCALE)
            total = jnp.sum(weights, axis=-1, keepdims=True)
            out = dot_nn(weights.astype(LOW), v_ref[:size, lanes]) / total
            log_total = top * EXP_SCALE + jnp.log2(total)
            for g in range(GROUP):
                outs.append(out[g * block : (g + 1) * block].astype(LOW))
                totals.append(log_total[g * block : (g + 1) * block])
        attended = jnp.concatenate(outs, axis=1)
        attended_ref[...] = attended
        share_ref[...] = dot_nn(attended, weight[...]).astype(LOW)
        lane = lax.broadcasted_iota(jnp.int32, (block, HEAD_SIZE), 1)
        count = len(totals) // HALVES
        for half in range(HALVES):
            packed = jnp.zeros((block, HEAD_SIZE), FULL)
            for i, column in enumerate(totals[half * count : (half + 1) * count]):
                packed = jnp.where(lane == i, column, packed)
            total_ref[:, half * HEAD_SIZE : (half + 1) * HEAD_SIZE] = packed

    place = place_ref[0] ^ (first + step)
    for j in range(n):
        pl.when(place == j)(functools.partial(work, j))


def attend(place, parts, q, k, v, seg_col, seg_row, n, chip, base):
    inner = len(parts) // 2
    length, q_width = q.shape
    k_width = k.shape[1]
    block = length // n
    first = 2 * chip
    whole = lambda i, p: (0, 0)
    natural = lambda i, p: (p[0] ^ (first + i), 0)
    slot = lambda i, p: (first + i, 0)
    plain = lambda i, p: (i, 0)
    base = list(base or ())
    before = 1 + len(parts) + 5
    return pl.pallas_call(
        functools.partial(attend_kernel, n, inner, first, bool(base)),
        out_shape=(
            jax.ShapeDtypeStruct((length, q_width), LOW),
            jax.ShapeDtypeStruct((length, HALVES * HEAD_SIZE), FULL),
            jax.ShapeDtypeStruct((2 * block, D), LOW),
        ),
        grid_spec=pltpu.PrefetchScalarGridSpec(
            num_scalar_prefetch=1,
            grid=(2,),
            in_specs=[resident(p.shape) for p in parts]
            + [
                pl.BlockSpec((block, q_width), natural),
                resident((length, k_width)),
                resident((length, k_width)),
                pl.BlockSpec((block, 1), natural),
                pl.BlockSpec((1, length), whole),
            ]
            + [ANYWHERE] * len(base),
            out_specs=(
                pl.BlockSpec((block, q_width), slot),
                pl.BlockSpec((block, HALVES * HEAD_SIZE), slot),
                pl.BlockSpec((block, D), plain),
            ),
            scratch_shapes=[pltpu.VMEM((q_width, D), LOW)],
        ),
        input_output_aliases={before: 0, before + 1: 1} if base else {},
        compiler_params=pltpu.CompilerParams(vmem_limit_bytes=48 * MIB),
        cost_estimate=pl.CostEstimate(
            flops=4 * block * q_width * (D + 2 * length), bytes_accessed=8 * MIB, transcendentals=0
        ),
        name="attend",
    )(place, *parts, q, k, v, seg_col, seg_row, *base)


def feed_kernel(chips, place_ref, *refs):
    gates, ups, shrinks = refs[:chips], refs[chips : 2 * chips], refs[2 * chips : 3 * chips]
    own_ref, other_ref, c_ref, c_other_ref = refs[3 * chips : 3 * chips + 4]
    refs = refs[3 * chips + 4 :]
    x_out, c_out, active_ref, grad_ref, share_ref, share_other, back_ref, back_other, expand, shrink = refs
    step = pl.program_id(0)
    mine = step < 2
    x = jnp.where(mine, own_ref[...], other_ref[...])
    c = jnp.where((step == 0) | (step == 3), c_ref[0], c_other_ref[0])
    x_out[...] = x
    c_out[...] = c
    size = gates[0].shape[1]
    half = chips * size

    @pl.when(step == 0)
    def _():
        for s in range(chips):
            here = slice(s * size, (s + 1) * size)
            expand[:, here] = gates[s][...]
            expand[:, half + s * size : half + (s + 1) * size] = ups[s][...]
            shrink[here, :] = shrinks[s][...]

    gate_up = dot_nn(x, expand[...])
    grad_active = dot_nt(c, shrink[...]).astype(LOW).astype(FULL)
    gate, up = gate_up[:, :half], gate_up[:, half:]
    gated = jax.nn.sigmoid(gate)
    silu = gate * gated
    active = (silu * up).astype(LOW)
    active_ref[...] = active
    grad_gate = (grad_active * up * gated * (1.0 + gate * (1.0 - gated))).astype(LOW)
    grad_up = (grad_active * silu).astype(LOW)
    grad = jnp.concatenate([grad_gate, grad_up], axis=1)
    grad_ref[...] = grad
    share = dot_nn(active, shrink[...]).astype(LOW)
    back = dot_nt(grad, expand[...]).astype(LOW)

    @pl.when(mine)
    def _():
        share_ref[...] = share
        back_ref[...] = back

    @pl.when(jnp.logical_not(mine))
    def _():
        share_other[...] = share
        back_other[...] = back


def feed(place, n, expand, shrink, own, other, c, c_other):
    chips = n // 2
    rows = own.shape[0]
    size = FF // n
    near = lambda i, p: (jnp.minimum(i, 1), 0)
    far = lambda i, p: (jnp.maximum(i - 2, 0), 0)
    flat = lambda i, p: (i, 0)
    core = lambda i, p: ((p[0] & 1) ^ (i // 2), 0, 0)
    block = rows // 2
    once = pl.Buffered(1)
    gates = [
        pl.BlockSpec((D, size), lambda i, p, s=s: (0, 2 * s + (p[0] & 1)), pipeline_mode=once)
        for s in range(chips)
    ]
    ups = [
        pl.BlockSpec((D, size), lambda i, p, s=s: (0, n + 2 * s + (p[0] & 1)), pipeline_mode=once)
        for s in range(chips)
    ]
    shrinks = [
        pl.BlockSpec((size, D), lambda i, p, s=s: (2 * s + (p[0] & 1), 0), pipeline_mode=once)
        for s in range(chips)
    ]
    wide = lambda w: jax.ShapeDtypeStruct((2 * rows, w), LOW)
    part = jax.ShapeDtypeStruct((rows, D), LOW)
    return pl.pallas_call(
        functools.partial(feed_kernel, chips),
        out_shape=(wide(D), wide(D), wide(FF // 2), wide(FF), part, part, part, part),
        grid_spec=pltpu.PrefetchScalarGridSpec(
            num_scalar_prefetch=1,
            grid=(4,),
            in_specs=gates
            + ups
            + shrinks
            + [
                pl.BlockSpec((block, D), near),
                pl.BlockSpec((block, D), far),
                pl.BlockSpec((1, block, D), core),
                pl.BlockSpec((1, block, D), core),
            ],
            out_specs=(
                pl.BlockSpec((block, D), flat),
                pl.BlockSpec((block, D), flat),
                pl.BlockSpec((block, FF // 2), flat),
                pl.BlockSpec((block, FF), flat),
                pl.BlockSpec((block, D), near),
                pl.BlockSpec((block, D), far),
                pl.BlockSpec((block, D), near),
                pl.BlockSpec((block, D), far),
            ),
            scratch_shapes=[pltpu.VMEM((D, FF), LOW), pltpu.VMEM((FF // 2, D), LOW)],
        ),
        compiler_params=pltpu.CompilerParams(vmem_limit_bytes=56 * MIB),
        cost_estimate=pl.CostEstimate(
            flops=12 * rows * D * FF, bytes_accessed=30 * MIB, transcendentals=0
        ),
        name="feed",
    )(place, *[expand] * (2 * chips), *[shrink] * chips, own, other, c, c_other)


def back_kernel(n, inner, half, place_ref, *refs):
    qkv_parts = refs[: n * inner]
    out_parts = refs[n * inner : (n + 2) * inner]
    refs = refs[(n + 2) * inner :]
    (
        h_ref,
        attended_ref,
        total_ref,
        q_ref,
        k_ref,
        v_ref,
        raw_ref,
        cos_ref,
        sin_ref,
        seg_col_ref,
        seg_row_ref,
        gain_q_ref,
        gain_k_ref,
    ) = refs[:13]
    refs = refs[13:]
    if half:
        base_ref, refs = refs[0], refs[2:]
    grad_ref, share_ref, gains_ref, qkv, out, key_sum, value_sum = refs
    block = q_ref.shape[0]
    heads = k_ref.shape[1] // HEAD_SIZE
    step = pl.program_id(0)

    @pl.when(step == 0)
    def _():
        assemble(qkv_parts, qkv, all_rows(place_ref, n, inner))
        rows = out_parts[0].shape[0]
        size = out.shape[0] // rows
        for part, spot in zip(out_parts, chip_rows(place_ref, inner)):

            @pl.when(spot // size == half)
            def _():
                out[pl.ds(pl.multiple_of((spot % size) * rows, rows), rows), :] = part[...]

        key_sum[...] = jnp.zeros_like(key_sum)
        value_sum[...] = jnp.zeros_like(value_sum)
        gains_ref[...] = jnp.zeros_like(gains_ref)

    def work(j):
        size = (j + 1) * block
        grad_attended = dot_nt(h_ref[...], out[...]).astype(LOW)
        attended = attended_ref[...]
        totals = total_ref[...].T
        same = seg_col_ref[:size, :] == seg_row_ref[:, j * block : size]
        key = lax.broadcasted_iota(jnp.int32, (size, block), 0)
        own = lax.broadcasted_iota(jnp.int32, (size, block), 1) + j * block
        allowed = same & (own >= key)
        allowed = jnp.concatenate([allowed] * GROUP, axis=1)
        cos, sin = cos_ref[...], sin_ref[...]
        gains = gains_ref[...]
        kind = lax.broadcasted_iota(jnp.int32, gains.shape, 0)

        def head_back(grad, values, gain):
            grad = grad * cos + pltpu.roll(grad * sin, HEAD_SIZE // 2, 1)
            grad, gain_part = norm_back(values.astype(FULL), gain, grad)
            return grad.astype(LOW), jnp.sum(gain_part, axis=0, keepdims=True)

        query_grads, key_grads, value_grads = [], [], []
        for h in range(heads):
            lanes = slice(h * HEAD_SIZE, (h + 1) * HEAD_SIZE)
            k, v = k_ref[:size, lanes], v_ref[:size, lanes]
            head_lanes = [
                slice((h * GROUP + g) * HEAD_SIZE, (h * GROUP + g + 1) * HEAD_SIZE)
                for g in range(GROUP)
            ]
            q = jnp.concatenate([q_ref[:, s] for s in head_lanes], axis=0)
            up = jnp.concatenate([grad_attended[:, s] for s in head_lanes], axis=0)
            seen = jnp.concatenate([attended[:, s] for s in head_lanes], axis=0)
            log_total = jnp.concatenate(
                [totals[h * GROUP + g : h * GROUP + g + 1, :] for g in range(GROUP)], axis=1
            )
            row = jnp.sum(up.astype(FULL) * seen.astype(FULL), axis=1, keepdims=True)
            row = jnp.broadcast_to(row, (GROUP * block, HEAD_SIZE)).T[:1, :]
            probs = jnp.where(allowed, jnp.exp2(dot_nt(k, q) * EXP_SCALE - log_total), 0.0)
            grad_probs = dot_nt(v, up)
            grad_scores = (probs * (grad_probs - row)).astype(LOW)
            value_sum[:size, lanes] += dot_nn(probs.astype(LOW), up)
            key_sum[:size, lanes] += dot_nn(grad_scores, q)
            query_grad = dot_tn(grad_scores, k) * SCALE
            for g in range(GROUP):
                grad, gain_part = head_back(
                    query_grad[g * block : (g + 1) * block], raw_ref[:, head_lanes[g]], gain_q_ref[...]
                )
                query_grads.append(grad)
                gains = jnp.where(kind == 0, gains + gain_part, gains)
        own_rows = slice(j * block, size)
        for h in range(heads):
            lanes = slice(h * HEAD_SIZE, (h + 1) * HEAD_SIZE)
            first = (heads * GROUP + h) * HEAD_SIZE
            grad, gain_part = head_back(
                key_sum[own_rows, lanes] * SCALE, raw_ref[:, first : first + HEAD_SIZE], gain_k_ref[...]
            )
            key_grads.append(grad)
            gains = jnp.where(kind == 1, gains + gain_part, gains)
            value_grads.append(value_sum[own_rows, lanes].astype(LOW))
        gains_ref[...] = gains
        grad = jnp.concatenate(query_grads + key_grads + value_grads, axis=1)
        grad_ref[...] = grad
        share = dot_nt(grad, qkv[...])

        if half:
            share = share + base_ref[...].astype(FULL)
        share_ref[...] = share.astype(LOW)

    for j in range(n):
        pl.when(step == n - 1 - j)(functools.partial(work, j))


def back(
    place, qkv_parts, out_parts, hidden_grad, attended, totals, q, k, v, raw, cos, sin, seg_col,
    seg_row, gain_q, gain_k, half, base,
):
    inner = len(out_parts) // 2
    n = len(qkv_parts) // inner
    length = q.shape[0]
    q_width, k_width = q.shape[1] // HALVES, k.shape[1] // HALVES
    block = length // n
    width = q_width + 2 * k_width
    whole = lambda i, p: (0, 0)
    natural = lambda i, p: (n - 1 - i, 0)
    slot = lambda i, p: (p[0] ^ (n - 1 - i), 0)
    natural_half = lambda i, p: (n - 1 - i, half)
    slot_half = lambda i, p: (p[0] ^ (n - 1 - i), half)
    base = list(base or ())
    before = 1 + len(qkv_parts) + len(out_parts) + 13
    return pl.pallas_call(
        functools.partial(back_kernel, n, inner, half),
        out_shape=(
            jax.ShapeDtypeStruct((length, HALVES * width), LOW),
            jax.ShapeDtypeStruct((length, D), LOW),
            jax.ShapeDtypeStruct((8, HEAD_SIZE), FULL),
        ),
        grid_spec=pltpu.PrefetchScalarGridSpec(
            num_scalar_prefetch=1,
            grid=(n,),
            in_specs=[resident((p.shape[0], width), half) for p in qkv_parts]
            + [resident(p.shape) for p in out_parts]
            + [
                pl.BlockSpec((block, D), slot),
                pl.BlockSpec((block, q_width), slot_half),
                pl.BlockSpec((block, HEAD_SIZE), slot_half),
                pl.BlockSpec((block, q_width), natural_half),
                resident((length, k_width), half),
                resident((length, k_width), half),
                pl.BlockSpec((block, q_width + k_width), natural_half),
                pl.BlockSpec((block, HEAD_SIZE), natural),
                pl.BlockSpec((block, HEAD_SIZE), natural),
                pl.BlockSpec((length, 1), whole),
                pl.BlockSpec((1, length), whole),
                pl.BlockSpec((1, HEAD_SIZE), whole),
                pl.BlockSpec((1, HEAD_SIZE), whole),
            ]
            + [pl.BlockSpec((block, D), slot), ANYWHERE][: len(base)],
            out_specs=(
                pl.BlockSpec((block, width), natural_half),
                pl.BlockSpec((block, D), slot),
                pl.BlockSpec((8, HEAD_SIZE), whole),
            ),
            scratch_shapes=[
                pltpu.VMEM((D, width), LOW),
                pltpu.VMEM((q_width, D), LOW),
                pltpu.VMEM((length, k_width), FULL),
                pltpu.VMEM((length, k_width), FULL),
            ],
        ),
        input_output_aliases={before + 1: 0} if base else {},
        compiler_params=pltpu.CompilerParams(vmem_limit_bytes=56 * MIB),
        cost_estimate=pl.CostEstimate(
            flops=2 * length * D * (q_width + width) + 5 * length * length * q_width,
            bytes_accessed=30 * MIB,
            transcendentals=0,
        ),
        name="back",
    )(
        place, *qkv_parts, *out_parts, hidden_grad, attended, totals, q, k, v, raw, cos, sin,
        seg_col, seg_row, gain_q, gain_k, *base,
    )


def adam_kernel(rate, key_ref, *refs):
    cuts = refs[:-7]
    weight_ref, first_ref, second_ref, new_first, new_second, new_weight, grad = refs[-7:]
    for s, cut in enumerate(cuts):

        @pl.when((pl.program_id(1) ^ key_ref[0]) == s)
        def _():
            grad[...] = cut[...].astype(FULL)

    results = adam_step(weight_ref[...], first_ref[...], second_ref[...], grad[...], rate)
    new_first[...], new_second[...], new_weight[...] = results


def adam_cuts(key, cuts, weight, first, second, rate, size, column):
    rows, columns = cuts[0].shape
    cut = pl.BlockSpec((rows, size), lambda i, s, p: (0, i))
    spec = pl.BlockSpec((rows, size), lambda i, s, p: (0, column(i, s)))
    shape = jax.ShapeDtypeStruct(weight.shape, FULL)
    return pl.pallas_call(
        functools.partial(adam_kernel, rate),
        out_shape=(shape, shape, shape),
        grid_spec=pltpu.PrefetchScalarGridSpec(
            num_scalar_prefetch=1,
            grid=(columns // size, len(cuts)),
            in_specs=[cut] * len(cuts) + [spec] * 3,
            out_specs=(spec,) * 3,
            scratch_shapes=[pltpu.VMEM((rows, size), FULL)],
        ),
        cost_estimate=pl.CostEstimate(
            flops=20 * weight.size, bytes_accessed=26 * weight.size, transcendentals=weight.size
        ),
        compiler_params=pltpu.CompilerParams(vmem_limit_bytes=24 * MIB),
        name="adam_cuts",
    )(key, *cuts, weight, first, second)


def adam_pair_kernel(rate, place_ref, own_ref, other_ref, weight_ref, first_ref, second_ref, *outs):
    mine = pl.program_id(1) == (place_ref[0] & 1)
    grad = jnp.where(mine, own_ref[...].astype(FULL), other_ref[...].astype(FULL))
    results = adam_step(weight_ref[...], first_ref[...], second_ref[...], grad, rate)
    outs[0][...], outs[1][...], outs[2][...] = results


def adam_pair(place, own, other, weight, first, second, rate, size):
    rows, width = own.shape
    cut = pl.BlockSpec((rows, size), lambda i, c, p: (0, i))
    spec = pl.BlockSpec((rows, size), lambda i, c, p: (0, 2 * i + c))
    shape = jax.ShapeDtypeStruct(weight.shape, FULL)
    return pl.pallas_call(
        functools.partial(adam_pair_kernel, rate),
        out_shape=(shape, shape, shape),
        grid_spec=pltpu.PrefetchScalarGridSpec(
            num_scalar_prefetch=1,
            grid=(width // size, 2),
            in_specs=[cut, cut] + [spec] * 3,
            out_specs=(spec,) * 3,
        ),
        cost_estimate=pl.CostEstimate(
            flops=20 * weight.size, bytes_accessed=26 * weight.size, transcendentals=weight.size
        ),
        compiler_params=pltpu.CompilerParams(vmem_limit_bytes=24 * MIB),
        name="adam_pair",
    )(place, own, other, weight, first, second)


def after(value, *others):
    return lax.optimization_barrier((value, *others))[0]


def make(n, inner, reps):
    chips = n // 2

    def swap_ctx(value, s):
        return lax.ppermute(value, "ctx", [(i, i ^ s) for i in range(n)])

    def swap_core(value):
        return swap_ctx(value, 1)

    def swap_chip(value, s):
        return swap_ctx(value, 2 * s)

    def swap_grp(value, t):
        return lax.ppermute(value, "grp", [(i, i ^ t) for i in range(inner)])

    def over_chips(value):
        return [value] + [swap_chip(value, s) for s in range(1, chips)]

    def over_grp(value):
        return [value] + [swap_grp(value, t) for t in range(1, inner)]

    def sum_of(parts):
        total = parts[0].astype(FULL)
        for part in parts[1:]:
            total = total + part.astype(FULL)
        return total

    def swap_plane(value, s, t):
        pairs = [(c * inner + g, (c ^ s) * inner + (g ^ t)) for c in range(n) for g in range(inner)]
        return lax.ppermute(value, ("ctx", "grp"), pairs)

    def pick(value, axis, index):
        return lax.dynamic_index_in_dim(value, index, axis, False)

    def on_device(
        tokens,
        segment_ids,
        positions,
        cotangent,
        qkv_weight,
        qkv_first,
        qkv_second,
        out_weight,
        out_first,
        out_second,
        expand_weight,
        expand_first,
        expand_second,
        shrink_weight,
        shrink_first,
        shrink_second,
        norm_gains,
        gains_first,
        gains_second,
    ):
        seqs, block, _ = tokens.shape
        length = n * block
        me = lax.axis_index("ctx")
        core = me & 1
        chip = me >> 1
        mine = lax.axis_index("grp")
        place = jnp.stack([me, mine]).astype(jnp.int32)
        order = me ^ jnp.arange(n)
        q_width = QUERY_FEATURES // chips
        k_width = KEY_FEATURES // chips
        width = q_width + 2 * k_width
        rows = qkv_weight.shape[0]

        rep = lax.axis_index("rep")

        def qkv_piece(s):
            to = chip ^ s
            parts = []
            for i in range(HALVES):
                for first, size in ((0, q_width), (QUERY_FEATURES, k_width), (QUERY_FEATURES + KEY_FEATURES, k_width)):
                    start = first + to * size + i * (size // HALVES)
                    parts.append(lax.dynamic_slice_in_dim(qkv_weight, start, size // HALVES, 1))
            return jnp.concatenate(parts, axis=1).astype(LOW)

        small = jnp.concatenate(
            [
                segment_ids.reshape(-1).astype(FULL),
                positions.reshape(-1).astype(FULL),
                norm_gains.astype(LOW).astype(FULL),
            ]
        ).reshape(1, -1)
        small = [
            swap_plane(small, s, t) if s or t else small for s in range(n) for t in range(inner)
        ]
        tokens, qkv_low, other_tokens, *small = lax.optimization_barrier(
            (tokens, [qkv_piece(s) for s in range(chips)], pick(tokens, 0, core ^ 1), *small)
        )
        small = jnp.stack(small)
        small = small.reshape(n, inner, -1)[order]
        notes = small[:, 0, : 2 * seqs * block].reshape(n, 2, seqs, block)
        notes = pick(notes, 2, core)
        notes = jnp.moveaxis(notes, 0, 1).reshape(2, length)
        gains = small[:, mine ^ jnp.arange(inner), 2 * seqs * block :].reshape(1, -1)
        gain_one, gain_two = gains[:, :D], gains[:, D : 2 * D]
        gain_query = gains[:, 2 * D : 2 * D + HEAD_SIZE]
        gain_key = gains[:, 2 * D + HEAD_SIZE :]

        token_slots = [pick(tokens, 0, core), swap_core(other_tokens)]
        for s in range(1, chips):
            token_slots += [swap_chip(part, s) for part in token_slots[:2]]

        landed = [qkv_low[0]] + [swap_chip(qkv_low[s], s) for s in range(1, chips)]
        qkv_parts = []
        for part in landed:
            near = over_grp(part)
            qkv_parts += near + [swap_core(p) for p in near]

        near = over_grp(out_weight.astype(LOW))
        out_parts = near + [swap_core(p) for p in near]
        def gather_all(weight):
            return lax.all_gather(weight.astype(LOW), ("ctx", "grp"), axis=0, tiled=True)

        expand_full = gather_all(expand_weight)
        shrink_full = gather_all(shrink_weight)
        other_cotangent = swap_core(cotangent)

        ladder = jnp.arange(HEAD_SIZE) % (HEAD_SIZE // 2)
        frequency = jnp.exp(ladder.astype(FULL) * (-2.0 * math.log(ROPE_BASE) / HEAD_SIZE))
        angles = notes[1][:, None] * frequency[None, :]
        sign = jnp.where(jnp.arange(HEAD_SIZE) < HEAD_SIZE // 2, -1.0, 1.0)
        cos, sin = jnp.cos(angles), jnp.sin(angles) * sign
        seg_col, seg_row = notes[0][:, None], notes[0][None, :]

        normed, q, k, v, raw = project(
            place, qkv_parts, token_slots, gain_one, gain_query, gain_key, cos, sin
        )
        base, shares = None, []
        for s in range(chips - 1, -1, -1):
            *base, share = attend(place, out_parts, q, k, v, seg_col, seg_row, n, s, base)
            shares.append(swap_chip(share, s) if s else share)
        attended, totals = base
        inputs = jnp.concatenate(token_slots[:2]).astype(FULL)
        hidden = inputs + sum_of(shares)
        normed_two = (hidden * inverse_rms(hidden) * gain_two).astype(LOW)

        x_all, c_all, active, grad_gate_up, share, share_other, back_share, back_other = feed(
            place, n, expand_full, shrink_full, normed_two, swap_core(normed_two), cotangent,
            other_cotangent,
        )
        grad_shrink = dot_tn(active, c_all).astype(LOW)
        shrink_cuts = grad_shrink.reshape(chips, inner, FF // (n * inner), D)
        shrink_sent = [swap_grp(pick(shrink_cuts, 1, mine ^ t), t) for t in range(1, inner)]
        normed_grad = sum_of([after(back_share, grad_shrink), swap_core(back_other)])
        hidden_grad, gain_part = norm_back(hidden, gain_two, normed_grad)
        gain_two_grad = jnp.sum(gain_part, axis=0)
        hidden_grad = hidden_grad + c_all[: 2 * block].astype(FULL)
        hidden_low = hidden_grad.astype(LOW)
        grad_slots = over_chips(hidden_low)

        def by_sequence(kept, landed):
            return jnp.where(core == 0, jnp.stack([kept, landed]), jnp.stack([landed, kept]))

        output = (hidden + sum_of([share, swap_core(share_other)])).astype(LOW)
        output = by_sequence(output[:block], swap_core(output[block:]))

        line = []

        def next_sum(kept, sent):
            if line:
                sent = lax.optimization_barrier((*sent, *line))[: len(sent)]
            total = sum_of([kept, *sent]).astype(LOW)
            line[:] = [total]
            return total

        def next_cut(kept, sent, axis, place, count):
            sent = lax.optimization_barrier((*sent, *line))[: len(sent)]
            pieces = [
                sum_of([pick(value, axis, place ^ s) for value in (kept, *sent)]).astype(LOW)
                for s in range(count)
            ]
            line[:] = pieces
            return pieces

        def send_x(parts):
            return parts[0], [swap_chip(parts[s], s) for s in range(1, chips)]

        def send_y(parts):
            return parts[0], [swap_grp(parts[t], t) for t in range(1, inner)]

        def cut_qkv(grad):
            grad_qkv = dot_tn(normed, grad).astype(LOW)
            cuts = grad_qkv.reshape(chips, 2, inner, rows, width)
            return pick(cuts, 1, core), [swap_core(pick(cuts, 1, core ^ 1))]

        grad_expand = dot_tn(after(x_all, hidden_low), grad_gate_up).astype(LOW)
        expand_cuts = grad_expand.reshape(chips, 2, inner, rows, FF)
        other_rows = pick(expand_cuts, 1, core ^ 1)
        other_sent = [swap_grp(pick(other_rows, 1, mine ^ t), t) for t in range(1, inner)]
        own_rows = pick(expand_cuts, 1, core)

        def first_over_x(t, *gates):
            cut = after(own_rows, *gates)
            sent = [swap_chip(pick(pick(cut, 0, chip ^ s), 0, mine ^ t), s) for s in range(1, chips)]
            return pick(pick(own_rows, 0, chip), 0, mine ^ t), sent

        def back_part(half, attended, base):
            return back(
                place, qkv_parts, out_parts, grad_all, attended, totals, q, k, v, raw, cos, sin, seg_col,
                seg_row, gain_query, gain_key, half, base,
            )

        own_far = [first_over_x(t, *grad_slots) for t in range(1, inner)]
        line[:] = [grad_expand]
        shrink_cut = send_x(next_cut(pick(shrink_cuts, 1, mine), shrink_sent, 0, chip, chips))
        grad_slots = lax.optimization_barrier((*grad_slots, *line))[:chips]
        grad_all = jnp.concatenate(grad_slots)
        grad, back_all, gains_first_part = back_part(0, attended, None)

        line[:] = [gains_first_part]
        shrink_cut = next_sum(*shrink_cut)
        total_shrink = lax.psum(shrink_cut, "rep")
        own_near = first_over_x(0, *line)
        own_sent = [swap_grp(next_sum(*own_far[t - 1]), t) for t in range(1, inner)]
        other_cut = send_x(next_cut(pick(other_rows, 1, mine), other_sent, 0, chip, chips))
        attended, back_all, grad = lax.optimization_barrier((attended, back_all, grad, *line))[:3]
        grad, back_all, head_gains = back_part(1, attended, (back_all, grad))

        line[:] = [head_gains]
        head_gains = head_gains + gains_first_part
        own_cut = next_sum(next_sum(*own_near), own_sent)
        other_cut = swap_core(next_sum(*other_cut))
        qkv_cuts, qkv_sent = cut_qkv(after(grad, *line))
        own_cut, other_cut, total_shrink = lax.optimization_barrier(
            (own_cut, other_cut, total_shrink, qkv_cuts, *line)
        )[:3]
        line[:] = [own_cut]
        own_cut, other_cut = lax.psum((own_cut, other_cut), "rep")
        grad_out = dot_tn(after(attended, *line), grad_all).astype(LOW)
        out_cuts = grad_out.reshape(2, inner, out_weight.shape[0], D)
        out_sent = [swap_core(pick(out_cuts, 0, core ^ 1))]
        line[:] = [grad_out]
        out_cut = send_y(next_cut(pick(out_cuts, 0, core), out_sent, 0, mine, inner))
        qkv_cut = send_y(next_cut(qkv_cuts, qkv_sent, 1, mine, inner))
        out_cut = next_sum(*out_cut)
        kept, sent = send_x(next_cut(*qkv_cut, 0, chip, chips))
        shares = []
        for s in range(1, chips):
            share = after(back_all[2 * s * block : 2 * (s + 1) * block], kept)
            shares.append(swap_chip(share, s))
        *qkv_cuts, out_cut, own_cut, other_cut = lax.optimization_barrier(
            (kept, *sent, out_cut, own_cut, other_cut, *line)
        )[: 3 + chips]
        total_out, *qkv_cuts = lax.psum((out_cut, *qkv_cuts), "rep")

        shares = [back_all[: 2 * block]] + [after(value, *line) for value in shares]
        input_part, gain_part = norm_back(inputs, gain_one, sum_of(shares))
        gain_one_grad = jnp.sum(gain_part, axis=0)
        input_grad = (input_part + hidden_grad).astype(LOW)
        input_landed = swap_core(input_grad[block:])
        grad_gains = jnp.concatenate([gain_one_grad, gain_two_grad, head_gains[0], head_gains[1]])
        grad_gains = grad_gains.reshape(n, inner, 1, -1)
        gains_of = lambda s, t: pick(pick(grad_gains, 0, me ^ s), 0, mine ^ t)
        gains_sent = [
            swap_plane(gains_of(s, t), s, t) for s in range(n) for t in range(inner) if s or t
        ]
        gains_sent = lax.optimization_barrier(tuple(gains_sent))
        total_gains = sum_of([gains_of(0, 0), *gains_sent])
        gains_sent = [
            lax.ppermute(total_gains, "rep", [(i, i ^ r) for i in range(reps)]) for r in range(1, reps)
        ]
        total_gains = sum_of([total_gains, *lax.optimization_barrier(tuple(gains_sent))])[0]
        input_grad = by_sequence(input_grad[:block], input_landed)

        size = k_width // HALVES

        def qkv_column(i, s):
            q_blocks = q_width // HALVES // size
            half, i = i // (q_blocks + 2), i % (q_blocks + 2)
            q_place = (s * HALVES + half) * q_blocks + i
            k_place = QUERY_FEATURES // size + s * HALVES + half
            v_place = k_place + KEY_FEATURES // size
            return jnp.where(i < q_blocks, q_place, jnp.where(i == q_blocks, k_place, v_place))

        key = chip.reshape(1).astype(jnp.int32)
        return (
            output,
            input_grad,
            *adam_cuts(
                key, qkv_cuts, qkv_weight, qkv_first, qkv_second, RATE_QKV, size, qkv_column
            ),
            *adam_step(out_weight, out_first, out_second, total_out.astype(FULL), RATE_OUT),
            *adam_pair(
                place, own_cut, other_cut, expand_weight, expand_first, expand_second, RATE_EXPAND,
                FF // n,
            ),
            *adam_step(
                shrink_weight, shrink_first, shrink_second, total_shrink.astype(FULL), RATE_SHRINK
            ),
            *adam_step(norm_gains, gains_first, gains_second, total_gains, RATE_GAINS),
        )

    return on_device


def solution(mesh):
    token_rows = P(("grp", "rep"), "ctx", None)
    token_notes = P(("grp", "rep"), "ctx")
    weight_rows = P(("ctx", "grp"), None)
    gain_rows = P(("ctx", "grp"))
    states = (weight_rows,) * 12 + (gain_rows,) * 3
    return jax.shard_map(
        make(mesh.shape["ctx"], mesh.shape["grp"], mesh.shape["rep"]),
        mesh=mesh,
        in_specs=(token_rows, token_notes, token_notes, token_rows) + states,
        out_specs=(token_rows, token_rows) + states,
        check_vma=False,
    )
```

```python
import functools
import math

import jax
import jax.numpy as jnp
from jax import lax
from jax.experimental import pallas as pl
from jax.experimental.pallas import tpu as pltpu
from jax.sharding import PartitionSpec as P

D = 1024
QUERY_HEADS = 16
KEY_VALUE_HEADS = 8
HEAD_SIZE = 128
FF = 3072
STEP = 10
QUERY_FEATURES = 2048
KEY_FEATURES = 1024
GROUP = QUERY_HEADS // KEY_VALUE_HEADS

EPS_NORM = 1e-06
ROPE_BASE = 1000000.0
MASKED_SCORE = -1e30
BETA_ONE = 0.9
BETA_TWO = 0.95
ADAM_EPS = 1e-08
WEIGHT_DECAY = 0.1
RATE_QKV = 0.1
RATE_OUT = 0.5
RATE_EXPAND = 0.1
RATE_SHRINK = 0.06
RATE_GAINS = 0.6

SCALE = HEAD_SIZE**-0.5
EXP_SCALE = SCALE * math.log2(math.e)
LOW = jnp.bfloat16
FULL = jnp.float32
MIB = 1 << 20
HALVES = 2


def dot_nn(a, b):
    return jnp.dot(a, b, preferred_element_type=FULL)


def dot_nt(a, b):
    return lax.dot_general(a, b, (((1,), (1,)), ((), ())), preferred_element_type=FULL)


def dot_tn(a, b):
    return lax.dot_general(a, b, (((0,), (0,)), ((), ())), preferred_element_type=FULL)


def inverse_rms(values):
    return lax.rsqrt(jnp.mean(values * values, axis=-1, keepdims=True) + EPS_NORM)


def norm_back(values, gain, incoming):
    scale = inverse_rms(values)
    normed = values * scale
    scaled = incoming * gain
    grad = scale * (scaled - normed * jnp.mean(scaled * normed, axis=-1, keepdims=True))
    return grad, incoming * normed


def adam_step(weight, first_moment, second_moment, gradient, step_rate):
    first_moment = BETA_ONE * first_moment + (1.0 - BETA_ONE) * gradient
    second_moment = BETA_TWO * second_moment + (1.0 - BETA_TWO) * gradient * gradient
    fix_one = 1.0 - BETA_ONE**STEP
    fix_two = 1.0 - BETA_TWO**STEP
    step_dir = first_moment / fix_one / (jnp.sqrt(second_moment / fix_two) + ADAM_EPS)
    return (first_moment, second_moment, weight - step_rate * (step_dir + WEIGHT_DECAY * weight))


def assemble(parts, whole, blocks):
    rows = whole.shape[0] // len(parts)
    for part, block in zip(parts, blocks):
        whole[pl.ds(pl.multiple_of(block * rows, rows), rows), :] = part[...]


def all_rows(place_ref, n, inner):
    return [(place_ref[0] ^ s) * inner + (place_ref[1] ^ t) for s in range(n) for t in range(inner)]


def chip_rows(place_ref, inner):
    return [
        ((place_ref[0] & 1) ^ k) * inner + (place_ref[1] ^ t) for k in range(2) for t in range(inner)
    ]


ANYWHERE = pl.BlockSpec(memory_space=pl.ANY)


def resident(shape, column=0):
    return pl.BlockSpec(shape, lambda *_: (0, column), pipeline_mode=pl.Buffered(1))


def project_kernel(n, inner, place_ref, *refs):
    parts = refs[: n * inner]
    pieces = refs[n * inner : n * inner + n]
    gain_ref, gain_q_ref, gain_k_ref, cos_ref, sin_ref = refs[n * inner + n : n * inner + n + 5]
    normed_ref, q_ref, k_ref, v_ref, raw_ref = refs[n * inner + n + 5 : n * inner + n + 10]
    weight, token = refs[n * inner + n + 10 :]
    step = pl.program_id(0)

    @pl.when(step == 0)
    def _():
        assemble(parts, weight, all_rows(place_ref, n, inner))

    for s in range(n):

        @pl.when((place_ref[0] ^ step) == s)
        def _():
            token[...] = pieces[s][...]

    x = token[...].astype(FULL)
    normed = (x * inverse_rms(x) * gain_ref[...]).astype(LOW)
    normed_ref[...] = normed
    projected = dot_nn(normed, weight[...])
    q_half, k_half = q_ref.shape[1] // HALVES, k_ref.shape[1] // HALVES
    raw_half = q_half + k_half
    half = raw_half + k_half
    cos, sin = cos_ref[...], sin_ref[...]

    def turn(values, gain):
        values = values * inverse_rms(values) * gain
        return (values * cos + pltpu.roll(values, HEAD_SIZE // 2, 1) * sin).astype(LOW)

    for i in range(HALVES):
        first = i * half
        raw_ref[:, i * raw_half : (i + 1) * raw_half] = projected[:, first : first + raw_half].astype(LOW)
        v_ref[:, i * k_half : (i + 1) * k_half] = projected[:, first + raw_half : first + half].astype(LOW)
        for h in range(0, q_half, HEAD_SIZE):
            values = projected[:, first + h : first + h + HEAD_SIZE]
            q_ref[:, i * q_half + h : i * q_half + h + HEAD_SIZE] = turn(values, gain_q_ref[...])
        for h in range(0, k_half, HEAD_SIZE):
            values = projected[:, first + q_half + h : first + q_half + h + HEAD_SIZE]
            k_ref[:, i * k_half + h : i * k_half + h + HEAD_SIZE] = turn(values, gain_k_ref[...])


def project(place, parts, pieces, gain, gain_q, gain_k, cos, sin):
    n = len(pieces)
    inner = len(parts) // n
    block = pieces[0].shape[0]
    length = n * block
    width = parts[0].shape[1]
    q_width, k_width = width // 2, width // 4
    whole = lambda j, p: (0, 0)
    natural = lambda j, p: (j, 0)
    return pl.pallas_call(
        functools.partial(project_kernel, n, inner),
        out_shape=(
            jax.ShapeDtypeStruct((length, D), LOW),
            jax.ShapeDtypeStruct((length, q_width), LOW),
            jax.ShapeDtypeStruct((length, k_width), LOW),
            jax.ShapeDtypeStruct((length, k_width), LOW),
            jax.ShapeDtypeStruct((length, q_width + k_width), LOW),
        ),
        grid_spec=pltpu.PrefetchScalarGridSpec(
            num_scalar_prefetch=1,
            grid=(n,),
            in_specs=[resident(p.shape) for p in parts]
            + [resident((block, D))] * n
            + [
                pl.BlockSpec((1, D), whole),
                pl.BlockSpec((1, HEAD_SIZE), whole),
                pl.BlockSpec((1, HEAD_SIZE), whole),
                pl.BlockSpec((block, HEAD_SIZE), natural),
                pl.BlockSpec((block, HEAD_SIZE), natural),
            ],
            out_specs=(
                pl.BlockSpec((block, D), natural),
                pl.BlockSpec((block, q_width), natural),
                pl.BlockSpec((block, k_width), natural),
                pl.BlockSpec((block, k_width), natural),
                pl.BlockSpec((block, q_width + k_width), natural),
            ),
            scratch_shapes=[
                pltpu.VMEM((D, width), LOW),
                pltpu.VMEM((block, D), LOW),
            ],
        ),
        compiler_params=pltpu.CompilerParams(vmem_limit_bytes=40 * MIB),
        cost_estimate=pl.CostEstimate(
            flops=2 * length * D * width, bytes_accessed=16 * MIB, transcendentals=0
        ),
        name="project",
    )(place, *parts, *pieces, gain, gain_q, gain_k, cos, sin)


def attend_kernel(n, inner, first, has_base, place_ref, *refs):
    parts = refs[: 2 * inner]
    q_ref, k_ref, v_ref, seg_col_ref, seg_row_ref = refs[2 * inner : 2 * inner + 5]
    rest = refs[2 * inner + 5 + (2 if has_base else 0) :]
    attended_ref, total_ref, share_ref, weight = rest
    block = q_ref.shape[0]
    heads = k_ref.shape[1] // HEAD_SIZE
    step = pl.program_id(0)

    @pl.when(step == 0)
    def _():
        assemble(parts, weight, chip_rows(place_ref, inner))

    def work(j):
        size = (j + 1) * block
        same = seg_col_ref[...] == seg_row_ref[:, :size]
        own = lax.broadcasted_iota(jnp.int32, (block, size), 0) + j * block
        key = lax.broadcasted_iota(jnp.int32, (block, size), 1)
        allowed = same & (own >= key)
        allowed = jnp.concatenate([allowed] * GROUP, axis=0)
        outs, totals = [], []
        for h in range(heads):
            lanes = slice(h * HEAD_SIZE, (h + 1) * HEAD_SIZE)
            q = jnp.concatenate(
                [
                    q_ref[:, (h * GROUP + g) * HEAD_SIZE : (h * GROUP + g + 1) * HEAD_SIZE]
                    for g in range(GROUP)
                ],
                axis=0,
            )
            scores = jnp.where(allowed, dot_nt(q, k_ref[:size, lanes]), MASKED_SCORE)
            top = jnp.max(scores, axis=-1, keepdims=True)
            weights = jnp.exp2((scores - top) * EXP_SCALE)
            total = jnp.sum(weights, axis=-1, keepdims=True)
            out = dot_nn(weights.astype(LOW), v_ref[:size, lanes]) / total
            log_total = top * EXP_SCALE + jnp.log2(total)
            for g in range(GROUP):
                outs.append(out[g * block : (g + 1) * block].astype(LOW))
                totals.append(log_total[g * block : (g + 1) * block])
        attended = jnp.concatenate(outs, axis=1)
        attended_ref[...] = attended
        share_ref[...] = dot_nn(attended, weight[...]).astype(LOW)
        lane = lax.broadcasted_iota(jnp.int32, (block, HEAD_SIZE), 1)
        count = len(totals) // HALVES
        for half in range(HALVES):
            packed = jnp.zeros((block, HEAD_SIZE), FULL)
            for i, column in enumerate(totals[half * count : (half + 1) * count]):
                packed = jnp.where(lane == i, column, packed)
            total_ref[:, half * HEAD_SIZE : (half + 1) * HEAD_SIZE] = packed

    place = place_ref[0] ^ (first + step)
    for j in range(n):
        pl.when(place == j)(functools.partial(work, j))


def attend(place, parts, q, k, v, seg_col, seg_row, n, chip, base):
    inner = len(parts) // 2
    length, q_width = q.shape
    k_width = k.shape[1]
    block = length // n
    first = 2 * chip
    whole = lambda i, p: (0, 0)
    natural = lambda i, p: (p[0] ^ (first + i), 0)
    slot = lambda i, p: (first + i, 0)
    plain = lambda i, p: (i, 0)
    base = list(base or ())
    before = 1 + len(parts) + 5
    return pl.pallas_call(
        functools.partial(attend_kernel, n, inner, first, bool(base)),
        out_shape=(
            jax.ShapeDtypeStruct((length, q_width), LOW),
            jax.ShapeDtypeStruct((length, HALVES * HEAD_SIZE), FULL),
            jax.ShapeDtypeStruct((2 * block, D), LOW),
        ),
        grid_spec=pltpu.PrefetchScalarGridSpec(
            num_scalar_prefetch=1,
            grid=(2,),
            in_specs=[resident(p.shape) for p in parts]
            + [
                pl.BlockSpec((block, q_width), natural),
                resident((length, k_width)),
                resident((length, k_width)),
                pl.BlockSpec((block, 1), natural),
                pl.BlockSpec((1, length), whole),
            ]
            + [ANYWHERE] * len(base),
            out_specs=(
                pl.BlockSpec((block, q_width), slot),
                pl.BlockSpec((block, HALVES * HEAD_SIZE), slot),
                pl.BlockSpec((block, D), plain),
            ),
            scratch_shapes=[pltpu.VMEM((q_width, D), LOW)],
        ),
        input_output_aliases={before: 0, before + 1: 1} if base else {},
        compiler_params=pltpu.CompilerParams(vmem_limit_bytes=48 * MIB),
        cost_estimate=pl.CostEstimate(
            flops=4 * block * q_width * (D + 2 * length), bytes_accessed=8 * MIB, transcendentals=0
        ),
        name="attend",
    )(place, *parts, q, k, v, seg_col, seg_row, *base)


def feed_kernel(chips, place_ref, *refs):
    gates, ups, shrinks = refs[:chips], refs[chips : 2 * chips], refs[2 * chips : 3 * chips]
    own_ref, other_ref, c_ref, c_other_ref = refs[3 * chips : 3 * chips + 4]
    refs = refs[3 * chips + 4 :]
    x_out, c_out, active_ref, grad_ref, share_ref, share_other, back_ref, back_other, expand, shrink = refs
    step = pl.program_id(0)
    mine = step < 2
    x = jnp.where(mine, own_ref[...], other_ref[...])
    c = jnp.where((step == 0) | (step == 3), c_ref[0], c_other_ref[0])
    x_out[...] = x
    c_out[...] = c
    size = gates[0].shape[1]
    half = chips * size

    @pl.when(step == 0)
    def _():
        for s in range(chips):
            here = slice(s * size, (s + 1) * size)
            expand[:, here] = gates[s][...]
            expand[:, half + s * size : half + (s + 1) * size] = ups[s][...]
            shrink[here, :] = shrinks[s][...]

    gate_up = dot_nn(x, expand[...])
    grad_active = dot_nt(c, shrink[...]).astype(LOW).astype(FULL)
    gate, up = gate_up[:, :half], gate_up[:, half:]
    gated = jax.nn.sigmoid(gate)
    silu = gate * gated
    active = (silu * up).astype(LOW)
    active_ref[...] = active
    grad_gate = (grad_active * up * gated * (1.0 + gate * (1.0 - gated))).astype(LOW)
    grad_up = (grad_active * silu).astype(LOW)
    grad = jnp.concatenate([grad_gate, grad_up], axis=1)
    grad_ref[...] = grad
    share = dot_nn(active, shrink[...]).astype(LOW)
    back = dot_nt(grad, expand[...]).astype(LOW)

    @pl.when(mine)
    def _():
        share_ref[...] = share
        back_ref[...] = back

    @pl.when(jnp.logical_not(mine))
    def _():
        share_other[...] = share
        back_other[...] = back


def feed(place, n, expand, shrink, own, other, c, c_other):
    chips = n // 2
    rows = own.shape[0]
    size = FF // n
    near = lambda i, p: (jnp.minimum(i, 1), 0)
    far = lambda i, p: (jnp.maximum(i - 2, 0), 0)
    flat = lambda i, p: (i, 0)
    core = lambda i, p: ((p[0] & 1) ^ (i // 2), 0, 0)
    block = rows // 2
    once = pl.Buffered(1)
    gates = [
        pl.BlockSpec((D, size), lambda i, p, s=s: (0, 2 * s + (p[0] & 1)), pipeline_mode=once)
        for s in range(chips)
    ]
    ups = [
        pl.BlockSpec((D, size), lambda i, p, s=s: (0, n + 2 * s + (p[0] & 1)), pipeline_mode=once)
        for s in range(chips)
    ]
    shrinks = [
        pl.BlockSpec((size, D), lambda i, p, s=s: (2 * s + (p[0] & 1), 0), pipeline_mode=once)
        for s in range(chips)
    ]
    wide = lambda w: jax.ShapeDtypeStruct((2 * rows, w), LOW)
    part = jax.ShapeDtypeStruct((rows, D), LOW)
    return pl.pallas_call(
        functools.partial(feed_kernel, chips),
        out_shape=(wide(D), wide(D), wide(FF // 2), wide(FF), part, part, part, part),
        grid_spec=pltpu.PrefetchScalarGridSpec(
            num_scalar_prefetch=1,
            grid=(4,),
            in_specs=gates
            + ups
            + shrinks
            + [
                pl.BlockSpec((block, D), near),
                pl.BlockSpec((block, D), far),
                pl.BlockSpec((1, block, D), core),
                pl.BlockSpec((1, block, D), core),
            ],
            out_specs=(
                pl.BlockSpec((block, D), flat),
                pl.BlockSpec((block, D), flat),
                pl.BlockSpec((block, FF // 2), flat),
                pl.BlockSpec((block, FF), flat),
                pl.BlockSpec((block, D), near),
                pl.BlockSpec((block, D), far),
                pl.BlockSpec((block, D), near),
                pl.BlockSpec((block, D), far),
            ),
            scratch_shapes=[pltpu.VMEM((D, FF), LOW), pltpu.VMEM((FF // 2, D), LOW)],
        ),
        compiler_params=pltpu.CompilerParams(vmem_limit_bytes=56 * MIB),
        cost_estimate=pl.CostEstimate(
            flops=12 * rows * D * FF, bytes_accessed=30 * MIB, transcendentals=0
        ),
        name="feed",
    )(place, *[expand] * (2 * chips), *[shrink] * chips, own, other, c, c_other)


def back_kernel(n, inner, half, place_ref, *refs):
    qkv_parts = refs[: n * inner]
    out_parts = refs[n * inner : (n + 2) * inner]
    refs = refs[(n + 2) * inner :]
    (
        h_ref,
        attended_ref,
        total_ref,
        q_ref,
        k_ref,
        v_ref,
        raw_ref,
        cos_ref,
        sin_ref,
        seg_col_ref,
        seg_row_ref,
        gain_q_ref,
        gain_k_ref,
    ) = refs[:13]
    refs = refs[13:]
    if half:
        base_ref, refs = refs[0], refs[2:]
    grad_ref, share_ref, gains_ref, qkv, out, key_sum, value_sum = refs
    block = q_ref.shape[0]
    heads = k_ref.shape[1] // HEAD_SIZE
    step = pl.program_id(0)

    @pl.when(step == 0)
    def _():
        assemble(qkv_parts, qkv, all_rows(place_ref, n, inner))
        rows = out_parts[0].shape[0]
        size = out.shape[0] // rows
        for part, spot in zip(out_parts, chip_rows(place_ref, inner)):

            @pl.when(spot // size == half)
            def _():
                out[pl.ds(pl.multiple_of((spot % size) * rows, rows), rows), :] = part[...]

        key_sum[...] = jnp.zeros_like(key_sum)
        value_sum[...] = jnp.zeros_like(value_sum)
        gains_ref[...] = jnp.zeros_like(gains_ref)

    def work(j):
        size = (j + 1) * block
        grad_attended = dot_nt(h_ref[...], out[...]).astype(LOW)
        attended = attended_ref[...]
        totals = total_ref[...].T
        same = seg_col_ref[:size, :] == seg_row_ref[:, j * block : size]
        key = lax.broadcasted_iota(jnp.int32, (size, block), 0)
        own = lax.broadcasted_iota(jnp.int32, (size, block), 1) + j * block
        allowed = same & (own >= key)
        allowed = jnp.concatenate([allowed] * GROUP, axis=1)
        cos, sin = cos_ref[...], sin_ref[...]
        gains = gains_ref[...]
        kind = lax.broadcasted_iota(jnp.int32, gains.shape, 0)

        def head_back(grad, values, gain):
            grad = grad * cos + pltpu.roll(grad * sin, HEAD_SIZE // 2, 1)
            grad, gain_part = norm_back(values.astype(FULL), gain, grad)
            return grad.astype(LOW), jnp.sum(gain_part, axis=0, keepdims=True)

        query_grads, key_grads, value_grads = [], [], []
        for h in range(heads):
            lanes = slice(h * HEAD_SIZE, (h + 1) * HEAD_SIZE)
            k, v = k_ref[:size, lanes], v_ref[:size, lanes]
            head_lanes = [
                slice((h * GROUP + g) * HEAD_SIZE, (h * GROUP + g + 1) * HEAD_SIZE)
                for g in range(GROUP)
            ]
            q = jnp.concatenate([q_ref[:, s] for s in head_lanes], axis=0)
            up = jnp.concatenate([grad_attended[:, s] for s in head_lanes], axis=0)
            seen = jnp.concatenate([attended[:, s] for s in head_lanes], axis=0)
            log_total = jnp.concatenate(
                [totals[h * GROUP + g : h * GROUP + g + 1, :] for g in range(GROUP)], axis=1
            )
            row = jnp.sum(up.astype(FULL) * seen.astype(FULL), axis=1, keepdims=True)
            row = jnp.broadcast_to(row, (GROUP * block, HEAD_SIZE)).T[:1, :]
            probs = jnp.where(allowed, jnp.exp2(dot_nt(k, q) * EXP_SCALE - log_total), 0.0)
            grad_probs = dot_nt(v, up)
            grad_scores = (probs * (grad_probs - row)).astype(LOW)
            value_sum[:size, lanes] += dot_nn(probs.astype(LOW), up)
            key_sum[:size, lanes] += dot_nn(grad_scores, q)
            query_grad = dot_tn(grad_scores, k) * SCALE
            for g in range(GROUP):
                grad, gain_part = head_back(
                    query_grad[g * block : (g + 1) * block], raw_ref[:, head_lanes[g]], gain_q_ref[...]
                )
                query_grads.append(grad)
                gains = jnp.where(kind == 0, gains + gain_part, gains)
        own_rows = slice(j * block, size)
        for h in range(heads):
            lanes = slice(h * HEAD_SIZE, (h + 1) * HEAD_SIZE)
            first = (heads * GROUP + h) * HEAD_SIZE
            grad, gain_part = head_back(
                key_sum[own_rows, lanes] * SCALE, raw_ref[:, first : first + HEAD_SIZE], gain_k_ref[...]
            )
            key_grads.append(grad)
            gains = jnp.where(kind == 1, gains + gain_part, gains)
            value_grads.append(value_sum[own_rows, lanes].astype(LOW))
        gains_ref[...] = gains
        grad = jnp.concatenate(query_grads + key_grads + value_grads, axis=1)
        grad_ref[...] = grad
        share = dot_nt(grad, qkv[...])

        if half:
            share = share + base_ref[...].astype(FULL)
        share_ref[...] = share.astype(LOW)

    for j in range(n):
        pl.when(step == n - 1 - j)(functools.partial(work, j))


def back(
    place, qkv_parts, out_parts, hidden_grad, attended, totals, q, k, v, raw, cos, sin, seg_col,
    seg_row, gain_q, gain_k, half, base,
):
    inner = len(out_parts) // 2
    n = len(qkv_parts) // inner
    length = q.shape[0]
    q_width, k_width = q.shape[1] // HALVES, k.shape[1] // HALVES
    block = length // n
    width = q_width + 2 * k_width
    whole = lambda i, p: (0, 0)
    natural = lambda i, p: (n - 1 - i, 0)
    slot = lambda i, p: (p[0] ^ (n - 1 - i), 0)
    natural_half = lambda i, p: (n - 1 - i, half)
    slot_half = lambda i, p: (p[0] ^ (n - 1 - i), half)
    base = list(base or ())
    before = 1 + len(qkv_parts) + len(out_parts) + 13
    return pl.pallas_call(
        functools.partial(back_kernel, n, inner, half),
        out_shape=(
            jax.ShapeDtypeStruct((length, HALVES * width), LOW),
            jax.ShapeDtypeStruct((length, D), LOW),
            jax.ShapeDtypeStruct((8, HEAD_SIZE), FULL),
        ),
        grid_spec=pltpu.PrefetchScalarGridSpec(
            num_scalar_prefetch=1,
            grid=(n,),
            in_specs=[resident((p.shape[0], width), half) for p in qkv_parts]
            + [resident(p.shape) for p in out_parts]
            + [
                pl.BlockSpec((block, D), slot),
                pl.BlockSpec((block, q_width), slot_half),
                pl.BlockSpec((block, HEAD_SIZE), slot_half),
                pl.BlockSpec((block, q_width), natural_half),
                resident((length, k_width), half),
                resident((length, k_width), half),
                pl.BlockSpec((block, q_width + k_width), natural_half),
                pl.BlockSpec((block, HEAD_SIZE), natural),
                pl.BlockSpec((block, HEAD_SIZE), natural),
                pl.BlockSpec((length, 1), whole),
                pl.BlockSpec((1, length), whole),
                pl.BlockSpec((1, HEAD_SIZE), whole),
                pl.BlockSpec((1, HEAD_SIZE), whole),
            ]
            + [pl.BlockSpec((block, D), slot), ANYWHERE][: len(base)],
            out_specs=(
                pl.BlockSpec((block, width), natural_half),
                pl.BlockSpec((block, D), slot),
                pl.BlockSpec((8, HEAD_SIZE), whole),
            ),
            scratch_shapes=[
                pltpu.VMEM((D, width), LOW),
                pltpu.VMEM((q_width, D), LOW),
                pltpu.VMEM((length, k_width), FULL),
                pltpu.VMEM((length, k_width), FULL),
            ],
        ),
        input_output_aliases={before + 1: 0} if base else {},
        compiler_params=pltpu.CompilerParams(vmem_limit_bytes=56 * MIB),
        cost_estimate=pl.CostEstimate(
            flops=2 * length * D * (q_width + width) + 5 * length * length * q_width,
            bytes_accessed=30 * MIB,
            transcendentals=0,
        ),
        name="back",
    )(
        place, *qkv_parts, *out_parts, hidden_grad, attended, totals, q, k, v, raw, cos, sin,
        seg_col, seg_row, gain_q, gain_k, *base,
    )


def adam_kernel(rate, key_ref, *refs):
    cuts = refs[:-7]
    weight_ref, first_ref, second_ref, new_first, new_second, new_weight, grad = refs[-7:]
    for s, cut in enumerate(cuts):

        @pl.when((pl.program_id(1) ^ key_ref[0]) % len(cuts) == s)
        def _():
            grad[...] = cut[...].astype(FULL)

    results = adam_step(weight_ref[...], first_ref[...], second_ref[...], grad[...], rate)
    new_first[...], new_second[...], new_weight[...] = results


def adam_cuts(key, cuts, weight, first, second, rate, size, column):
    rows, columns = cuts[0].shape
    cut = pl.BlockSpec((rows, size), lambda i, s, p: (0, i))
    spec = pl.BlockSpec((rows, size), lambda i, s, p: (0, column(i, s)))
    shape = jax.ShapeDtypeStruct(weight.shape, FULL)
    return pl.pallas_call(
        functools.partial(adam_kernel, rate),
        out_shape=(shape, shape, shape),
        grid_spec=pltpu.PrefetchScalarGridSpec(
            num_scalar_prefetch=1,
            grid=(columns // size, len(cuts)),
            in_specs=[cut] * len(cuts) + [spec] * 3,
            out_specs=(spec,) * 3,
            scratch_shapes=[pltpu.VMEM((rows, size), FULL)],
        ),
        cost_estimate=pl.CostEstimate(
            flops=20 * weight.size, bytes_accessed=26 * weight.size, transcendentals=weight.size
        ),
        compiler_params=pltpu.CompilerParams(vmem_limit_bytes=24 * MIB),
        name="adam_cuts",
    )(key, *cuts, weight, first, second)


def adam_pair_kernel(rate, place_ref, own_ref, other_ref, weight_ref, first_ref, second_ref, *outs):
    mine = pl.program_id(1) == (place_ref[0] & 1)
    grad = jnp.where(mine, own_ref[...].astype(FULL), other_ref[...].astype(FULL))
    results = adam_step(weight_ref[...], first_ref[...], second_ref[...], grad, rate)
    outs[0][...], outs[1][...], outs[2][...] = results


def adam_pair(place, own, other, weight, first, second, rate, size):
    rows, width = own.shape
    cut = pl.BlockSpec((rows, size), lambda i, c, p: (0, i))
    spec = pl.BlockSpec((rows, size), lambda i, c, p: (0, 2 * i + c))
    shape = jax.ShapeDtypeStruct(weight.shape, FULL)
    return pl.pallas_call(
        functools.partial(adam_pair_kernel, rate),
        out_shape=(shape, shape, shape),
        grid_spec=pltpu.PrefetchScalarGridSpec(
            num_scalar_prefetch=1,
            grid=(width // size, 2),
            in_specs=[cut, cut] + [spec] * 3,
            out_specs=(spec,) * 3,
        ),
        cost_estimate=pl.CostEstimate(
            flops=20 * weight.size, bytes_accessed=26 * weight.size, transcendentals=weight.size
        ),
        compiler_params=pltpu.CompilerParams(vmem_limit_bytes=24 * MIB),
        name="adam_pair",
    )(place, own, other, weight, first, second)


def after(value, *others):
    return lax.optimization_barrier((value, *others))[0]


def make(n, inner, reps):
    chips = n // 2

    def swap_ctx(value, s):
        return lax.ppermute(value, "ctx", [(i, i ^ s) for i in range(n)])

    def swap_core(value):
        return swap_ctx(value, 1)

    def swap_chip(value, s):
        return swap_ctx(value, 2 * s)

    def swap_grp(value, t):
        return lax.ppermute(value, "grp", [(i, i ^ t) for i in range(inner)])

    def over_chips(value):
        return [value] + [swap_chip(value, s) for s in range(1, chips)]

    def over_grp(value):
        return [value] + [swap_grp(value, t) for t in range(1, inner)]

    def sum_of(parts):
        total = parts[0].astype(FULL)
        for part in parts[1:]:
            total = total + part.astype(FULL)
        return total

    def swap_plane(value, s, t):
        pairs = [(c * inner + g, (c ^ s) * inner + (g ^ t)) for c in range(n) for g in range(inner)]
        return lax.ppermute(value, ("ctx", "grp"), pairs)

    def pick(value, axis, index):
        return lax.dynamic_index_in_dim(value, index, axis, False)

    def on_device(
        tokens,
        segment_ids,
        positions,
        cotangent,
        qkv_weight,
        qkv_first,
        qkv_second,
        out_weight,
        out_first,
        out_second,
        expand_weight,
        expand_first,
        expand_second,
        shrink_weight,
        shrink_first,
        shrink_second,
        norm_gains,
        gains_first,
        gains_second,
    ):
        seqs, block, _ = tokens.shape
        length = n * block
        me = lax.axis_index("ctx")
        core = me & 1
        chip = me >> 1
        mine = lax.axis_index("grp")
        place = jnp.stack([me, mine]).astype(jnp.int32)
        order = me ^ jnp.arange(n)
        q_width = QUERY_FEATURES // chips
        k_width = KEY_FEATURES // chips
        width = q_width + 2 * k_width
        rows = qkv_weight.shape[0]

        rep = lax.axis_index("rep")

        def qkv_piece(s):
            to = chip ^ s
            parts = []
            for i in range(HALVES):
                for first, size in ((0, q_width), (QUERY_FEATURES, k_width), (QUERY_FEATURES + KEY_FEATURES, k_width)):
                    start = first + to * size + i * (size // HALVES)
                    parts.append(lax.dynamic_slice_in_dim(qkv_weight, start, size // HALVES, 1))
            return jnp.concatenate(parts, axis=1).astype(LOW)

        small = jnp.concatenate(
            [
                segment_ids.reshape(-1).astype(FULL),
                positions.reshape(-1).astype(FULL),
                norm_gains.astype(LOW).astype(FULL),
            ]
        ).reshape(1, -1)
        small = [
            swap_plane(small, s, t) if s or t else small for s in range(n) for t in range(inner)
        ]
        tokens, qkv_low, other_tokens, *small = lax.optimization_barrier(
            (tokens, [qkv_piece(s) for s in range(chips)], pick(tokens, 0, core ^ 1), *small)
        )
        small = jnp.stack(small)
        small = small.reshape(n, inner, -1)[order]
        notes = small[:, 0, : 2 * seqs * block].reshape(n, 2, seqs, block)
        notes = pick(notes, 2, core)
        notes = jnp.moveaxis(notes, 0, 1).reshape(2, length)
        gains = small[:, mine ^ jnp.arange(inner), 2 * seqs * block :].reshape(1, -1)
        gain_one, gain_two = gains[:, :D], gains[:, D : 2 * D]
        gain_query = gains[:, 2 * D : 2 * D + HEAD_SIZE]
        gain_key = gains[:, 2 * D + HEAD_SIZE :]

        token_slots = [pick(tokens, 0, core), swap_core(other_tokens)]
        for s in range(1, chips):
            token_slots += [swap_chip(part, s) for part in token_slots[:2]]

        landed = [qkv_low[0]] + [swap_chip(qkv_low[s], s) for s in range(1, chips)]
        qkv_parts = []
        for part in landed:
            near = over_grp(part)
            qkv_parts += near + [swap_core(p) for p in near]

        near = over_grp(out_weight.astype(LOW))
        out_parts = near + [swap_core(p) for p in near]
        def gather_all(weight):
            return lax.all_gather(weight.astype(LOW), ("ctx", "grp"), axis=0, tiled=True)

        expand_full = gather_all(expand_weight)
        shrink_full = gather_all(shrink_weight)
        other_cotangent = swap_core(cotangent)

        ladder = jnp.arange(HEAD_SIZE) % (HEAD_SIZE // 2)
        frequency = jnp.exp(ladder.astype(FULL) * (-2.0 * math.log(ROPE_BASE) / HEAD_SIZE))
        angles = notes[1][:, None] * frequency[None, :]
        sign = jnp.where(jnp.arange(HEAD_SIZE) < HEAD_SIZE // 2, -1.0, 1.0)
        cos, sin = jnp.cos(angles), jnp.sin(angles) * sign
        seg_col, seg_row = notes[0][:, None], notes[0][None, :]

        normed, q, k, v, raw = project(
            place, qkv_parts, token_slots, gain_one, gain_query, gain_key, cos, sin
        )
        base, shares = None, []
        for s in range(chips - 1, -1, -1):
            *base, share = attend(place, out_parts, q, k, v, seg_col, seg_row, n, s, base)
            shares.append(swap_chip(share, s) if s else share)
        attended, totals = base
        inputs = jnp.concatenate(token_slots[:2]).astype(FULL)
        hidden = inputs + sum_of(shares)
        normed_two = (hidden * inverse_rms(hidden) * gain_two).astype(LOW)

        x_all, c_all, active, grad_gate_up, share, share_other, back_share, back_other = feed(
            place, n, expand_full, shrink_full, normed_two, swap_core(normed_two), cotangent,
            other_cotangent,
        )
        grad_shrink = dot_tn(active, c_all).astype(LOW)
        shrink_cuts = grad_shrink.reshape(chips, inner, FF // (n * inner), D)
        shrink_sent = [swap_grp(pick(shrink_cuts, 1, mine ^ t), t) for t in range(1, inner)]
        normed_grad = sum_of([after(back_share, grad_shrink), swap_core(back_other)])
        hidden_grad, gain_part = norm_back(hidden, gain_two, normed_grad)
        gain_two_grad = jnp.sum(gain_part, axis=0)
        hidden_grad = hidden_grad + c_all[: 2 * block].astype(FULL)
        hidden_low = hidden_grad.astype(LOW)
        grad_slots = over_chips(hidden_low)

        def by_sequence(kept, landed):
            return jnp.where(core == 0, jnp.stack([kept, landed]), jnp.stack([landed, kept]))

        output = (hidden + sum_of([share, swap_core(share_other)])).astype(LOW)
        output = by_sequence(output[:block], swap_core(output[block:]))

        line = []

        def next_sum(kept, sent):
            if line:
                sent = lax.optimization_barrier((*sent, *line))[: len(sent)]
            total = sum_of([kept, *sent]).astype(LOW)
            line[:] = [total]
            return total

        def next_cut(kept, sent, axis, place, count):
            sent = lax.optimization_barrier((*sent, *line))[: len(sent)]
            pieces = [
                sum_of([pick(value, axis, place ^ s) for value in (kept, *sent)]).astype(LOW)
                for s in range(count)
            ]
            line[:] = pieces
            return pieces

        def send_x(parts):
            return parts[0], [swap_chip(parts[s], s) for s in range(1, chips)]

        def send_y(parts):
            return parts[0], [swap_grp(parts[t], t) for t in range(1, inner)]

        def cut_qkv(grad):
            grad_qkv = dot_tn(normed, grad).astype(LOW)
            cuts = grad_qkv.reshape(chips, 2, inner, rows, width)
            return pick(cuts, 1, core), [swap_core(pick(cuts, 1, core ^ 1))]

        grad_expand = dot_tn(after(x_all, hidden_low), grad_gate_up).astype(LOW)
        expand_cuts = grad_expand.reshape(chips, 2, inner, rows, FF)
        other_rows = pick(expand_cuts, 1, core ^ 1)
        other_sent = [swap_grp(pick(other_rows, 1, mine ^ t), t) for t in range(1, inner)]
        own_rows = pick(expand_cuts, 1, core)

        def first_over_x(t, *gates):
            cut = after(own_rows, *gates)
            sent = [swap_chip(pick(pick(cut, 0, chip ^ s), 0, mine ^ t), s) for s in range(1, chips)]
            return pick(pick(own_rows, 0, chip), 0, mine ^ t), sent

        def back_part(half, attended, base):
            return back(
                place, qkv_parts, out_parts, grad_all, attended, totals, q, k, v, raw, cos, sin, seg_col,
                seg_row, gain_query, gain_key, half, base,
            )

        own_far = [first_over_x(t, *grad_slots) for t in range(1, inner)]
        line[:] = [grad_expand]
        shrink_cut = send_x(next_cut(pick(shrink_cuts, 1, mine), shrink_sent, 0, chip, chips))
        grad_slots = lax.optimization_barrier((*grad_slots, *line))[:chips]
        grad_all = jnp.concatenate(grad_slots)
        grad_out = dot_tn(attended, grad_all).astype(LOW)
        out_cuts = grad_out.reshape(2, inner, out_weight.shape[0], D)
        out_sent = [swap_core(pick(out_cuts, 0, core ^ 1))]
        attended = after(attended, out_cuts)
        grad, back_all, gains_first_part = back_part(0, attended, None)

        line[:] = [gains_first_part]
        shrink_cut = next_sum(*shrink_cut)
        total_shrink = lax.psum(shrink_cut, "rep")
        own_near = first_over_x(0, *line)
        own_sent = [swap_grp(next_sum(*own_far[t - 1]), t) for t in range(1, inner)]
        other_cut = send_x(next_cut(pick(other_rows, 1, mine), other_sent, 0, chip, chips))
        out_cut = send_y(next_cut(pick(out_cuts, 0, core), out_sent, 0, mine, inner))
        attended, back_all, grad = lax.optimization_barrier((attended, back_all, grad, *line))[:3]
        grad, back_all, head_gains = back_part(1, attended, (back_all, grad))

        line[:] = [head_gains]
        head_gains = head_gains + gains_first_part
        own_cut = next_sum(next_sum(*own_near), own_sent)
        other_cut = swap_core(next_sum(*other_cut))
        own_cut, other_cut, total_shrink, grad, back_all = lax.optimization_barrier(
            (own_cut, other_cut, total_shrink, grad, back_all, *line)
        )[:5]
        line[:] = [own_cut]
        own_cut, other_cut = lax.psum((own_cut, other_cut), "rep")
        qkv_cuts, qkv_sent = cut_qkv(grad)
        qkv_cut = send_y(next_cut(qkv_cuts, qkv_sent, 1, mine, inner))
        out_cut = next_sum(*out_cut)
        kept, sent = send_x(next_cut(*qkv_cut, 0, chip, chips))
        *qkv_cuts, out_cut, own_cut, other_cut, back_all = lax.optimization_barrier(
            (kept, *sent, out_cut, own_cut, other_cut, back_all, *line)
        )[: 4 + chips]
        total_out, *qkv_cuts = lax.psum((out_cut, *qkv_cuts), "rep")
        shares = [back_all[: 2 * block]]
        for s in range(1, chips):
            shares.append(swap_chip(back_all[2 * s * block : 2 * (s + 1) * block], s))
        input_part, gain_part = norm_back(inputs, gain_one, sum_of(shares))
        gain_one_grad = jnp.sum(gain_part, axis=0)
        input_grad = (input_part + hidden_grad).astype(LOW)
        input_landed = swap_core(input_grad[block:])
        grad_gains = jnp.concatenate([gain_one_grad, gain_two_grad, head_gains[0], head_gains[1]])
        grad_gains = grad_gains.reshape(n, inner, 1, -1)
        gains_of = lambda s, t: pick(pick(grad_gains, 0, me ^ s), 0, mine ^ t)
        gains_sent = [
            swap_plane(gains_of(s, t), s, t) for s in range(n) for t in range(inner) if s or t
        ]
        gains_sent = lax.optimization_barrier(tuple(gains_sent))
        total_gains = sum_of([gains_of(0, 0), *gains_sent])
        gains_sent = [
            lax.ppermute(total_gains, "rep", [(i, i ^ r) for i in range(reps)]) for r in range(1, reps)
        ]
        total_gains = sum_of([total_gains, *lax.optimization_barrier(tuple(gains_sent))])[0]
        input_grad = by_sequence(input_grad[:block], input_landed)

        size = k_width // HALVES

        def qkv_column(i, s):
            q_blocks = q_width // HALVES // size
            half, i = i // (q_blocks + 2), i % (q_blocks + 2)
            q_place = (s * HALVES + half) * q_blocks + i
            k_place = QUERY_FEATURES // size + s * HALVES + half
            v_place = k_place + KEY_FEATURES // size
            return jnp.where(i < q_blocks, q_place, jnp.where(i == q_blocks, k_place, v_place))

        key = chip.reshape(1).astype(jnp.int32)
        return (
            output,
            input_grad,
            *adam_cuts(
                key, qkv_cuts, qkv_weight, qkv_first, qkv_second, RATE_QKV, size, qkv_column
            ),
            *adam_cuts(
                key, [total_out], out_weight, out_first, out_second, RATE_OUT, D // 4, lambda i, s: i
            ),
            *adam_pair(
                place, own_cut, other_cut, expand_weight, expand_first, expand_second, RATE_EXPAND,
                FF // n,
            ),
            *adam_cuts(
                key, [total_shrink], shrink_weight, shrink_first, shrink_second, RATE_SHRINK, D // 4,
                lambda i, s: i,
            ),
            *adam_step(norm_gains, gains_first, gains_second, total_gains, RATE_GAINS),
        )

    return on_device


def solution(mesh):
    token_rows = P(("grp", "rep"), "ctx", None)
    token_notes = P(("grp", "rep"), "ctx")
    weight_rows = P(("ctx", "grp"), None)
    gain_rows = P(("ctx", "grp"))
    states = (weight_rows,) * 12 + (gain_rows,) * 3
    return jax.shard_map(
        make(mesh.shape["ctx"], mesh.shape["grp"], mesh.shape["rep"]),
        mesh=mesh,
        in_specs=(token_rows, token_notes, token_notes, token_rows) + states,
        out_specs=(token_rows, token_rows) + states,
        check_vma=False,
    )
```

```python
import functools
import math

import jax
import jax.numpy as jnp
from jax import lax
from jax.experimental import pallas as pl
from jax.experimental.pallas import tpu as pltpu
from jax.sharding import PartitionSpec as P

D = 1024
QUERY_HEADS = 16
KEY_VALUE_HEADS = 8
HEAD_SIZE = 128
FF = 3072
STEP = 10
QUERY_FEATURES = 2048
KEY_FEATURES = 1024
GROUP = QUERY_HEADS // KEY_VALUE_HEADS

EPS_NORM = 1e-06
ROPE_BASE = 1000000.0
MASKED_SCORE = -1e30
BETA_ONE = 0.9
BETA_TWO = 0.95
ADAM_EPS = 1e-08
WEIGHT_DECAY = 0.1
RATE_QKV = 0.1
RATE_OUT = 0.5
RATE_EXPAND = 0.1
RATE_SHRINK = 0.06
RATE_GAINS = 0.6

SCALE = HEAD_SIZE**-0.5
EXP_SCALE = SCALE * math.log2(math.e)
LOW = jnp.bfloat16
FULL = jnp.float32
MIB = 1 << 20
HALVES = 2


def dot_nn(a, b):
    return jnp.dot(a, b, preferred_element_type=FULL)


def dot_nt(a, b):
    return lax.dot_general(a, b, (((1,), (1,)), ((), ())), preferred_element_type=FULL)


def dot_tn(a, b):
    return lax.dot_general(a, b, (((0,), (0,)), ((), ())), preferred_element_type=FULL)


def inverse_rms(values):
    return lax.rsqrt(jnp.mean(values * values, axis=-1, keepdims=True) + EPS_NORM)


def norm_back(values, gain, incoming):
    scale = inverse_rms(values)
    normed = values * scale
    scaled = incoming * gain
    grad = scale * (scaled - normed * jnp.mean(scaled * normed, axis=-1, keepdims=True))
    return grad, incoming * normed


def adam_step(weight, first_moment, second_moment, gradient, step_rate):
    first_moment = BETA_ONE * first_moment + (1.0 - BETA_ONE) * gradient
    second_moment = BETA_TWO * second_moment + (1.0 - BETA_TWO) * gradient * gradient
    fix_one = 1.0 - BETA_ONE**STEP
    fix_two = 1.0 - BETA_TWO**STEP
    step_dir = first_moment / fix_one / (jnp.sqrt(second_moment / fix_two) + ADAM_EPS)
    return (first_moment, second_moment, weight - step_rate * (step_dir + WEIGHT_DECAY * weight))


def assemble(parts, whole, blocks):
    rows = whole.shape[0] // len(parts)
    for part, block in zip(parts, blocks):
        whole[pl.ds(pl.multiple_of(block * rows, rows), rows), :] = part[...]


def all_rows(place_ref, n, inner):
    return [(place_ref[0] ^ s) * inner + (place_ref[1] ^ t) for s in range(n) for t in range(inner)]


def chip_rows(place_ref, inner):
    return [
        ((place_ref[0] & 1) ^ k) * inner + (place_ref[1] ^ t) for k in range(2) for t in range(inner)
    ]


ANYWHERE = pl.BlockSpec(memory_space=pl.ANY)


def resident(shape, column=0):
    return pl.BlockSpec(shape, lambda *_: (0, column), pipeline_mode=pl.Buffered(1))


def project_kernel(n, inner, place_ref, *refs):
    parts = refs[: n * inner]
    pieces = refs[n * inner : n * inner + n]
    gain_ref, gain_q_ref, gain_k_ref, cos_ref, sin_ref = refs[n * inner + n : n * inner + n + 5]
    normed_ref, q_ref, k_ref, v_ref, raw_ref = refs[n * inner + n + 5 : n * inner + n + 10]
    weight, token = refs[n * inner + n + 10 :]
    step = pl.program_id(0)

    @pl.when(step == 0)
    def _():
        assemble(parts, weight, all_rows(place_ref, n, inner))

    for s in range(n):

        @pl.when((place_ref[0] ^ step) == s)
        def _():
            token[...] = pieces[s][...]

    x = token[...].astype(FULL)
    normed = (x * inverse_rms(x) * gain_ref[...]).astype(LOW)
    normed_ref[...] = normed
    projected = dot_nn(normed, weight[...])
    q_half, k_half = q_ref.shape[1] // HALVES, k_ref.shape[1] // HALVES
    raw_half = q_half + k_half
    half = raw_half + k_half
    cos, sin = cos_ref[...], sin_ref[...]

    def turn(values, gain):
        values = values * inverse_rms(values) * gain
        return (values * cos + pltpu.roll(values, HEAD_SIZE // 2, 1) * sin).astype(LOW)

    for i in range(HALVES):
        first = i * half
        raw_ref[:, i * raw_half : (i + 1) * raw_half] = projected[:, first : first + raw_half].astype(LOW)
        v_ref[:, i * k_half : (i + 1) * k_half] = projected[:, first + raw_half : first + half].astype(LOW)
        for h in range(0, q_half, HEAD_SIZE):
            values = projected[:, first + h : first + h + HEAD_SIZE]
            q_ref[:, i * q_half + h : i * q_half + h + HEAD_SIZE] = turn(values, gain_q_ref[...])
        for h in range(0, k_half, HEAD_SIZE):
            values = projected[:, first + q_half + h : first + q_half + h + HEAD_SIZE]
            k_ref[:, i * k_half + h : i * k_half + h + HEAD_SIZE] = turn(values, gain_k_ref[...])


def project(place, parts, pieces, gain, gain_q, gain_k, cos, sin):
    n = len(pieces)
    inner = len(parts) // n
    block = pieces[0].shape[0]
    length = n * block
    width = parts[0].shape[1]
    q_width, k_width = width // 2, width // 4
    whole = lambda j, p: (0, 0)
    natural = lambda j, p: (j, 0)
    return pl.pallas_call(
        functools.partial(project_kernel, n, inner),
        out_shape=(
            jax.ShapeDtypeStruct((length, D), LOW),
            jax.ShapeDtypeStruct((length, q_width), LOW),
            jax.ShapeDtypeStruct((length, k_width), LOW),
            jax.ShapeDtypeStruct((length, k_width), LOW),
            jax.ShapeDtypeStruct((length, q_width + k_width), LOW),
        ),
        grid_spec=pltpu.PrefetchScalarGridSpec(
            num_scalar_prefetch=1,
            grid=(n,),
            in_specs=[resident(p.shape) for p in parts]
            + [resident((block, D))] * n
            + [
                pl.BlockSpec((1, D), whole),
                pl.BlockSpec((1, HEAD_SIZE), whole),
                pl.BlockSpec((1, HEAD_SIZE), whole),
                pl.BlockSpec((block, HEAD_SIZE), natural),
                pl.BlockSpec((block, HEAD_SIZE), natural),
            ],
            out_specs=(
                pl.BlockSpec((block, D), natural),
                pl.BlockSpec((block, q_width), natural),
                pl.BlockSpec((block, k_width), natural),
                pl.BlockSpec((block, k_width), natural),
                pl.BlockSpec((block, q_width + k_width), natural),
            ),
            scratch_shapes=[
                pltpu.VMEM((D, width), LOW),
                pltpu.VMEM((block, D), LOW),
            ],
        ),
        compiler_params=pltpu.CompilerParams(vmem_limit_bytes=40 * MIB),
        cost_estimate=pl.CostEstimate(
            flops=2 * length * D * width, bytes_accessed=16 * MIB, transcendentals=0
        ),
        name="project",
    )(place, *parts, *pieces, gain, gain_q, gain_k, cos, sin)


def attend_kernel(n, inner, first, has_base, place_ref, *refs):
    parts = refs[: 2 * inner]
    q_ref, k_ref, v_ref, seg_col_ref, seg_row_ref = refs[2 * inner : 2 * inner + 5]
    rest = refs[2 * inner + 5 + (2 if has_base else 0) :]
    attended_ref, total_ref, share_ref, weight = rest
    block = q_ref.shape[0]
    heads = k_ref.shape[1] // HEAD_SIZE
    step = pl.program_id(0)

    @pl.when(step == 0)
    def _():
        assemble(parts, weight, chip_rows(place_ref, inner))

    def work(j):
        size = (j + 1) * block
        same = seg_col_ref[...] == seg_row_ref[:, :size]
        own = lax.broadcasted_iota(jnp.int32, (block, size), 0) + j * block
        key = lax.broadcasted_iota(jnp.int32, (block, size), 1)
        allowed = same & (own >= key)
        allowed = jnp.concatenate([allowed] * GROUP, axis=0)
        outs, totals = [], []
        for h in range(heads):
            lanes = slice(h * HEAD_SIZE, (h + 1) * HEAD_SIZE)
            q = jnp.concatenate(
                [
                    q_ref[:, (h * GROUP + g) * HEAD_SIZE : (h * GROUP + g + 1) * HEAD_SIZE]
                    for g in range(GROUP)
                ],
                axis=0,
            )
            scores = jnp.where(allowed, dot_nt(q, k_ref[:size, lanes]), MASKED_SCORE)
            top = jnp.max(scores, axis=-1, keepdims=True)
            weights = jnp.exp2((scores - top) * EXP_SCALE)
            total = jnp.sum(weights, axis=-1, keepdims=True)
            out = dot_nn(weights.astype(LOW), v_ref[:size, lanes]) / total
            log_total = top * EXP_SCALE + jnp.log2(total)
            for g in range(GROUP):
                outs.append(out[g * block : (g + 1) * block].astype(LOW))
                totals.append(log_total[g * block : (g + 1) * block])
        attended = jnp.concatenate(outs, axis=1)
        attended_ref[...] = attended
        share_ref[...] = dot_nn(attended, weight[...]).astype(LOW)
        lane = lax.broadcasted_iota(jnp.int32, (block, HEAD_SIZE), 1)
        count = len(totals) // HALVES
        for half in range(HALVES):
            packed = jnp.zeros((block, HEAD_SIZE), FULL)
            for i, column in enumerate(totals[half * count : (half + 1) * count]):
                packed = jnp.where(lane == i, column, packed)
            total_ref[:, half * HEAD_SIZE : (half + 1) * HEAD_SIZE] = packed

    place = place_ref[0] ^ (first + step)
    for j in range(n):
        pl.when(place == j)(functools.partial(work, j))


def attend(place, parts, q, k, v, seg_col, seg_row, n, chip, base):
    inner = len(parts) // 2
    length, q_width = q.shape
    k_width = k.shape[1]
    block = length // n
    first = 2 * chip
    whole = lambda i, p: (0, 0)
    natural = lambda i, p: (p[0] ^ (first + i), 0)
    slot = lambda i, p: (first + i, 0)
    plain = lambda i, p: (i, 0)
    base = list(base or ())
    before = 1 + len(parts) + 5
    return pl.pallas_call(
        functools.partial(attend_kernel, n, inner, first, bool(base)),
        out_shape=(
            jax.ShapeDtypeStruct((length, q_width), LOW),
            jax.ShapeDtypeStruct((length, HALVES * HEAD_SIZE), FULL),
            jax.ShapeDtypeStruct((2 * block, D), LOW),
        ),
        grid_spec=pltpu.PrefetchScalarGridSpec(
            num_scalar_prefetch=1,
            grid=(2,),
            in_specs=[resident(p.shape) for p in parts]
            + [
                pl.BlockSpec((block, q_width), natural),
                resident((length, k_width)),
                resident((length, k_width)),
                pl.BlockSpec((block, 1), natural),
                pl.BlockSpec((1, length), whole),
            ]
            + [ANYWHERE] * len(base),
            out_specs=(
                pl.BlockSpec((block, q_width), slot),
                pl.BlockSpec((block, HALVES * HEAD_SIZE), slot),
                pl.BlockSpec((block, D), plain),
            ),
            scratch_shapes=[pltpu.VMEM((q_width, D), LOW)],
        ),
        input_output_aliases={before: 0, before + 1: 1} if base else {},
        compiler_params=pltpu.CompilerParams(vmem_limit_bytes=48 * MIB),
        cost_estimate=pl.CostEstimate(
            flops=4 * block * q_width * (D + 2 * length), bytes_accessed=8 * MIB, transcendentals=0
        ),
        name="attend",
    )(place, *parts, q, k, v, seg_col, seg_row, *base)


def feed_kernel(chips, inner, place_ref, *refs):
    gates, ups = refs[:chips], refs[chips : 2 * chips]
    halves = refs[2 * chips : 2 * chips + 2]
    own_ref, other_ref, c_ref, c_other_ref = refs[2 * chips + 2 : 2 * chips + 6]
    refs = refs[2 * chips + 6 :]
    x_out, c_out, active_ref, grad_ref, share_ref, share_other, back_ref, back_other, expand, shrink = refs
    step = pl.program_id(0)
    mine = step < 2
    x = jnp.where(mine, own_ref[...], other_ref[...])
    c = jnp.where((step == 0) | (step == 3), c_ref[0], c_other_ref[0])
    x_out[...] = x
    c_out[...] = c
    size = gates[0].shape[1]
    half = chips * size

    @pl.when(step == 0)
    def _():
        for s in range(chips):
            here = slice(s * size, (s + 1) * size)
            expand[:, here] = gates[s][...]
            expand[:, half + s * size : half + (s + 1) * size] = ups[s][...]

    rows = half // (2 * chips * inner)
    for odd in range(2):

        @pl.when((step == 0) & (place_ref[2] == odd))
        def _():
            for i in range(chips * inner):
                source = slice(i * rows, (i + 1) * rows)
                for part, side in zip(halves, (odd, 1 - odd)):
                    start = (2 * i + side) * rows
                    shrink[start : start + rows, :] = part[source, :]

    gate_up = dot_nn(x, expand[...])
    grad_active = dot_nt(c, shrink[...]).astype(LOW).astype(FULL)
    gate, up = gate_up[:, :half], gate_up[:, half:]
    gated = jax.nn.sigmoid(gate)
    silu = gate * gated
    active = (silu * up).astype(LOW)
    active_ref[...] = active
    grad_gate = (grad_active * up * gated * (1.0 + gate * (1.0 - gated))).astype(LOW)
    grad_up = (grad_active * silu).astype(LOW)
    grad = jnp.concatenate([grad_gate, grad_up], axis=1)
    grad_ref[...] = grad
    share = dot_nn(active, shrink[...]).astype(LOW)
    back = dot_nt(grad, expand[...]).astype(LOW)

    @pl.when(mine)
    def _():
        share_ref[...] = share
        back_ref[...] = back

    @pl.when(jnp.logical_not(mine))
    def _():
        share_other[...] = share
        back_other[...] = back


def feed(place, n, inner, expand, shrink_halves, own, other, c, c_other):
    chips = n // 2
    rows = own.shape[0]
    size = FF // n
    near = lambda i, p: (jnp.minimum(i, 1), 0)
    far = lambda i, p: (jnp.maximum(i - 2, 0), 0)
    flat = lambda i, p: (i, 0)
    core = lambda i, p: ((p[0] & 1) ^ (i // 2), 0, 0)
    block = rows // 2
    once = pl.Buffered(1)
    gates = [
        pl.BlockSpec((D, size), lambda i, p, s=s: (0, 2 * s + (p[0] & 1)), pipeline_mode=once)
        for s in range(chips)
    ]
    ups = [
        pl.BlockSpec((D, size), lambda i, p, s=s: (0, n + 2 * s + (p[0] & 1)), pipeline_mode=once)
        for s in range(chips)
    ]
    wide = lambda w: jax.ShapeDtypeStruct((2 * rows, w), LOW)
    part = jax.ShapeDtypeStruct((rows, D), LOW)
    return pl.pallas_call(
        functools.partial(feed_kernel, chips, inner),
        out_shape=(wide(D), wide(D), wide(FF // 2), wide(FF), part, part, part, part),
        grid_spec=pltpu.PrefetchScalarGridSpec(
            num_scalar_prefetch=1,
            grid=(4,),
            in_specs=gates
            + ups
            + [resident(half.shape) for half in shrink_halves]
            + [
                pl.BlockSpec((block, D), near),
                pl.BlockSpec((block, D), far),
                pl.BlockSpec((1, block, D), core),
                pl.BlockSpec((1, block, D), core),
            ],
            out_specs=(
                pl.BlockSpec((block, D), flat),
                pl.BlockSpec((block, D), flat),
                pl.BlockSpec((block, FF // 2), flat),
                pl.BlockSpec((block, FF), flat),
                pl.BlockSpec((block, D), near),
                pl.BlockSpec((block, D), far),
                pl.BlockSpec((block, D), near),
                pl.BlockSpec((block, D), far),
            ),
            scratch_shapes=[pltpu.VMEM((D, FF), LOW), pltpu.VMEM((FF // 2, D), LOW)],
        ),
        compiler_params=pltpu.CompilerParams(vmem_limit_bytes=56 * MIB),
        cost_estimate=pl.CostEstimate(
            flops=12 * rows * D * FF, bytes_accessed=30 * MIB, transcendentals=0
        ),
        name="feed",
    )(place, *[expand] * (2 * chips), *shrink_halves, own, other, c, c_other)


def back_kernel(n, inner, half, place_ref, *refs):
    qkv_parts = refs[: n * inner]
    out_parts = refs[n * inner : (n + 2) * inner]
    refs = refs[(n + 2) * inner :]
    (
        h_ref,
        attended_ref,
        total_ref,
        q_ref,
        k_ref,
        v_ref,
        raw_ref,
        cos_ref,
        sin_ref,
        seg_col_ref,
        seg_row_ref,
        gain_q_ref,
        gain_k_ref,
    ) = refs[:13]
    refs = refs[13:]
    if half:
        base_ref, refs = refs[0], refs[2:]
    grad_ref, share_ref, gains_ref, qkv, out, key_sum, value_sum = refs
    block = q_ref.shape[0]
    heads = k_ref.shape[1] // HEAD_SIZE
    step = pl.program_id(0)

    @pl.when(step == 0)
    def _():
        assemble(qkv_parts, qkv, all_rows(place_ref, n, inner))
        rows = out_parts[0].shape[0]
        size = out.shape[0] // rows
        for part, spot in zip(out_parts, chip_rows(place_ref, inner)):

            @pl.when(spot // size == half)
            def _():
                out[pl.ds(pl.multiple_of((spot % size) * rows, rows), rows), :] = part[...]

        key_sum[...] = jnp.zeros_like(key_sum)
        value_sum[...] = jnp.zeros_like(value_sum)
        gains_ref[...] = jnp.zeros_like(gains_ref)

    def work(j):
        size = (j + 1) * block
        grad_attended = dot_nt(h_ref[...], out[...]).astype(LOW)
        attended = attended_ref[...]
        totals = total_ref[...].T
        same = seg_col_ref[:size, :] == seg_row_ref[:, j * block : size]
        key = lax.broadcasted_iota(jnp.int32, (size, block), 0)
        own = lax.broadcasted_iota(jnp.int32, (size, block), 1) + j * block
        allowed = same & (own >= key)
        allowed = jnp.concatenate([allowed] * GROUP, axis=1)
        cos, sin = cos_ref[...], sin_ref[...]
        gains = gains_ref[...]
        kind = lax.broadcasted_iota(jnp.int32, gains.shape, 0)

        def head_back(grad, values, gain):
            grad = grad * cos + pltpu.roll(grad * sin, HEAD_SIZE // 2, 1)
            grad, gain_part = norm_back(values.astype(FULL), gain, grad)
            return grad.astype(LOW), jnp.sum(gain_part, axis=0, keepdims=True)

        query_grads, key_grads, value_grads = [], [], []
        for h in range(heads):
            lanes = slice(h * HEAD_SIZE, (h + 1) * HEAD_SIZE)
            k, v = k_ref[:size, lanes], v_ref[:size, lanes]
            head_lanes = [
                slice((h * GROUP + g) * HEAD_SIZE, (h * GROUP + g + 1) * HEAD_SIZE)
                for g in range(GROUP)
            ]
            q = jnp.concatenate([q_ref[:, s] for s in head_lanes], axis=0)
            up = jnp.concatenate([grad_attended[:, s] for s in head_lanes], axis=0)
            seen = jnp.concatenate([attended[:, s] for s in head_lanes], axis=0)
            log_total = jnp.concatenate(
                [totals[h * GROUP + g : h * GROUP + g + 1, :] for g in range(GROUP)], axis=1
            )
            row = jnp.sum(up.astype(FULL) * seen.astype(FULL), axis=1, keepdims=True)
            row = jnp.broadcast_to(row, (GROUP * block, HEAD_SIZE)).T[:1, :]
            probs = jnp.where(allowed, jnp.exp2(dot_nt(k, q) * EXP_SCALE - log_total), 0.0)
            grad_probs = dot_nt(v, up)
            grad_scores = (probs * (grad_probs - row)).astype(LOW)
            value_sum[:size, lanes] += dot_nn(probs.astype(LOW), up)
            key_sum[:size, lanes] += dot_nn(grad_scores, q)
            query_grad = dot_tn(grad_scores, k) * SCALE
            for g in range(GROUP):
                grad, gain_part = head_back(
                    query_grad[g * block : (g + 1) * block], raw_ref[:, head_lanes[g]], gain_q_ref[...]
                )
                query_grads.append(grad)
                gains = jnp.where(kind == 0, gains + gain_part, gains)
        own_rows = slice(j * block, size)
        for h in range(heads):
            lanes = slice(h * HEAD_SIZE, (h + 1) * HEAD_SIZE)
            first = (heads * GROUP + h) * HEAD_SIZE
            grad, gain_part = head_back(
                key_sum[own_rows, lanes] * SCALE, raw_ref[:, first : first + HEAD_SIZE], gain_k_ref[...]
            )
            key_grads.append(grad)
            gains = jnp.where(kind == 1, gains + gain_part, gains)
            value_grads.append(value_sum[own_rows, lanes].astype(LOW))
        gains_ref[...] = gains
        grad = jnp.concatenate(query_grads + key_grads + value_grads, axis=1)
        grad_ref[...] = grad
        share = dot_nt(grad, qkv[...])

        if half:
            share = share + base_ref[...].astype(FULL)
        share_ref[...] = share.astype(LOW)

    for j in range(n):
        pl.when(step == n - 1 - j)(functools.partial(work, j))


def back(
    place, qkv_parts, out_parts, hidden_grad, attended, totals, q, k, v, raw, cos, sin, seg_col,
    seg_row, gain_q, gain_k, half, base,
):
    inner = len(out_parts) // 2
    n = len(qkv_parts) // inner
    length = q.shape[0]
    q_width, k_width = q.shape[1] // HALVES, k.shape[1] // HALVES
    block = length // n
    width = q_width + 2 * k_width
    whole = lambda i, p: (0, 0)
    natural = lambda i, p: (n - 1 - i, 0)
    slot = lambda i, p: (p[0] ^ (n - 1 - i), 0)
    natural_half = lambda i, p: (n - 1 - i, half)
    slot_half = lambda i, p: (p[0] ^ (n - 1 - i), half)
    base = list(base or ())
    before = 1 + len(qkv_parts) + len(out_parts) + 13
    return pl.pallas_call(
        functools.partial(back_kernel, n, inner, half),
        out_shape=(
            jax.ShapeDtypeStruct((length, HALVES * width), LOW),
            jax.ShapeDtypeStruct((length, D), LOW),
            jax.ShapeDtypeStruct((8, HEAD_SIZE), FULL),
        ),
        grid_spec=pltpu.PrefetchScalarGridSpec(
            num_scalar_prefetch=1,
            grid=(n,),
            in_specs=[resident((p.shape[0], width), half) for p in qkv_parts]
            + [resident(p.shape) for p in out_parts]
            + [
                pl.BlockSpec((block, D), slot),
                pl.BlockSpec((block, q_width), slot_half),
                pl.BlockSpec((block, HEAD_SIZE), slot_half),
                pl.BlockSpec((block, q_width), natural_half),
                resident((length, k_width), half),
                resident((length, k_width), half),
                pl.BlockSpec((block, q_width + k_width), natural_half),
                pl.BlockSpec((block, HEAD_SIZE), natural),
                pl.BlockSpec((block, HEAD_SIZE), natural),
                pl.BlockSpec((length, 1), whole),
                pl.BlockSpec((1, length), whole),
                pl.BlockSpec((1, HEAD_SIZE), whole),
                pl.BlockSpec((1, HEAD_SIZE), whole),
            ]
            + [pl.BlockSpec((block, D), slot), ANYWHERE][: len(base)],
            out_specs=(
                pl.BlockSpec((block, width), natural_half),
                pl.BlockSpec((block, D), slot),
                pl.BlockSpec((8, HEAD_SIZE), whole),
            ),
            scratch_shapes=[
                pltpu.VMEM((D, width), LOW),
                pltpu.VMEM((q_width, D), LOW),
                pltpu.VMEM((length, k_width), FULL),
                pltpu.VMEM((length, k_width), FULL),
            ],
        ),
        input_output_aliases={before + 1: 0} if base else {},
        compiler_params=pltpu.CompilerParams(vmem_limit_bytes=56 * MIB),
        cost_estimate=pl.CostEstimate(
            flops=2 * length * D * (q_width + width) + 5 * length * length * q_width,
            bytes_accessed=30 * MIB,
            transcendentals=0,
        ),
        name="back",
    )(
        place, *qkv_parts, *out_parts, hidden_grad, attended, totals, q, k, v, raw, cos, sin,
        seg_col, seg_row, gain_q, gain_k, *base,
    )


def adam_kernel(rate, key_ref, *refs):
    cuts = refs[:-7]
    weight_ref, first_ref, second_ref, new_first, new_second, new_weight, grad = refs[-7:]
    for s, cut in enumerate(cuts):

        @pl.when((pl.program_id(1) ^ key_ref[0]) % len(cuts) == s)
        def _():
            grad[...] = cut[...].astype(FULL)

    results = adam_step(weight_ref[...], first_ref[...], second_ref[...], grad[...], rate)
    new_first[...], new_second[...], new_weight[...] = results


def adam_cuts(key, cuts, weight, first, second, rate, size, column):
    rows, columns = cuts[0].shape
    cut = pl.BlockSpec((rows, size), lambda i, s, p: (0, i))
    spec = pl.BlockSpec((rows, size), lambda i, s, p: (0, column(i, s)))
    shape = jax.ShapeDtypeStruct(weight.shape, FULL)
    return pl.pallas_call(
        functools.partial(adam_kernel, rate),
        out_shape=(shape, shape, shape),
        grid_spec=pltpu.PrefetchScalarGridSpec(
            num_scalar_prefetch=1,
            grid=(columns // size, len(cuts)),
            in_specs=[cut] * len(cuts) + [spec] * 3,
            out_specs=(spec,) * 3,
            scratch_shapes=[pltpu.VMEM((rows, size), FULL)],
        ),
        cost_estimate=pl.CostEstimate(
            flops=20 * weight.size, bytes_accessed=26 * weight.size, transcendentals=weight.size
        ),
        compiler_params=pltpu.CompilerParams(vmem_limit_bytes=24 * MIB),
        name="adam_cuts",
    )(key, *cuts, weight, first, second)


def adam_pair_kernel(rate, place_ref, own_ref, other_ref, weight_ref, first_ref, second_ref, *outs):
    mine = pl.program_id(1) == (place_ref[0] & 1)
    grad = jnp.where(mine, own_ref[...].astype(FULL), other_ref[...].astype(FULL))
    results = adam_step(weight_ref[...], first_ref[...], second_ref[...], grad, rate)
    outs[0][...], outs[1][...], outs[2][...] = results


def adam_pair(place, own, other, weight, first, second, rate, size):
    rows, width = own.shape
    cut = pl.BlockSpec((rows, size), lambda i, c, p: (0, i))
    spec = pl.BlockSpec((rows, size), lambda i, c, p: (0, 2 * i + c))
    shape = jax.ShapeDtypeStruct(weight.shape, FULL)
    return pl.pallas_call(
        functools.partial(adam_pair_kernel, rate),
        out_shape=(shape, shape, shape),
        grid_spec=pltpu.PrefetchScalarGridSpec(
            num_scalar_prefetch=1,
            grid=(width // size, 2),
            in_specs=[cut, cut] + [spec] * 3,
            out_specs=(spec,) * 3,
        ),
        cost_estimate=pl.CostEstimate(
            flops=20 * weight.size, bytes_accessed=26 * weight.size, transcendentals=weight.size
        ),
        compiler_params=pltpu.CompilerParams(vmem_limit_bytes=24 * MIB),
        name="adam_pair",
    )(place, own, other, weight, first, second)


def after(value, *others):
    return lax.optimization_barrier((value, *others))[0]


def make(n, inner, reps):
    chips = n // 2

    def swap_ctx(value, s):
        return lax.ppermute(value, "ctx", [(i, i ^ s) for i in range(n)])

    def swap_core(value):
        return swap_ctx(value, 1)

    def swap_chip(value, s):
        return swap_ctx(value, 2 * s)

    def swap_grp(value, t):
        return lax.ppermute(value, "grp", [(i, i ^ t) for i in range(inner)])

    def over_chips(value):
        return [value] + [swap_chip(value, s) for s in range(1, chips)]

    def over_grp(value):
        return [value] + [swap_grp(value, t) for t in range(1, inner)]

    def sum_of(parts):
        total = parts[0].astype(FULL)
        for part in parts[1:]:
            total = total + part.astype(FULL)
        return total

    def swap_plane(value, s, t):
        pairs = [(c * inner + g, (c ^ s) * inner + (g ^ t)) for c in range(n) for g in range(inner)]
        return lax.ppermute(value, ("ctx", "grp"), pairs)

    def pick(value, axis, index):
        return lax.dynamic_index_in_dim(value, index, axis, False)

    def on_device(
        tokens,
        segment_ids,
        positions,
        cotangent,
        qkv_weight,
        qkv_first,
        qkv_second,
        out_weight,
        out_first,
        out_second,
        expand_weight,
        expand_first,
        expand_second,
        shrink_weight,
        shrink_first,
        shrink_second,
        norm_gains,
        gains_first,
        gains_second,
    ):
        seqs, block, _ = tokens.shape
        length = n * block
        me = lax.axis_index("ctx")
        core = me & 1
        chip = me >> 1
        mine = lax.axis_index("grp")
        rep = lax.axis_index("rep")
        place = jnp.stack([me, mine, rep & 1]).astype(jnp.int32)
        order = me ^ jnp.arange(n)
        q_width = QUERY_FEATURES // chips
        k_width = KEY_FEATURES // chips
        width = q_width + 2 * k_width
        rows = qkv_weight.shape[0]

        def qkv_piece(s):
            to = chip ^ s
            parts = []
            for i in range(HALVES):
                for first, size in ((0, q_width), (QUERY_FEATURES, k_width), (QUERY_FEATURES + KEY_FEATURES, k_width)):
                    start = first + to * size + i * (size // HALVES)
                    parts.append(lax.dynamic_slice_in_dim(qkv_weight, start, size // HALVES, 1))
            return jnp.concatenate(parts, axis=1).astype(LOW)

        small = jnp.concatenate(
            [
                segment_ids.reshape(-1).astype(FULL),
                positions.reshape(-1).astype(FULL),
                norm_gains.astype(LOW).astype(FULL),
            ]
        ).reshape(1, -1)
        small = [
            swap_plane(small, s, t) if s or t else small for s in range(n) for t in range(inner)
        ]
        tokens, qkv_low, other_tokens, *small = lax.optimization_barrier(
            (tokens, [qkv_piece(s) for s in range(chips)], pick(tokens, 0, core ^ 1), *small)
        )
        small = jnp.stack(small)
        small = small.reshape(n, inner, -1)[order]
        notes = small[:, 0, : 2 * seqs * block].reshape(n, 2, seqs, block)
        notes = pick(notes, 2, core)
        notes = jnp.moveaxis(notes, 0, 1).reshape(2, length)
        gains = small[:, mine ^ jnp.arange(inner), 2 * seqs * block :].reshape(1, -1)
        gain_one, gain_two = gains[:, :D], gains[:, D : 2 * D]
        gain_query = gains[:, 2 * D : 2 * D + HEAD_SIZE]
        gain_key = gains[:, 2 * D + HEAD_SIZE :]

        token_slots = [pick(tokens, 0, core), swap_core(other_tokens)]
        for s in range(1, chips):
            token_slots += [swap_chip(part, s) for part in token_slots[:2]]

        landed = [qkv_low[0]] + [swap_chip(qkv_low[s], s) for s in range(1, chips)]
        qkv_parts = []
        for part in landed:
            near = over_grp(part)
            qkv_parts += near + [swap_core(p) for p in near]

        near = over_grp(out_weight.astype(LOW))
        out_parts = near + [swap_core(p) for p in near]
        def gather_all(weight):
            return lax.all_gather(weight.astype(LOW), ("ctx", "grp"), axis=0, tiled=True)

        expand_full = gather_all(expand_weight)
        odd = rep & 1
        half_rows = shrink_weight.shape[0] // 2
        low = lax.dynamic_slice_in_dim(shrink_weight, odd * half_rows, half_rows, 0).astype(LOW)
        low = lax.all_gather(low, ("ctx", "grp"), axis=0, tiled=True)
        low = pick(low.reshape(chips, 2, inner * half_rows, D), 1, core).reshape(-1, D)
        shrink_halves = [low, lax.ppermute(low, "rep", [(i, i ^ 1) for i in range(reps)])]
        other_cotangent = swap_core(cotangent)

        ladder = jnp.arange(HEAD_SIZE) % (HEAD_SIZE // 2)
        frequency = jnp.exp(ladder.astype(FULL) * (-2.0 * math.log(ROPE_BASE) / HEAD_SIZE))
        angles = notes[1][:, None] * frequency[None, :]
        sign = jnp.where(jnp.arange(HEAD_SIZE) < HEAD_SIZE // 2, -1.0, 1.0)
        cos, sin = jnp.cos(angles), jnp.sin(angles) * sign
        seg_col, seg_row = notes[0][:, None], notes[0][None, :]

        normed, q, k, v, raw = project(
            place, qkv_parts, token_slots, gain_one, gain_query, gain_key, cos, sin
        )
        base, shares = None, []
        for s in range(chips - 1, -1, -1):
            *base, share = attend(place, out_parts, q, k, v, seg_col, seg_row, n, s, base)
            shares.append(swap_chip(share, s) if s else share)
        attended, totals = base
        *shares, shrink_halves[1] = lax.optimization_barrier((*shares, shrink_halves[1]))
        inputs = jnp.concatenate(token_slots[:2]).astype(FULL)
        hidden = inputs + sum_of(shares)
        normed_two = (hidden * inverse_rms(hidden) * gain_two).astype(LOW)

        x_all, c_all, active, grad_gate_up, share, share_other, back_share, back_other = feed(
            place, n, inner, expand_full, shrink_halves, normed_two, swap_core(normed_two), cotangent,
            other_cotangent,
        )
        grad_shrink = dot_tn(active, c_all).astype(LOW)
        shrink_cuts = grad_shrink.reshape(chips, inner, FF // (n * inner), D)
        shrink_sent = [swap_grp(pick(shrink_cuts, 1, mine ^ t), t) for t in range(1, inner)]
        normed_grad = sum_of([after(back_share, grad_shrink), swap_core(back_other)])
        hidden_grad, gain_part = norm_back(hidden, gain_two, normed_grad)
        gain_two_grad = jnp.sum(gain_part, axis=0)
        hidden_grad = hidden_grad + c_all[: 2 * block].astype(FULL)
        hidden_low = hidden_grad.astype(LOW)
        grad_slots = over_chips(hidden_low)

        def by_sequence(kept, landed):
            return jnp.where(core == 0, jnp.stack([kept, landed]), jnp.stack([landed, kept]))

        output = (hidden + sum_of([share, swap_core(share_other)])).astype(LOW)
        output = by_sequence(output[:block], swap_core(output[block:]))

        line = []

        def next_sum(kept, sent):
            if line:
                sent = lax.optimization_barrier((*sent, *line))[: len(sent)]
            total = sum_of([kept, *sent]).astype(LOW)
            line[:] = [total]
            return total

        def next_cut(kept, sent, axis, place, count):
            sent = lax.optimization_barrier((*sent, *line))[: len(sent)]
            pieces = [
                sum_of([pick(value, axis, place ^ s) for value in (kept, *sent)]).astype(LOW)
                for s in range(count)
            ]
            line[:] = pieces
            return pieces

        def send_x(parts):
            return parts[0], [swap_chip(parts[s], s) for s in range(1, chips)]

        def send_y(parts):
            return parts[0], [swap_grp(parts[t], t) for t in range(1, inner)]

        def cut_qkv(grad):
            grad_qkv = dot_tn(normed, grad).astype(LOW)
            cuts = grad_qkv.reshape(chips, 2, inner, rows, width)
            return pick(cuts, 1, core), [swap_core(pick(cuts, 1, core ^ 1))]

        grad_expand = dot_tn(after(x_all, hidden_low), grad_gate_up).astype(LOW)
        expand_cuts = grad_expand.reshape(chips, 2, inner, rows, FF)
        other_rows = pick(expand_cuts, 1, core ^ 1)
        other_sent = [swap_grp(pick(other_rows, 1, mine ^ t), t) for t in range(1, inner)]
        own_rows = pick(expand_cuts, 1, core)

        def first_over_x(t, *gates):
            cut = after(own_rows, *gates)
            sent = [swap_chip(pick(pick(cut, 0, chip ^ s), 0, mine ^ t), s) for s in range(1, chips)]
            return pick(pick(own_rows, 0, chip), 0, mine ^ t), sent

        def back_part(half, attended, base):
            return back(
                place, qkv_parts, out_parts, grad_all, attended, totals, q, k, v, raw, cos, sin, seg_col,
                seg_row, gain_query, gain_key, half, base,
            )

        own_far = [first_over_x(t, *grad_slots) for t in range(1, inner)]
        line[:] = [grad_expand]
        shrink_cut = send_x(next_cut(pick(shrink_cuts, 1, mine), shrink_sent, 0, chip, chips))
        grad_slots = lax.optimization_barrier((*grad_slots, *line))[:chips]
        grad_all = jnp.concatenate(grad_slots)
        grad, back_all, gains_first_part = back_part(0, attended, None)

        line[:] = [gains_first_part]
        shrink_cut = next_sum(*shrink_cut)
        total_shrink = lax.psum(shrink_cut, "rep")
        own_near = first_over_x(0, *line)
        own_sent = [swap_grp(next_sum(*own_far[t - 1]), t) for t in range(1, inner)]
        other_cut = send_x(next_cut(pick(other_rows, 1, mine), other_sent, 0, chip, chips))
        grad_out = dot_tn(after(attended, *line), grad_all).astype(LOW)
        out_cuts = grad_out.reshape(2, inner, out_weight.shape[0], D)
        out_kept, out_sent = pick(out_cuts, 0, core), pick(out_cuts, 0, core ^ 1)
        attended, out_kept, out_sent = lax.optimization_barrier((attended, out_kept, out_sent))
        out_sent = [swap_core(out_sent)]
        attended, back_all, grad = lax.optimization_barrier((attended, back_all, grad, *line))[:3]
        grad, back_all, head_gains = back_part(1, attended, (back_all, grad))

        line[:] = [head_gains]
        head_gains = head_gains + gains_first_part
        own_cut = next_sum(next_sum(*own_near), own_sent)
        other_cut = swap_core(next_sum(*other_cut))
        own_cut, other_cut, total_shrink, grad = lax.optimization_barrier(
            (own_cut, other_cut, total_shrink, grad, *line)
        )[:4]
        line[:] = [own_cut]
        qkv_cuts, qkv_sent = cut_qkv(grad)
        own_cut, other_cut = lax.psum((own_cut, other_cut), "rep")
        qkv_cut = send_y(next_cut(qkv_cuts, qkv_sent, 1, mine, inner))
        out_cut = send_y(next_cut(out_kept, out_sent, 0, mine, inner))
        out_cut = next_sum(*out_cut)
        kept, sent = send_x(next_cut(*qkv_cut, 0, chip, chips))
        *qkv_cuts, out_cut, own_cut, other_cut, back_all = lax.optimization_barrier(
            (kept, *sent, out_cut, own_cut, other_cut, back_all, *line)
        )[: 4 + chips]
        total_out, *qkv_cuts = lax.psum((out_cut, *qkv_cuts), "rep")
        shares = [back_all[: 2 * block]]
        for s in range(1, chips):
            shares.append(swap_chip(back_all[2 * s * block : 2 * (s + 1) * block], s))
        input_part, gain_part = norm_back(inputs, gain_one, sum_of(shares))
        gain_one_grad = jnp.sum(gain_part, axis=0)
        input_grad = (input_part + hidden_grad).astype(LOW)
        input_landed = swap_core(input_grad[block:])
        grad_gains = jnp.concatenate([gain_one_grad, gain_two_grad, head_gains[0], head_gains[1]])
        grad_gains = grad_gains.reshape(n, inner, 1, -1)
        gains_of = lambda s, t: pick(pick(grad_gains, 0, me ^ s), 0, mine ^ t)
        gains_sent = [
            swap_plane(gains_of(s, t), s, t) for s in range(n) for t in range(inner) if s or t
        ]
        gains_sent = lax.optimization_barrier(tuple(gains_sent))
        total_gains = sum_of([gains_of(0, 0), *gains_sent])
        gains_sent = [
            lax.ppermute(total_gains, "rep", [(i, i ^ r) for i in range(reps)]) for r in range(1, reps)
        ]
        total_gains = sum_of([total_gains, *lax.optimization_barrier(tuple(gains_sent))])[0]
        input_grad = by_sequence(input_grad[:block], input_landed)

        size = k_width // HALVES

        def qkv_column(i, s):
            q_blocks = q_width // HALVES // size
            half, i = i // (q_blocks + 2), i % (q_blocks + 2)
            q_place = (s * HALVES + half) * q_blocks + i
            k_place = QUERY_FEATURES // size + s * HALVES + half
            v_place = k_place + KEY_FEATURES // size
            return jnp.where(i < q_blocks, q_place, jnp.where(i == q_blocks, k_place, v_place))

        key = chip.reshape(1).astype(jnp.int32)
        return (
            output,
            input_grad,
            *adam_cuts(
                key, qkv_cuts, qkv_weight, qkv_first, qkv_second, RATE_QKV, size, qkv_column
            ),
            *adam_cuts(
                key, [total_out], out_weight, out_first, out_second, RATE_OUT, D // 4, lambda i, s: i
            ),
            *adam_pair(
                place, own_cut, other_cut, expand_weight, expand_first, expand_second, RATE_EXPAND,
                FF // n,
            ),
            *adam_cuts(
                key, [total_shrink], shrink_weight, shrink_first, shrink_second, RATE_SHRINK, D // 4,
                lambda i, s: i,
            ),
            *adam_step(norm_gains, gains_first, gains_second, total_gains, RATE_GAINS),
        )

    return on_device


def solution(mesh):
    token_rows = P(("grp", "rep"), "ctx", None)
    token_notes = P(("grp", "rep"), "ctx")
    weight_rows = P(("ctx", "grp"), None)
    gain_rows = P(("ctx", "grp"))
    states = (weight_rows,) * 12 + (gain_rows,) * 3
    return jax.shard_map(
        make(mesh.shape["ctx"], mesh.shape["grp"], mesh.shape["rep"]),
        mesh=mesh,
        in_specs=(token_rows, token_notes, token_notes, token_rows) + states,
        out_specs=(token_rows, token_rows) + states,
        check_vma=False,
    )
```

```python
import functools
import math

import jax
import jax.numpy as jnp
from jax import lax
from jax.experimental import pallas as pl
from jax.experimental.pallas import tpu as pltpu
from jax.sharding import PartitionSpec as P

D = 1024
QUERY_HEADS = 16
KEY_VALUE_HEADS = 8
HEAD_SIZE = 128
FF = 3072
STEP = 10
QUERY_FEATURES = 2048
KEY_FEATURES = 1024
GROUP = QUERY_HEADS // KEY_VALUE_HEADS

EPS_NORM = 1e-06
ROPE_BASE = 1000000.0
MASKED_SCORE = -1e30
BETA_ONE = 0.9
BETA_TWO = 0.95
ADAM_EPS = 1e-08
WEIGHT_DECAY = 0.1
RATE_QKV = 0.1
RATE_OUT = 0.5
RATE_EXPAND = 0.1
RATE_SHRINK = 0.06
RATE_GAINS = 0.6

SCALE = HEAD_SIZE**-0.5
EXP_SCALE = SCALE * math.log2(math.e)
LOW = jnp.bfloat16
FULL = jnp.float32
MIB = 1 << 20
HALVES = 2


def dot_nn(a, b):
    return jnp.dot(a, b, preferred_element_type=FULL)


def dot_nt(a, b):
    return lax.dot_general(a, b, (((1,), (1,)), ((), ())), preferred_element_type=FULL)


def dot_tn(a, b):
    return lax.dot_general(a, b, (((0,), (0,)), ((), ())), preferred_element_type=FULL)


def inverse_rms(values):
    return lax.rsqrt(jnp.mean(values * values, axis=-1, keepdims=True) + EPS_NORM)


def norm_back(values, gain, incoming):
    scale = inverse_rms(values)
    normed = values * scale
    scaled = incoming * gain
    grad = scale * (scaled - normed * jnp.mean(scaled * normed, axis=-1, keepdims=True))
    return grad, incoming * normed


def adam_step(weight, first_moment, second_moment, gradient, step_rate):
    first_moment = BETA_ONE * first_moment + (1.0 - BETA_ONE) * gradient
    second_moment = BETA_TWO * second_moment + (1.0 - BETA_TWO) * gradient * gradient
    fix_one = 1.0 - BETA_ONE**STEP
    fix_two = 1.0 - BETA_TWO**STEP
    step_dir = first_moment / fix_one / (jnp.sqrt(second_moment / fix_two) + ADAM_EPS)
    return (first_moment, second_moment, weight - step_rate * (step_dir + WEIGHT_DECAY * weight))


def assemble(parts, whole, blocks):
    rows = whole.shape[0] // len(parts)
    for part, block in zip(parts, blocks):
        whole[pl.ds(pl.multiple_of(block * rows, rows), rows), :] = part[...]


def all_rows(place_ref, n, inner):
    return [(place_ref[0] ^ s) * inner + (place_ref[1] ^ t) for s in range(n) for t in range(inner)]


def chip_rows(place_ref, inner):
    return [
        ((place_ref[0] & 1) ^ k) * inner + (place_ref[1] ^ t) for k in range(2) for t in range(inner)
    ]


ANYWHERE = pl.BlockSpec(memory_space=pl.ANY)


def resident(shape, column=0):
    return pl.BlockSpec(shape, lambda *_: (0, column), pipeline_mode=pl.Buffered(1))


def project_kernel(n, inner, place_ref, *refs):
    parts = refs[: n * inner]
    pieces = refs[n * inner : n * inner + n]
    gain_ref, gain_q_ref, gain_k_ref, cos_ref, sin_ref = refs[n * inner + n : n * inner + n + 5]
    normed_ref, q_ref, k_ref, v_ref, raw_ref = refs[n * inner + n + 5 : n * inner + n + 10]
    weight, token = refs[n * inner + n + 10 :]
    step = pl.program_id(0)

    @pl.when(step == 0)
    def _():
        assemble(parts, weight, all_rows(place_ref, n, inner))

    for s in range(n):

        @pl.when((place_ref[0] ^ step) == s)
        def _():
            token[...] = pieces[s][...]

    x = token[...].astype(FULL)
    normed = (x * inverse_rms(x) * gain_ref[...]).astype(LOW)
    normed_ref[...] = normed
    projected = dot_nn(normed, weight[...])
    q_half, k_half = q_ref.shape[1] // HALVES, k_ref.shape[1] // HALVES
    raw_half = q_half + k_half
    half = raw_half + k_half
    cos, sin = cos_ref[...], sin_ref[...]

    def turn(values, gain):
        values = values * inverse_rms(values) * gain
        return (values * cos + pltpu.roll(values, HEAD_SIZE // 2, 1) * sin).astype(LOW)

    for i in range(HALVES):
        first = i * half
        raw_ref[:, i * raw_half : (i + 1) * raw_half] = projected[:, first : first + raw_half].astype(LOW)
        v_ref[:, i * k_half : (i + 1) * k_half] = projected[:, first + raw_half : first + half].astype(LOW)
        for h in range(0, q_half, HEAD_SIZE):
            values = projected[:, first + h : first + h + HEAD_SIZE]
            q_ref[:, i * q_half + h : i * q_half + h + HEAD_SIZE] = turn(values, gain_q_ref[...])
        for h in range(0, k_half, HEAD_SIZE):
            values = projected[:, first + q_half + h : first + q_half + h + HEAD_SIZE]
            k_ref[:, i * k_half + h : i * k_half + h + HEAD_SIZE] = turn(values, gain_k_ref[...])


def project(place, parts, pieces, gain, gain_q, gain_k, cos, sin):
    n = len(pieces)
    inner = len(parts) // n
    block = pieces[0].shape[0]
    length = n * block
    width = parts[0].shape[1]
    q_width, k_width = width // 2, width // 4
    whole = lambda j, p: (0, 0)
    natural = lambda j, p: (j, 0)
    return pl.pallas_call(
        functools.partial(project_kernel, n, inner),
        out_shape=(
            jax.ShapeDtypeStruct((length, D), LOW),
            jax.ShapeDtypeStruct((length, q_width), LOW),
            jax.ShapeDtypeStruct((length, k_width), LOW),
            jax.ShapeDtypeStruct((length, k_width), LOW),
            jax.ShapeDtypeStruct((length, q_width + k_width), LOW),
        ),
        grid_spec=pltpu.PrefetchScalarGridSpec(
            num_scalar_prefetch=1,
            grid=(n,),
            in_specs=[resident(p.shape) for p in parts]
            + [resident((block, D))] * n
            + [
                pl.BlockSpec((1, D), whole),
                pl.BlockSpec((1, HEAD_SIZE), whole),
                pl.BlockSpec((1, HEAD_SIZE), whole),
                pl.BlockSpec((block, HEAD_SIZE), natural),
                pl.BlockSpec((block, HEAD_SIZE), natural),
            ],
            out_specs=(
                pl.BlockSpec((block, D), natural),
                pl.BlockSpec((block, q_width), natural),
                pl.BlockSpec((block, k_width), natural),
                pl.BlockSpec((block, k_width), natural),
                pl.BlockSpec((block, q_width + k_width), natural),
            ),
            scratch_shapes=[
                pltpu.VMEM((D, width), LOW),
                pltpu.VMEM((block, D), LOW),
            ],
        ),
        compiler_params=pltpu.CompilerParams(vmem_limit_bytes=40 * MIB),
        cost_estimate=pl.CostEstimate(
            flops=2 * length * D * width, bytes_accessed=16 * MIB, transcendentals=0
        ),
        name="project",
    )(place, *parts, *pieces, gain, gain_q, gain_k, cos, sin)


def attend_kernel(n, inner, first, has_base, place_ref, *refs):
    parts = refs[: 2 * inner]
    q_ref, k_ref, v_ref, seg_col_ref, seg_row_ref = refs[2 * inner : 2 * inner + 5]
    rest = refs[2 * inner + 5 + (2 if has_base else 0) :]
    attended_ref, total_ref, share_ref, weight = rest
    block = q_ref.shape[0]
    heads = k_ref.shape[1] // HEAD_SIZE
    step = pl.program_id(0)

    @pl.when(step == 0)
    def _():
        assemble(parts, weight, chip_rows(place_ref, inner))

    def work(j):
        size = (j + 1) * block
        same = seg_col_ref[...] == seg_row_ref[:, :size]
        own = lax.broadcasted_iota(jnp.int32, (block, size), 0) + j * block
        key = lax.broadcasted_iota(jnp.int32, (block, size), 1)
        allowed = same & (own >= key)
        allowed = jnp.concatenate([allowed] * GROUP, axis=0)
        outs, totals = [], []
        for h in range(heads):
            lanes = slice(h * HEAD_SIZE, (h + 1) * HEAD_SIZE)
            q = jnp.concatenate(
                [
                    q_ref[:, (h * GROUP + g) * HEAD_SIZE : (h * GROUP + g + 1) * HEAD_SIZE]
                    for g in range(GROUP)
                ],
                axis=0,
            )
            scores = jnp.where(allowed, dot_nt(q, k_ref[:size, lanes]), MASKED_SCORE)
            top = jnp.max(scores, axis=-1, keepdims=True)
            weights = jnp.exp2((scores - top) * EXP_SCALE)
            total = jnp.sum(weights, axis=-1, keepdims=True)
            out = dot_nn(weights.astype(LOW), v_ref[:size, lanes]) / total
            log_total = top * EXP_SCALE + jnp.log2(total)
            for g in range(GROUP):
                outs.append(out[g * block : (g + 1) * block].astype(LOW))
                totals.append(log_total[g * block : (g + 1) * block])
        attended = jnp.concatenate(outs, axis=1)
        attended_ref[...] = attended
        share_ref[...] = dot_nn(attended, weight[...]).astype(LOW)
        lane = lax.broadcasted_iota(jnp.int32, (block, HEAD_SIZE), 1)
        count = len(totals) // HALVES
        for half in range(HALVES):
            packed = jnp.zeros((block, HEAD_SIZE), FULL)
            for i, column in enumerate(totals[half * count : (half + 1) * count]):
                packed = jnp.where(lane == i, column, packed)
            total_ref[:, half * HEAD_SIZE : (half + 1) * HEAD_SIZE] = packed

    place = place_ref[0] ^ (first + step)
    for j in range(n):
        pl.when(place == j)(functools.partial(work, j))


def attend(place, parts, q, k, v, seg_col, seg_row, n, chip, base):
    inner = len(parts) // 2
    length, q_width = q.shape
    k_width = k.shape[1]
    block = length // n
    first = 2 * chip
    whole = lambda i, p: (0, 0)
    natural = lambda i, p: (p[0] ^ (first + i), 0)
    slot = lambda i, p: (first + i, 0)
    plain = lambda i, p: (i, 0)
    base = list(base or ())
    before = 1 + len(parts) + 5
    return pl.pallas_call(
        functools.partial(attend_kernel, n, inner, first, bool(base)),
        out_shape=(
            jax.ShapeDtypeStruct((length, q_width), LOW),
            jax.ShapeDtypeStruct((length, HALVES * HEAD_SIZE), FULL),
            jax.ShapeDtypeStruct((2 * block, D), LOW),
        ),
        grid_spec=pltpu.PrefetchScalarGridSpec(
            num_scalar_prefetch=1,
            grid=(2,),
            in_specs=[resident(p.shape) for p in parts]
            + [
                pl.BlockSpec((block, q_width), natural),
                resident((length, k_width)),
                resident((length, k_width)),
                pl.BlockSpec((block, 1), natural),
                pl.BlockSpec((1, length), whole),
            ]
            + [ANYWHERE] * len(base),
            out_specs=(
                pl.BlockSpec((block, q_width), slot),
                pl.BlockSpec((block, HALVES * HEAD_SIZE), slot),
                pl.BlockSpec((block, D), plain),
            ),
            scratch_shapes=[pltpu.VMEM((q_width, D), LOW)],
        ),
        input_output_aliases={before: 0, before + 1: 1} if base else {},
        compiler_params=pltpu.CompilerParams(vmem_limit_bytes=48 * MIB),
        cost_estimate=pl.CostEstimate(
            flops=4 * block * q_width * (D + 2 * length), bytes_accessed=8 * MIB, transcendentals=0
        ),
        name="attend",
    )(place, *parts, q, k, v, seg_col, seg_row, *base)


def feed_kernel(chips, inner, place_ref, *refs):
    gates, ups = refs[:chips], refs[chips : 2 * chips]
    halves = refs[2 * chips : 2 * chips + 2]
    own_ref, other_ref, c_ref, c_other_ref = refs[2 * chips + 2 : 2 * chips + 6]
    refs = refs[2 * chips + 6 :]
    x_out, c_out, active_ref, grad_ref, share_ref, share_other, back_ref, back_other, expand, shrink = refs
    step = pl.program_id(0)
    mine = step < 2
    x = jnp.where(mine, own_ref[...], other_ref[...])
    c = jnp.where((step == 0) | (step == 3), c_ref[0], c_other_ref[0])
    x_out[...] = x
    c_out[...] = c
    size = gates[0].shape[1]
    half = chips * size

    @pl.when(step == 0)
    def _():
        for s in range(chips):
            here = slice(s * size, (s + 1) * size)
            expand[:, here] = gates[s][...]
            expand[:, half + s * size : half + (s + 1) * size] = ups[s][...]

    rows = half // (2 * chips * inner)
    for odd in range(2):

        @pl.when((step == 0) & (place_ref[2] == odd))
        def _():
            for i in range(chips * inner):
                source = slice(i * rows, (i + 1) * rows)
                for part, side in zip(halves, (odd, 1 - odd)):
                    start = (2 * i + side) * rows
                    shrink[start : start + rows, :] = part[source, :]

    gate_up = dot_nn(x, expand[...])
    grad_active = dot_nt(c, shrink[...]).astype(LOW).astype(FULL)
    gate, up = gate_up[:, :half], gate_up[:, half:]
    gated = jax.nn.sigmoid(gate)
    silu = gate * gated
    active = (silu * up).astype(LOW)
    active_ref[...] = active
    grad_gate = (grad_active * up * gated * (1.0 + gate * (1.0 - gated))).astype(LOW)
    grad_up = (grad_active * silu).astype(LOW)
    grad = jnp.concatenate([grad_gate, grad_up], axis=1)
    grad_ref[...] = grad
    share = dot_nn(active, shrink[...]).astype(LOW)
    back = dot_nt(grad, expand[...]).astype(LOW)

    @pl.when(mine)
    def _():
        share_ref[...] = share
        back_ref[...] = back

    @pl.when(jnp.logical_not(mine))
    def _():
        share_other[...] = share
        back_other[...] = back


def feed(place, n, inner, expand, shrink_halves, own, other, c, c_other):
    chips = n // 2
    rows = own.shape[0]
    size = FF // n
    near = lambda i, p: (jnp.minimum(i, 1), 0)
    far = lambda i, p: (jnp.maximum(i - 2, 0), 0)
    flat = lambda i, p: (i, 0)
    core = lambda i, p: ((p[0] & 1) ^ (i // 2), 0, 0)
    block = rows // 2
    once = pl.Buffered(1)
    gates = [
        pl.BlockSpec((D, size), lambda i, p, s=s: (0, 2 * s + (p[0] & 1)), pipeline_mode=once)
        for s in range(chips)
    ]
    ups = [
        pl.BlockSpec((D, size), lambda i, p, s=s: (0, n + 2 * s + (p[0] & 1)), pipeline_mode=once)
        for s in range(chips)
    ]
    wide = lambda w: jax.ShapeDtypeStruct((2 * rows, w), LOW)
    part = jax.ShapeDtypeStruct((rows, D), LOW)
    return pl.pallas_call(
        functools.partial(feed_kernel, chips, inner),
        out_shape=(wide(D), wide(D), wide(FF // 2), wide(FF), part, part, part, part),
        grid_spec=pltpu.PrefetchScalarGridSpec(
            num_scalar_prefetch=1,
            grid=(4,),
            in_specs=gates
            + ups
            + [resident(half.shape) for half in shrink_halves]
            + [
                pl.BlockSpec((block, D), near),
                pl.BlockSpec((block, D), far),
                pl.BlockSpec((1, block, D), core),
                pl.BlockSpec((1, block, D), core),
            ],
            out_specs=(
                pl.BlockSpec((block, D), flat),
                pl.BlockSpec((block, D), flat),
                pl.BlockSpec((block, FF // 2), flat),
                pl.BlockSpec((block, FF), flat),
                pl.BlockSpec((block, D), near),
                pl.BlockSpec((block, D), far),
                pl.BlockSpec((block, D), near),
                pl.BlockSpec((block, D), far),
            ),
            scratch_shapes=[pltpu.VMEM((D, FF), LOW), pltpu.VMEM((FF // 2, D), LOW)],
        ),
        compiler_params=pltpu.CompilerParams(vmem_limit_bytes=56 * MIB),
        cost_estimate=pl.CostEstimate(
            flops=12 * rows * D * FF, bytes_accessed=30 * MIB, transcendentals=0
        ),
        name="feed",
    )(place, *[expand] * (2 * chips), *shrink_halves, own, other, c, c_other)


def back_kernel(n, inner, half, place_ref, *refs):
    qkv_parts = refs[: n * inner]
    out_parts = refs[n * inner : (n + 2) * inner]
    refs = refs[(n + 2) * inner :]
    (
        h_ref,
        attended_ref,
        total_ref,
        q_ref,
        k_ref,
        v_ref,
        raw_ref,
        cos_ref,
        sin_ref,
        seg_col_ref,
        seg_row_ref,
        gain_q_ref,
        gain_k_ref,
        normed_ref,
    ) = refs[:14]
    refs = refs[14:]
    if half:
        base_ref, refs = refs[0], refs[3:]
    sent_ref, kept_ref, share_ref, gains_ref, qkv, out, key_sum, value_sum, weight_sum = refs
    block = q_ref.shape[0]
    heads = k_ref.shape[1] // HEAD_SIZE
    step = pl.program_id(0)

    @pl.when(step == 0)
    def _():
        assemble(qkv_parts, qkv, all_rows(place_ref, n, inner))
        rows = out_parts[0].shape[0]
        size = out.shape[0] // rows
        for part, spot in zip(out_parts, chip_rows(place_ref, inner)):

            @pl.when(spot // size == half)
            def _():
                out[pl.ds(pl.multiple_of((spot % size) * rows, rows), rows), :] = part[...]

        key_sum[...] = jnp.zeros_like(key_sum)
        value_sum[...] = jnp.zeros_like(value_sum)
        gains_ref[...] = jnp.zeros_like(gains_ref)
        weight_sum[...] = jnp.zeros_like(weight_sum)

    def work(j):
        size = (j + 1) * block
        grad_attended = dot_nt(h_ref[...], out[...]).astype(LOW)
        attended = attended_ref[...]
        totals = total_ref[...].T
        same = seg_col_ref[:size, :] == seg_row_ref[:, j * block : size]
        key = lax.broadcasted_iota(jnp.int32, (size, block), 0)
        own = lax.broadcasted_iota(jnp.int32, (size, block), 1) + j * block
        allowed = same & (own >= key)
        allowed = jnp.concatenate([allowed] * GROUP, axis=1)
        cos, sin = cos_ref[...], sin_ref[...]
        gains = gains_ref[...]
        kind = lax.broadcasted_iota(jnp.int32, gains.shape, 0)

        def head_back(grad, values, gain):
            grad = grad * cos + pltpu.roll(grad * sin, HEAD_SIZE // 2, 1)
            grad, gain_part = norm_back(values.astype(FULL), gain, grad)
            return grad.astype(LOW), jnp.sum(gain_part, axis=0, keepdims=True)

        query_grads, key_grads, value_grads = [], [], []
        for h in range(heads):
            lanes = slice(h * HEAD_SIZE, (h + 1) * HEAD_SIZE)
            k, v = k_ref[:size, lanes], v_ref[:size, lanes]
            head_lanes = [
                slice((h * GROUP + g) * HEAD_SIZE, (h * GROUP + g + 1) * HEAD_SIZE)
                for g in range(GROUP)
            ]
            q = jnp.concatenate([q_ref[:, s] for s in head_lanes], axis=0)
            up = jnp.concatenate([grad_attended[:, s] for s in head_lanes], axis=0)
            seen = jnp.concatenate([attended[:, s] for s in head_lanes], axis=0)
            log_total = jnp.concatenate(
                [totals[h * GROUP + g : h * GROUP + g + 1, :] for g in range(GROUP)], axis=1
            )
            row = jnp.sum(up.astype(FULL) * seen.astype(FULL), axis=1, keepdims=True)
            row = jnp.broadcast_to(row, (GROUP * block, HEAD_SIZE)).T[:1, :]
            probs = jnp.where(allowed, jnp.exp2(dot_nt(k, q) * EXP_SCALE - log_total), 0.0)
            grad_probs = dot_nt(v, up)
            grad_scores = (probs * (grad_probs - row)).astype(LOW)
            value_sum[:size, lanes] += dot_nn(probs.astype(LOW), up)
            key_sum[:size, lanes] += dot_nn(grad_scores, q)
            query_grad = dot_tn(grad_scores, k) * SCALE
            for g in range(GROUP):
                grad, gain_part = head_back(
                    query_grad[g * block : (g + 1) * block], raw_ref[:, head_lanes[g]], gain_q_ref[...]
                )
                query_grads.append(grad)
                gains = jnp.where(kind == 0, gains + gain_part, gains)
        own_rows = slice(j * block, size)
        for h in range(heads):
            lanes = slice(h * HEAD_SIZE, (h + 1) * HEAD_SIZE)
            first = (heads * GROUP + h) * HEAD_SIZE
            grad, gain_part = head_back(
                key_sum[own_rows, lanes] * SCALE, raw_ref[:, first : first + HEAD_SIZE], gain_k_ref[...]
            )
            key_grads.append(grad)
            gains = jnp.where(kind == 1, gains + gain_part, gains)
            value_grads.append(value_sum[own_rows, lanes].astype(LOW))
        gains_ref[...] = gains
        grad = jnp.concatenate(query_grads + key_grads + value_grads, axis=1)
        weight_sum[...] += dot_tn(normed_ref[...], grad)
        share = dot_nt(grad, qkv[...])

        if half:
            share = share + base_ref[...].astype(FULL)
        share_ref[...] = share.astype(LOW)

    for j in range(n):
        pl.when(step == n - 1 - j)(functools.partial(work, j))

    @pl.when(step == n - 1)
    def _():
        chips, rows, _ = sent_ref.shape
        core = place_ref[0] & 1
        for i in range(chips):
            for ref, side in ((sent_ref, core ^ 1), (kept_ref, core)):
                start = pl.multiple_of((2 * i + side) * rows, rows)
                ref[i] = weight_sum[pl.ds(start, rows), :].astype(LOW)


def back(
    place, qkv_parts, out_parts, hidden_grad, attended, totals, q, k, v, raw, cos, sin, seg_col,
    seg_row, gain_q, gain_k, normed, half, base,
):
    inner = len(out_parts) // 2
    n = len(qkv_parts) // inner
    length = q.shape[0]
    q_width, k_width = q.shape[1] // HALVES, k.shape[1] // HALVES
    block = length // n
    width = q_width + 2 * k_width
    whole = lambda i, p: (0, 0)
    natural = lambda i, p: (n - 1 - i, 0)
    slot = lambda i, p: (p[0] ^ (n - 1 - i), 0)
    natural_half = lambda i, p: (n - 1 - i, half)
    slot_half = lambda i, p: (p[0] ^ (n - 1 - i), half)
    base = list(base or ())
    before = 1 + len(qkv_parts) + len(out_parts) + 14
    chips = n // 2
    cut = jax.ShapeDtypeStruct((chips, D // n, HALVES * width), LOW)
    cut_half = pl.BlockSpec((chips, D // n, width), lambda i, p: (0, 0, half))
    return pl.pallas_call(
        functools.partial(back_kernel, n, inner, half),
        out_shape=(
            cut,
            cut,
            jax.ShapeDtypeStruct((length, D), LOW),
            jax.ShapeDtypeStruct((8, HEAD_SIZE), FULL),
        ),
        grid_spec=pltpu.PrefetchScalarGridSpec(
            num_scalar_prefetch=1,
            grid=(n,),
            in_specs=[resident((p.shape[0], width), half) for p in qkv_parts]
            + [resident(p.shape) for p in out_parts]
            + [
                pl.BlockSpec((block, D), slot),
                pl.BlockSpec((block, q_width), slot_half),
                pl.BlockSpec((block, HEAD_SIZE), slot_half),
                pl.BlockSpec((block, q_width), natural_half),
                resident((length, k_width), half),
                resident((length, k_width), half),
                pl.BlockSpec((block, q_width + k_width), natural_half),
                pl.BlockSpec((block, HEAD_SIZE), natural),
                pl.BlockSpec((block, HEAD_SIZE), natural),
                pl.BlockSpec((length, 1), whole),
                pl.BlockSpec((1, length), whole),
                pl.BlockSpec((1, HEAD_SIZE), whole),
                pl.BlockSpec((1, HEAD_SIZE), whole),
                pl.BlockSpec((block, D), natural),
            ]
            + [pl.BlockSpec((block, D), slot), ANYWHERE, ANYWHERE][: len(base)],
            out_specs=(
                cut_half,
                cut_half,
                pl.BlockSpec((block, D), slot),
                pl.BlockSpec((8, HEAD_SIZE), whole),
            ),
            scratch_shapes=[
                pltpu.VMEM((D, width), LOW),
                pltpu.VMEM((q_width, D), LOW),
                pltpu.VMEM((length, k_width), FULL),
                pltpu.VMEM((length, k_width), FULL),
                pltpu.VMEM((D, width), FULL),
            ],
        ),
        input_output_aliases={before + 1: 0, before + 2: 1} if base else {},
        compiler_params=pltpu.CompilerParams(vmem_limit_bytes=56 * MIB),
        cost_estimate=pl.CostEstimate(
            flops=2 * length * D * (q_width + width) + 5 * length * length * q_width,
            bytes_accessed=30 * MIB,
            transcendentals=0,
        ),
        name="back",
    )(
        place, *qkv_parts, *out_parts, hidden_grad, attended, totals, q, k, v, raw, cos, sin,
        seg_col, seg_row, gain_q, gain_k, normed, *base,
    )


def adam_kernel(rate, key_ref, *refs):
    cuts = refs[:-7]
    weight_ref, first_ref, second_ref, new_first, new_second, new_weight, grad = refs[-7:]
    for s, cut in enumerate(cuts):

        @pl.when((pl.program_id(1) ^ key_ref[0]) % len(cuts) == s)
        def _():
            grad[...] = cut[...].astype(FULL)

    results = adam_step(weight_ref[...], first_ref[...], second_ref[...], grad[...], rate)
    new_first[...], new_second[...], new_weight[...] = results


def adam_cuts(key, cuts, weight, first, second, rate, size, column):
    rows, columns = cuts[0].shape
    cut = pl.BlockSpec((rows, size), lambda i, s, p: (0, i))
    spec = pl.BlockSpec((rows, size), lambda i, s, p: (0, column(i, s)))
    shape = jax.ShapeDtypeStruct(weight.shape, FULL)
    return pl.pallas_call(
        functools.partial(adam_kernel, rate),
        out_shape=(shape, shape, shape),
        grid_spec=pltpu.PrefetchScalarGridSpec(
            num_scalar_prefetch=1,
            grid=(columns // size, len(cuts)),
            in_specs=[cut] * len(cuts) + [spec] * 3,
            out_specs=(spec,) * 3,
            scratch_shapes=[pltpu.VMEM((rows, size), FULL)],
        ),
        cost_estimate=pl.CostEstimate(
            flops=20 * weight.size, bytes_accessed=26 * weight.size, transcendentals=weight.size
        ),
        compiler_params=pltpu.CompilerParams(vmem_limit_bytes=24 * MIB),
        name="adam_cuts",
    )(key, *cuts, weight, first, second)


def adam_pair_kernel(rate, place_ref, own_ref, other_ref, weight_ref, first_ref, second_ref, *outs):
    mine = pl.program_id(1) == (place_ref[0] & 1)
    grad = jnp.where(mine, own_ref[...].astype(FULL), other_ref[...].astype(FULL))
    results = adam_step(weight_ref[...], first_ref[...], second_ref[...], grad, rate)
    outs[0][...], outs[1][...], outs[2][...] = results


def adam_pair(place, own, other, weight, first, second, rate, size):
    rows, width = own.shape
    cut = pl.BlockSpec((rows, size), lambda i, c, p: (0, i))
    spec = pl.BlockSpec((rows, size), lambda i, c, p: (0, 2 * i + c))
    shape = jax.ShapeDtypeStruct(weight.shape, FULL)
    return pl.pallas_call(
        functools.partial(adam_pair_kernel, rate),
        out_shape=(shape, shape, shape),
        grid_spec=pltpu.PrefetchScalarGridSpec(
            num_scalar_prefetch=1,
            grid=(width // size, 2),
            in_specs=[cut, cut] + [spec] * 3,
            out_specs=(spec,) * 3,
        ),
        cost_estimate=pl.CostEstimate(
            flops=20 * weight.size, bytes_accessed=26 * weight.size, transcendentals=weight.size
        ),
        compiler_params=pltpu.CompilerParams(vmem_limit_bytes=24 * MIB),
        name="adam_pair",
    )(place, own, other, weight, first, second)


def after(value, *others):
    return lax.optimization_barrier((value, *others))[0]


def make(n, inner, reps):
    chips = n // 2

    def swap_ctx(value, s):
        return lax.ppermute(value, "ctx", [(i, i ^ s) for i in range(n)])

    def swap_core(value):
        return swap_ctx(value, 1)

    def swap_chip(value, s):
        return swap_ctx(value, 2 * s)

    def swap_grp(value, t):
        return lax.ppermute(value, "grp", [(i, i ^ t) for i in range(inner)])

    def over_chips(value):
        return [value] + [swap_chip(value, s) for s in range(1, chips)]

    def over_grp(value):
        return [value] + [swap_grp(value, t) for t in range(1, inner)]

    def sum_of(parts):
        total = parts[0].astype(FULL)
        for part in parts[1:]:
            total = total + part.astype(FULL)
        return total

    def swap_plane(value, s, t):
        pairs = [(c * inner + g, (c ^ s) * inner + (g ^ t)) for c in range(n) for g in range(inner)]
        return lax.ppermute(value, ("ctx", "grp"), pairs)

    def pick(value, axis, index):
        return lax.dynamic_index_in_dim(value, index, axis, False)

    def on_device(
        tokens,
        segment_ids,
        positions,
        cotangent,
        qkv_weight,
        qkv_first,
        qkv_second,
        out_weight,
        out_first,
        out_second,
        expand_weight,
        expand_first,
        expand_second,
        shrink_weight,
        shrink_first,
        shrink_second,
        norm_gains,
        gains_first,
        gains_second,
    ):
        seqs, block, _ = tokens.shape
        length = n * block
        me = lax.axis_index("ctx")
        core = me & 1
        chip = me >> 1
        mine = lax.axis_index("grp")
        rep = lax.axis_index("rep")
        place = jnp.stack([me, mine, rep & 1]).astype(jnp.int32)
        order = me ^ jnp.arange(n)
        q_width = QUERY_FEATURES // chips
        k_width = KEY_FEATURES // chips
        width = q_width + 2 * k_width
        rows = qkv_weight.shape[0]

        def qkv_piece(s):
            to = chip ^ s
            parts = []
            for i in range(HALVES):
                for first, size in ((0, q_width), (QUERY_FEATURES, k_width), (QUERY_FEATURES + KEY_FEATURES, k_width)):
                    start = first + to * size + i * (size // HALVES)
                    parts.append(lax.dynamic_slice_in_dim(qkv_weight, start, size // HALVES, 1))
            return jnp.concatenate(parts, axis=1).astype(LOW)

        small = jnp.concatenate(
            [
                segment_ids.reshape(-1).astype(FULL),
                positions.reshape(-1).astype(FULL),
                norm_gains.astype(LOW).astype(FULL),
            ]
        ).reshape(1, -1)
        small = [
            swap_plane(small, s, t) if s or t else small for s in range(n) for t in range(inner)
        ]
        tokens, qkv_low, other_tokens, *small = lax.optimization_barrier(
            (tokens, [qkv_piece(s) for s in range(chips)], pick(tokens, 0, core ^ 1), *small)
        )
        small = jnp.stack(small)
        small = small.reshape(n, inner, -1)[order]
        notes = small[:, 0, : 2 * seqs * block].reshape(n, 2, seqs, block)
        notes = pick(notes, 2, core)
        notes = jnp.moveaxis(notes, 0, 1).reshape(2, length)
        gains = small[:, mine ^ jnp.arange(inner), 2 * seqs * block :].reshape(1, -1)
        gain_one, gain_two = gains[:, :D], gains[:, D : 2 * D]
        gain_query = gains[:, 2 * D : 2 * D + HEAD_SIZE]
        gain_key = gains[:, 2 * D + HEAD_SIZE :]

        token_slots = [pick(tokens, 0, core), swap_core(other_tokens)]
        for s in range(1, chips):
            token_slots += [swap_chip(part, s) for part in token_slots[:2]]

        landed = [qkv_low[0]] + [swap_chip(qkv_low[s], s) for s in range(1, chips)]
        qkv_parts = []
        for part in landed:
            near = over_grp(part)
            qkv_parts += near + [swap_core(p) for p in near]

        near = over_grp(out_weight.astype(LOW))
        out_parts = near + [swap_core(p) for p in near]
        def gather_all(weight):
            return lax.all_gather(weight.astype(LOW), ("ctx", "grp"), axis=0, tiled=True)

        expand_full = gather_all(expand_weight)
        odd = rep & 1
        half_rows = shrink_weight.shape[0] // 2
        low = lax.dynamic_slice_in_dim(shrink_weight, odd * half_rows, half_rows, 0).astype(LOW)
        low = lax.all_gather(low, ("ctx", "grp"), axis=0, tiled=True)
        low = pick(low.reshape(chips, 2, inner * half_rows, D), 1, core).reshape(-1, D)
        shrink_halves = [low, lax.ppermute(low, "rep", [(i, i ^ 1) for i in range(reps)])]
        other_cotangent = swap_core(cotangent)

        ladder = jnp.arange(HEAD_SIZE) % (HEAD_SIZE // 2)
        frequency = jnp.exp(ladder.astype(FULL) * (-2.0 * math.log(ROPE_BASE) / HEAD_SIZE))
        angles = notes[1][:, None] * frequency[None, :]
        sign = jnp.where(jnp.arange(HEAD_SIZE) < HEAD_SIZE // 2, -1.0, 1.0)
        cos, sin = jnp.cos(angles), jnp.sin(angles) * sign
        seg_col, seg_row = notes[0][:, None], notes[0][None, :]

        normed, q, k, v, raw = project(
            place, qkv_parts, token_slots, gain_one, gain_query, gain_key, cos, sin
        )
        base, shares = None, []
        for s in range(chips - 1, -1, -1):
            *base, share = attend(place, out_parts, q, k, v, seg_col, seg_row, n, s, base)
            shares.append(swap_chip(share, s) if s else share)
        attended, totals = base
        *shares, shrink_halves[1] = lax.optimization_barrier((*shares, shrink_halves[1]))
        inputs = jnp.concatenate(token_slots[:2]).astype(FULL)
        hidden = inputs + sum_of(shares)
        normed_two = (hidden * inverse_rms(hidden) * gain_two).astype(LOW)

        x_all, c_all, active, grad_gate_up, share, share_other, back_share, back_other = feed(
            place, n, inner, expand_full, shrink_halves, normed_two, swap_core(normed_two), cotangent,
            other_cotangent,
        )
        grad_shrink = dot_tn(active, c_all).astype(LOW)
        shrink_cuts = grad_shrink.reshape(chips, inner, FF // (n * inner), D)
        shrink_sent = [swap_grp(pick(shrink_cuts, 1, mine ^ t), t) for t in range(1, inner)]
        normed_grad = sum_of([after(back_share, grad_shrink), swap_core(back_other)])
        hidden_grad, gain_part = norm_back(hidden, gain_two, normed_grad)
        gain_two_grad = jnp.sum(gain_part, axis=0)
        hidden_grad = hidden_grad + c_all[: 2 * block].astype(FULL)
        hidden_low = hidden_grad.astype(LOW)
        grad_slots = over_chips(hidden_low)

        def by_sequence(kept, landed):
            return jnp.where(core == 0, jnp.stack([kept, landed]), jnp.stack([landed, kept]))

        output = (hidden + sum_of([share, swap_core(share_other)])).astype(LOW)
        output = by_sequence(output[:block], swap_core(output[block:]))

        line = []

        def next_sum(kept, sent):
            if line:
                sent = lax.optimization_barrier((*sent, *line))[: len(sent)]
            total = sum_of([kept, *sent]).astype(LOW)
            line[:] = [total]
            return total

        def next_cut(kept, sent, axis, place, count):
            sent = lax.optimization_barrier((*sent, *line))[: len(sent)]
            pieces = [
                sum_of([pick(value, axis, place ^ s) for value in (kept, *sent)]).astype(LOW)
                for s in range(count)
            ]
            line[:] = pieces
            return pieces

        def send_x(parts):
            return parts[0], [swap_chip(parts[s], s) for s in range(1, chips)]

        def send_y(parts):
            return parts[0], [swap_grp(parts[t], t) for t in range(1, inner)]

        grad_expand = dot_tn(after(x_all, hidden_low), grad_gate_up).astype(LOW)
        expand_cuts = grad_expand.reshape(chips, 2, inner, rows, FF)
        other_rows = pick(expand_cuts, 1, core ^ 1)
        other_sent = [swap_grp(pick(other_rows, 1, mine ^ t), t) for t in range(1, inner)]
        own_rows = pick(expand_cuts, 1, core)

        def first_over_x(t, *gates):
            cut = after(own_rows, *gates)
            sent = [swap_chip(pick(pick(cut, 0, chip ^ s), 0, mine ^ t), s) for s in range(1, chips)]
            return pick(pick(own_rows, 0, chip), 0, mine ^ t), sent

        def back_part(half, attended, base):
            return back(
                place, qkv_parts, out_parts, grad_all, attended, totals, q, k, v, raw, cos, sin, seg_col,
                seg_row, gain_query, gain_key, normed, half, base,
            )

        own_far = [first_over_x(t, *grad_slots) for t in range(1, inner)]
        line[:] = [grad_expand]
        shrink_cut = send_x(next_cut(pick(shrink_cuts, 1, mine), shrink_sent, 0, chip, chips))
        grad_slots = lax.optimization_barrier((*grad_slots, *line))[:chips]
        grad_all = jnp.concatenate(grad_slots)
        sent, kept, back_all, gains_first_part = back_part(0, attended, None)

        line[:] = [gains_first_part]
        shrink_cut = next_sum(*shrink_cut)
        total_shrink = lax.psum(shrink_cut, "rep")
        own_near = first_over_x(0, *line)
        own_sent = [swap_grp(next_sum(*own_far[t - 1]), t) for t in range(1, inner)]
        other_cut = send_x(next_cut(pick(other_rows, 1, mine), other_sent, 0, chip, chips))
        grad_out = dot_tn(after(attended, *line), grad_all).astype(LOW)
        out_cuts = grad_out.reshape(2, inner, out_weight.shape[0], D)
        out_kept, out_sent = pick(out_cuts, 0, core), pick(out_cuts, 0, core ^ 1)
        attended, out_kept, out_sent = lax.optimization_barrier((attended, out_kept, out_sent))
        out_sent = [swap_core(out_sent)]
        attended, back_all, sent, kept = lax.optimization_barrier((attended, back_all, sent, kept, *line))[:4]
        sent, kept, back_all, head_gains = back_part(1, attended, (back_all, sent, kept))

        line[:] = [head_gains]
        head_gains = head_gains + gains_first_part
        own_cut = next_sum(next_sum(*own_near), own_sent)
        other_cut = swap_core(next_sum(*other_cut))
        own_cut, other_cut, total_shrink = lax.optimization_barrier(
            (own_cut, other_cut, total_shrink, *line)
        )[:3]
        line[:] = [own_cut]
        shape = (chips, inner, rows, width)
        qkv_cuts, qkv_sent = kept.reshape(shape), [swap_core(sent.reshape(shape))]
        own_cut, other_cut = lax.psum((own_cut, other_cut), "rep")
        qkv_cut = send_y(next_cut(qkv_cuts, qkv_sent, 1, mine, inner))
        out_cut = send_y(next_cut(out_kept, out_sent, 0, mine, inner))
        out_cut = next_sum(*out_cut)
        kept, sent = send_x(next_cut(*qkv_cut, 0, chip, chips))
        *qkv_cuts, out_cut, own_cut, other_cut, back_all = lax.optimization_barrier(
            (kept, *sent, out_cut, own_cut, other_cut, back_all, *line)
        )[: 4 + chips]
        total_out, *qkv_cuts = lax.psum((out_cut, *qkv_cuts), "rep")
        shares = [back_all[: 2 * block]]
        for s in range(1, chips):
            shares.append(swap_chip(back_all[2 * s * block : 2 * (s + 1) * block], s))
        input_part, gain_part = norm_back(inputs, gain_one, sum_of(shares))
        gain_one_grad = jnp.sum(gain_part, axis=0)
        input_grad = (input_part + hidden_grad).astype(LOW)
        input_landed = swap_core(input_grad[block:])
        grad_gains = jnp.concatenate([gain_one_grad, gain_two_grad, head_gains[0], head_gains[1]])
        grad_gains = grad_gains.reshape(n, inner, 1, -1)
        gains_of = lambda s, t: pick(pick(grad_gains, 0, me ^ s), 0, mine ^ t)
        gains_sent = [
            swap_plane(gains_of(s, t), s, t) for s in range(n) for t in range(inner) if s or t
        ]
        gains_sent = lax.optimization_barrier(tuple(gains_sent))
        total_gains = sum_of([gains_of(0, 0), *gains_sent])
        gains_sent = [
            lax.ppermute(total_gains, "rep", [(i, i ^ r) for i in range(reps)]) for r in range(1, reps)
        ]
        total_gains = sum_of([total_gains, *lax.optimization_barrier(tuple(gains_sent))])[0]
        input_grad = by_sequence(input_grad[:block], input_landed)

        size = k_width // HALVES

        def qkv_column(i, s):
            q_blocks = q_width // HALVES // size
            half, i = i // (q_blocks + 2), i % (q_blocks + 2)
            q_place = (s * HALVES + half) * q_blocks + i
            k_place = QUERY_FEATURES // size + s * HALVES + half
            v_place = k_place + KEY_FEATURES // size
            return jnp.where(i < q_blocks, q_place, jnp.where(i == q_blocks, k_place, v_place))

        total_shrink = after(total_shrink, total_gains)
        key = chip.reshape(1).astype(jnp.int32)
        return (
            output,
            input_grad,
            *adam_cuts(
                key, qkv_cuts, qkv_weight, qkv_first, qkv_second, RATE_QKV, size, qkv_column
            ),
            *adam_cuts(
                key, [total_out], out_weight, out_first, out_second, RATE_OUT, D // 4, lambda i, s: i
            ),
            *adam_pair(
                place, own_cut, other_cut, expand_weight, expand_first, expand_second, RATE_EXPAND,
                FF // n,
            ),
            *adam_cuts(
                key, [total_shrink], shrink_weight, shrink_first, shrink_second, RATE_SHRINK, D // 4,
                lambda i, s: i,
            ),
            *adam_step(norm_gains, gains_first, gains_second, total_gains, RATE_GAINS),
        )

    return on_device


def solution(mesh):
    token_rows = P(("grp", "rep"), "ctx", None)
    token_notes = P(("grp", "rep"), "ctx")
    weight_rows = P(("ctx", "grp"), None)
    gain_rows = P(("ctx", "grp"))
    states = (weight_rows,) * 12 + (gain_rows,) * 3
    return jax.shard_map(
        make(mesh.shape["ctx"], mesh.shape["grp"], mesh.shape["rep"]),
        mesh=mesh,
        in_specs=(token_rows, token_notes, token_notes, token_rows) + states,
        out_specs=(token_rows, token_rows) + states,
        check_vma=False,
    )
```
